32 devices in a mesh: groups: 2 (over y), ex: 8 (over z, x), dim: 2 (over core).
Axes of the slice: x: 2, y: 2, z: 4, core: 2. Of those that a mesh axis runs over, the one named last changes fastest.
Arguments:
- queries: bfloat16 [8, 64, 16384], P('ex', None, 'dim'), may hold values from -0.078125 to 0.078125
- codes: bfloat16 [4096, 16384], P(('groups', 'ex'), 'dim'), parts along dimension 0, may hold values from -3.75 to 3.75, as said below
- exponents: int32 [4096, 128], P(('groups', 'ex'), 'dim'), parts along dimension 0, may hold values from -3 to 0
- example_ids: int32 [16, 256], P(('groups', 'ex')), parts along dimension 0, may hold values from 0 to 255, each once within a row
Outputs:
- scores: float32 [8, 64, 4096], P(None, 'dim', ('groups', 'ex')), parts along dimension 2
The draws below stay inside these ranges and needn't reach their ends.
There are 2 independent parts, one for each index of `groups`. The reference program is written for one: setup_inputs(seed, part) draws one part's arguments, and reference() takes and returns one part's arrays. A program takes and returns all parts, laid end to end along the dimension named above; an argument that names none is the same for every part. Nothing has to cross between parts.
Inputs may be any that keep to these rules, and one draw needn't show every extreme that they name: `example_ids`: each row is a permutation of 0 to 255. `codes`: every value is an 8-bit e4m3 float of the form sign * (1 + m / 8) * 2 ** e with whole m from 0 to 7 and whole e from -3 to 1.
All inputs are finite; a program needn't handle non-finite values.
Results may differ from the reference program's by a relative error of at most 0.0003.
Values may be sent and summed in bfloat16 or wider, within the bound.
No kernel may reach another device: no remote copies, remote signals or barrier semaphores. Data moves between devices by JAX's collectives and lax.ppermute only.
A program may use at most 64 MiB of HBM per device.

```python
import jax
import jax.numpy as jnp
from jax import lax

K = 16384
BLOCK = 128
EX_DEV = 256
KB = 128
QBLK = 8
QPER = 64
SLABS = 8
EXAMPLES = 2048


def draw_codes(key, part):
    key = jax.random.fold_in(key, 7)
    key_sign, key_mant, key_expo = jax.random.split(key, 3)
    shape = (EXAMPLES, K)
    signs = jax.random.randint(key_sign, shape, 0, 2).astype(jnp.float32) * 2.0 - 1.0
    mantissa = jax.random.randint(key_mant, shape, 0, 8).astype(jnp.float32)
    power = jax.random.randint(key_expo, shape, -3, 2).astype(jnp.float32)
    values = signs * (1.0 + mantissa / 8.0) * jnp.exp2(power)
    return values.astype(jnp.bfloat16)


def with_ends(drawn, rng, smallest, top_value):
    place = [jax.random.randint(jax.random.fold_in(rng, axis), (), 0, length) for axis, length in enumerate(drawn.shape)]
    longest = drawn.shape.index(max(drawn.shape))
    neighbour = place[:longest] + [(place[longest] + 1) % drawn.shape[longest]] + place[longest + 1:]
    return drawn.at[tuple(place)].set(smallest).at[tuple(neighbour)].set(top_value)


def block_scale(rng, dims, cuts, smallest, largest):
    def one(axis_at, blocks):
        heights = jax.random.uniform(jax.random.fold_in(jax.random.fold_in(rng, 6), axis_at), (blocks,), jnp.float32, smallest / len(cuts), largest / len(cuts))
        return jnp.repeat(jnp.exp(heights), dims[axis_at] // blocks).reshape((-1,) + (1,) * (len(dims) - axis_at - 1))

    level = one(*cuts[0])
    for cut in cuts[1:]:
        level = level * one(*cut)
    return level


def noise(stream_key, dims, spread, most, shards=(), held_as=jnp.bfloat16):
    drawn = spread * jax.random.normal(stream_key, dims, jnp.float32)
    if shards:
        drawn = drawn * block_scale(stream_key, dims, shards, -0.22, 0.18)
    return jnp.clip(drawn, -most, most).astype(held_as)


def setup_inputs(seed: int = 0, part: int = 0) -> dict:
    seeds = jax.random.split(jax.random.key(seed), 5)
    part_splits = jax.random.split(jax.random.fold_in(seeds[4], part), 5)
    queries = noise(seeds[0], (QBLK, QPER, K), (K // 3) ** -0.5, 0.078125, ((0, 8), (2, 2)))
    codes = draw_codes(jax.random.fold_in(jax.random.fold_in(seeds[4], part), 71), part)
    exponents = with_ends(jax.random.randint(part_splits[2], (EXAMPLES, KB), -3, 1), jax.random.fold_in(part_splits[2], 1), -3, 0).astype(jnp.int32)
    example_ids = jax.vmap(lambda own: jax.random.permutation(own, EX_DEV))(jax.random.split(part_splits[3], SLABS)).reshape((SLABS, EX_DEV)).astype(jnp.int32)
    return dict(queries=queries, codes=codes, exponents=exponents, example_ids=example_ids)


def dequantize(codes, exponents):
    rows = codes.shape[0]
    scaled = codes.reshape(rows, KB, BLOCK).astype(jnp.float32) * jnp.exp2(exponents.astype(jnp.float32))[:, :, None]
    return scaled.astype(jnp.bfloat16).reshape(rows, KB * BLOCK)


def reference(queries, codes, exponents, example_ids):
    flat_queries = queries.reshape(QBLK * QPER, K)

    def one_slab(items):
        slab_codes, slab_exps, slab_ids = items
        grads = dequantize(slab_codes, slab_exps)
        raw = jnp.dot(flat_queries, grads.T, preferred_element_type=jnp.float32)
        inverse = jnp.argsort(slab_ids).astype(jnp.int32)
        return jnp.take(raw, inverse, axis=1)

    placed = lax.map(one_slab, (codes.reshape(SLABS, EX_DEV, K), exponents.reshape(SLABS, EX_DEV, KB), example_ids))
    return placed.transpose(1, 0, 2).reshape(QBLK, QPER, EXAMPLES)
```

```python
import functools

import jax
import jax.numpy as jnp
from jax import lax
from jax.experimental import pallas as pl
from jax.experimental.pallas import tpu as pltpu
from jax.sharding import PartitionSpec as P

BLOCK = 128
SENT_CHUNKS = 2
QUERY_CHUNKS = 2


def fast_length(mesh):
    line = list(mesh.devices[0, :, 0])
    size = len(line)
    if size < 2 or not all(hasattr(device, "coords") for device in line):
        return 2 if size % 2 == 0 else size

    def moved(a, b):
        return tuple(i for i, (p, q) in enumerate(zip(a.coords, b.coords)) if p != q)

    along = moved(line[0], line[1])
    length = 2
    while length < size and moved(line[0], line[length]) == along:
        length += 1
    return length if size % length == 0 else size


def scale_kernel(half_ref, codes_ref, scales_ref, out_ref):
    for block in range(codes_ref.shape[1] // BLOCK):
        columns = pl.ds(block * BLOCK, BLOCK)
        out_ref[:, columns] = codes_ref[:, columns] * scales_ref[:, block : block + 1].astype(jnp.bfloat16)


def dequantize(codes, scales, half, first, rows, parts):
    width = codes.shape[1] // parts
    tile = min(rows, 64)
    return pl.pallas_call(
        scale_kernel,
        out_shape=jax.ShapeDtypeStruct((rows, width), jnp.bfloat16),
        grid_spec=pltpu.PrefetchScalarGridSpec(
            num_scalar_prefetch=1,
            grid=(rows // tile,),
            in_specs=[
                pl.BlockSpec((tile, width), lambda i, half: (first // tile + i, half[0])),
                pl.BlockSpec((tile, width // BLOCK), lambda i, half: (first // tile + i, 0)),
            ],
            out_specs=pl.BlockSpec((tile, width), lambda i, half: (i, 0)),
        ),
        compiler_params=pltpu.CompilerParams(vmem_limit_bytes=16 << 20),
        cost_estimate=pl.CostEstimate(flops=rows * width, bytes_accessed=4 * rows * width, transcendentals=0),
        name="scale_codes",
    )(half, codes, scales)


def place_kernel(rows, order_ref, ids_ref, own_ref, received_ref, out_ref):
    raw = own_ref[...] + received_ref[...]
    count = raw.shape[1]
    slots = lax.broadcasted_iota(jnp.int32, (count, count), 0)
    table = (slots == jnp.broadcast_to(ids_ref[...], (count, count))).astype(jnp.float32)
    placed = lax.dot_general(
        raw, table, (((1,), (1,)), ((), ())),
        precision=lax.Precision.HIGHEST, preferred_element_type=jnp.float32,
    )
    for j in range(raw.shape[0] // rows):
        out_ref[order_ref[j]] = placed[j * rows : (j + 1) * rows]


def place(order, ids, own, received, rows):
    vmem = pl.BlockSpec(memory_space=pltpu.VMEM)
    return pl.pallas_call(
        functools.partial(place_kernel, rows),
        out_shape=jax.ShapeDtypeStruct((own.shape[0] // rows, rows, own.shape[1]), jnp.float32),
        in_specs=[pl.BlockSpec(memory_space=pltpu.SMEM), vmem, vmem, vmem],
        out_specs=vmem,
        compiler_params=pltpu.CompilerParams(vmem_limit_bytes=16 << 20),
        name="place_scores",
    )(order, ids, own, received)


def line_arrivals(length):
    table = []
    for p in range(length):
        arrivals = []
        for s in range(1, length):
            if p - s >= 0:
                arrivals.append(("up", s, p - s))
            if p + s < length:
                arrivals.append(("down", s, p + s))
        table.append(arrivals)
    return table


def chosen(position, where, value, other):
    return jnp.where(functools.reduce(jnp.logical_or, [position == p for p in where]), value, other)


def gather_line(block, position, length, stride, total):
    if length == 1:
        return [block]

    def shift(value, by):
        pairs = [
            (i, i + by * stride)
            for i in range(total)
            if 0 <= (i // stride) % length + by < length
        ]
        return lax.ppermute(value, "ex", pairs)

    if length == 2:
        pairs = [(i, i + stride if (i // stride) % 2 == 0 else i - stride) for i in range(total)]
        return [block, lax.ppermute(block, "ex", pairs)]
    came = {("up", 0): block, ("down", 0): block}
    for s in range(1, length):
        came["up", s] = shift(came["up", s - 1], 1)
        came["down", s] = shift(came["down", s - 1], -1)
    table = line_arrivals(length)
    blocks = [block]
    for j in range(length - 1):
        ways = {}
        for p in range(length):
            ways.setdefault(table[p][j][:2], []).append(p)
        (way, _), *rest = sorted(ways.items())
        value = came[way]
        for way, where in rest:
            value = chosen(position, where, came[way], value)
        blocks.append(value)
    return blocks


def line_sources(position, length):
    if length == 2:
        return [position, 1 - position]
    table = line_arrivals(length)
    sources = [position]
    for j in range(length - 1):
        value = jnp.int32(table[0][j][2])
        for p in range(1, length):
            value = jnp.where(position == p, table[p][j][2], value)
        sources.append(value)
    return sources


def shards(fast, parts, total, queries, codes, exponents, example_ids):
    part = lax.axis_index("groups")
    here = lax.axis_index("ex")
    half = lax.axis_index("dim")
    slow = total // fast
    rows, width = queries.shape[1], queries.shape[2] // parts
    count = codes.shape[0]
    blocks = exponents.shape[1] // parts

    mine = lax.dynamic_slice(queries[0], (0, part * width), (rows, width))
    chunks = QUERY_CHUNKS if rows % (16 * QUERY_CHUNKS) == 0 else 1
    step = rows // chunks
    arrived = []
    for c in range(chunks):
        column = gather_line(mine[c * step : (c + 1) * step], here // fast, slow, fast, total)
        arrived.append([b for block in column for b in gather_line(block, here % fast, fast, 1, total)])

    scales = (jnp.int32(1) << (exponents + 3)).astype(jnp.float32) * 0.125
    other = 1 - part
    sent_scales = lax.dynamic_slice(scales, (0, other * blocks), (count, blocks))
    kept_scales = lax.dynamic_slice(scales, (0, part * blocks), (count, blocks))
    swap = [(i, parts - 1 - i) for i in range(parts)]
    piece = count // SENT_CHUNKS
    theirs = [
        lax.ppermute(dequantize(codes, sent_scales, other[None], c * piece, piece, parts), "groups", swap)
        for c in range(SENT_CHUNKS)
    ]
    ours = dequantize(codes, kept_scales, part[None], 0, count, parts)

    def score(block, grads):
        return lax.dot_general(block, grads, (((1,), (1,)), ((), ())), preferred_element_type=jnp.float32)

    sums = []
    for j in range(total):
        for c in range(chunks):
            sums.append(jnp.concatenate([score(arrived[c][j], g) for g in [ours] + theirs], axis=1))
    sums = jnp.stack(sums).reshape(total, 2, rows // 2, 2 * count)

    keep = lax.dynamic_index_in_dim(sums, half, 1, keepdims=False)
    send = lax.dynamic_index_in_dim(sums, 1 - half, 1, keepdims=False)
    sums = keep + lax.ppermute(send, "dim", [(0, 1), (1, 0)])
    own, given = sums[..., :count], sums[..., count:]
    received = lax.ppermute(given, "groups", swap)

    order = jnp.stack([
        jnp.asarray(s * fast + f, jnp.int32)
        for s in line_sources(here // fast, slow)
        for f in line_sources(here % fast, fast)
    ])
    flat = (total * (rows // 2), count)
    return place(order, example_ids, own.reshape(flat), received.reshape(flat), rows // 2)


def solution(mesh):
    placed = (
        P("ex", None, "dim"),
        P(("groups", "ex"), "dim"),
        P(("groups", "ex"), "dim"),
        P(("groups", "ex"), None),
    )
    return jax.shard_map(
        functools.partial(shards, fast_length(mesh), mesh.shape["groups"], mesh.shape["ex"]),
        mesh=mesh,
        in_specs=placed,
        out_specs=P(None, "dim", ("groups", "ex")),
        check_vma=False,
    )
```

```python
import functools

import jax
import jax.numpy as jnp
from jax import lax
from jax.experimental import pallas as pl
from jax.experimental.pallas import tpu as pltpu
from jax.sharding import PartitionSpec as P

BLOCK = 128
VMEM = pl.BlockSpec(memory_space=pltpu.VMEM)
SMEM = pl.BlockSpec(memory_space=pltpu.SMEM)
NT = (((1,), (1,)), ((), ()))


def fast_length(mesh):
    line = list(mesh.devices[0, :, 0])
    size = len(line)
    if size < 2 or not all(hasattr(device, "coords") for device in line):
        return 2 if size % 2 == 0 else size

    def moved(a, b):
        return tuple(i for i, (p, q) in enumerate(zip(a.coords, b.coords)) if p != q)

    along = moved(line[0], line[1])
    length = 2
    while length < size and moved(line[0], line[length]) == along:
        length += 1
    return length if size % length == 0 else size


def scale_kernel(alone, tile, starts_ref, codes_ref, given_ref, kept_ref, sent_ref, grads_ref, buffer, sems):
    count = codes_ref.shape[0]

    def fetch(i):
        return pltpu.make_async_copy(codes_ref.at[pl.ds(i * tile, tile)], buffer.at[i], sems.at[i])

    tiles = count // tile
    for i in range(tiles):
        fetch(i).start()
    for i in range(tiles):
        fetch(i).wait()
        rows = pl.ds(i * tile, tile)

        def scaled(first, block, scales_ref, at):
            columns = pl.ds(pl.multiple_of((first + block) * BLOCK, BLOCK), BLOCK)
            return buffer[i, :, columns] * scales_ref[rows, at : at + 1].astype(jnp.bfloat16)

        for block in range(alone):
            sent_ref[rows, block * BLOCK : (block + 1) * BLOCK] = scaled(starts_ref[1], block, given_ref, block)
        for block in range(grads_ref.shape[1] // BLOCK):
            first = starts_ref[0] if block < alone else 0
            grads_ref[rows, block * BLOCK : (block + 1) * BLOCK] = scaled(first, block, kept_ref, block)


def scale_codes(codes, starts, given, kept, alone):
    count = codes.shape[0]
    tile = min(count, 64)
    blocks = kept.shape[1]
    return pl.pallas_call(
        functools.partial(scale_kernel, alone, tile),
        out_shape=[
            jax.ShapeDtypeStruct((count, alone * BLOCK), jnp.bfloat16),
            jax.ShapeDtypeStruct((count, blocks * BLOCK), jnp.bfloat16),
        ],
        in_specs=[SMEM, pl.BlockSpec(memory_space=pltpu.HBM), VMEM, VMEM],
        out_specs=[VMEM, VMEM],
        scratch_shapes=[
            pltpu.VMEM((count // tile, tile, codes.shape[1]), codes.dtype),
            pltpu.SemaphoreType.DMA((count // tile,)),
        ],
        compiler_params=pltpu.CompilerParams(vmem_limit_bytes=16 << 20),
        cost_estimate=pl.CostEstimate(flops=codes.size, bytes_accessed=4 * codes.size, transcendentals=0),
        name="scale_codes",
    )(starts, codes, given, kept)


def score_kernel(parts, *refs):
    *refs, out_ref = refs
    query_refs, grad_refs = refs[: sum(parts)], refs[sum(parts) :]
    at = 0
    row = 0
    for part in parts:
        pieces = query_refs[at : at + part]
        at += part
        rows = pieces[0].shape[0]
        column = 0
        for grads in grad_refs:
            total = None
            first = 0
            for piece in pieces:
                width = min(piece.shape[1], grads.shape[1] - first)
                if width <= 0:
                    break
                term = lax.dot_general(
                    piece[:, :width], grads[:, first : first + width], NT, preferred_element_type=jnp.float32
                )
                total = term if total is None else total + term
                first += width
            out_ref[row : row + rows, column : column + grads.shape[0]] = total
            column += grads.shape[0]
        row += rows


def score(queries, grads):
    rows = sum(pieces[0].shape[0] for pieces in queries)
    columns = sum(g.shape[0] for g in grads)
    operands = [piece for pieces in queries for piece in pieces] + list(grads)
    flops = 2 * rows * sum(g.size for g in grads)
    return pl.pallas_call(
        functools.partial(score_kernel, [len(pieces) for pieces in queries]),
        out_shape=jax.ShapeDtypeStruct((rows, columns), jnp.float32),
        in_specs=[VMEM] * len(operands),
        out_specs=VMEM,
        compiler_params=pltpu.CompilerParams(vmem_limit_bytes=16 << 20),
        cost_estimate=pl.CostEstimate(
            flops=flops, bytes_accessed=2 * sum(o.size for o in operands), transcendentals=0
        ),
        name="score",
    )(*operands)


def place_kernel(rows, order_ref, ids_ref, own_ref, received_ref, out_ref):
    raw = own_ref[...] + received_ref[...]
    count = raw.shape[1]
    slots = lax.broadcasted_iota(jnp.int32, (count, count), 0)
    table = (slots == jnp.broadcast_to(ids_ref[...], (count, count))).astype(jnp.float32)
    placed = lax.dot_general(raw, table, NT, precision=lax.Precision.HIGHEST, preferred_element_type=jnp.float32)
    for j in range(raw.shape[0] // rows):
        out_ref[order_ref[j]] = placed[j * rows : (j + 1) * rows]


def place(order, ids, own, received, rows):
    return pl.pallas_call(
        functools.partial(place_kernel, rows),
        out_shape=jax.ShapeDtypeStruct((own.shape[0] // rows, rows, own.shape[1]), jnp.float32),
        in_specs=[SMEM, VMEM, VMEM, VMEM],
        out_specs=VMEM,
        compiler_params=pltpu.CompilerParams(vmem_limit_bytes=16 << 20),
        name="place_scores",
    )(order, ids, own, received)


def shards(fast, parts, total, queries, codes, exponents, example_ids):
    part = lax.axis_index("groups")
    here = lax.axis_index("ex")
    half = lax.axis_index("dim")
    slow = total // fast
    rows = queries.shape[1]
    count = codes.shape[0]
    blocks = exponents.shape[1]
    alone = blocks * 25 // 64
    shared = blocks - parts * alone
    held = alone + shared
    direct = held * 33 // 39

    def step(value, length, stride):
        pairs = [
            (i, i + stride if (i // stride) % length < length - 1 else i - (length - 1) * stride)
            for i in range(total)
        ]
        return lax.ppermute(value, "ex", pairs)

    def along_fast(value):
        values = [value]
        for _ in range(fast - 1):
            values.append(step(values[-1], fast, 1))
        return values

    first = part * (blocks - alone)
    rest = (1 - part) * (blocks - alone)

    def columns(array, start, width, unit=1):
        return lax.dynamic_slice(array, (0, start * unit), (array.shape[0], width * unit))

    mine = jnp.concatenate(
        [columns(queries[0], first, alone, BLOCK), columns(queries[0], alone, shared, BLOCK)], axis=1
    )
    cut = direct * BLOCK
    direct_columns = [mine[:, :cut]]
    for _ in range(slow - 1):
        direct_columns.append(step(direct_columns[-1], slow, fast))
    whole = along_fast(mine)
    pairs = [jnp.concatenate([block[:, cut:] for block in whole], axis=0)]
    for _ in range(slow - 1):
        pairs.append(step(pairs[-1], slow, fast))

    scales = (jnp.int32(1) << (exponents + 3)).astype(jnp.float32) * 0.125
    kept_scales = jnp.concatenate([columns(scales, first, alone), columns(scales, alone, shared)], axis=1)
    sent, ours = scale_codes(codes, jnp.stack([first, rest]), columns(scales, rest, alone), kept_scales, alone)
    swap = [(i, parts - 1 - i) for i in range(parts)]
    theirs = lax.ppermute(sent, "groups", swap)

    arrived = [[[block] for block in whole]]
    for s in range(1, slow):
        near = along_fast(direct_columns[s])
        arrived.append([[block, pairs[s][t * rows : (t + 1) * rows]] for t, block in enumerate(near)])

    def summed(steps):
        given = [pieces for s in steps for pieces in arrived[s]]
        if rows % 16:
            given = [[jnp.concatenate([block[0][:, :cut] for block in arrived[s]]), pairs[s]] for s in steps]
        sums = jnp.concatenate([score(given, [ours]), score(given, [theirs])], axis=1)
        sums = sums.reshape(-1, 2, rows // 2, 2 * count)
        keep = lax.dynamic_index_in_dim(sums, half, 1, keepdims=False)
        send = lax.dynamic_index_in_dim(sums, 1 - half, 1, keepdims=False)
        sums = keep + lax.ppermute(send, "dim", [(0, 1), (1, 0)])
        received = lax.ppermute(sums[..., count:], "groups", swap)
        return sums[..., :count].reshape(-1, count), received.reshape(-1, count)

    early, late = summed(range(slow - 1)), summed([slow - 1])
    own, received = (jnp.concatenate([e, l]) for e, l in zip(early, late))
    order = jnp.stack([
        lax.rem(here // fast + slow - s, slow) * fast + lax.rem(here % fast + fast - t, fast)
        for s in range(slow)
        for t in range(fast)
    ]).astype(jnp.int32)
    return place(order, example_ids, own, received, rows // 2)


def solution(mesh):
    placed = (
        P("ex", None, "dim"),
        P(("groups", "ex"), "dim"),
        P(("groups", "ex"), "dim"),
        P(("groups", "ex"), None),
    )
    return jax.shard_map(
        functools.partial(shards, fast_length(mesh), mesh.shape["groups"], mesh.shape["ex"]),
        mesh=mesh,
        in_specs=placed,
        out_specs=P(None, "dim", ("groups", "ex")),
        check_vma=False,
    )
```

```python
import functools

import jax
import jax.numpy as jnp
from jax import lax
from jax.experimental import pallas as pl
from jax.experimental.pallas import tpu as pltpu
from jax.sharding import PartitionSpec as P

BLOCK = 128
ALONE = 28
CHUNKS = 2
FIRST_VMEM = 60 << 20
VMEM = pl.BlockSpec(memory_space=pltpu.VMEM)
SMEM = pl.BlockSpec(memory_space=pltpu.SMEM)
NT = (((1,), (1,)), ((), ()))


def fast_length(mesh):
    line = list(mesh.devices[0, :, 0])
    size = len(line)
    if size < 2 or not all(hasattr(device, "coords") for device in line):
        return 2 if size % 2 == 0 else size

    def moved(a, b):
        return tuple(i for i, (p, q) in enumerate(zip(a.coords, b.coords)) if p != q)

    along = moved(line[0], line[1])
    length = 2
    while length < size and moved(line[0], line[length]) == along:
        length += 1
    return length if size % length == 0 else size


def scaled(codes, scales, at):
    return codes * scales[:, at : at + 1].astype(jnp.bfloat16)


def scales_of(exponents):
    powers = (jnp.int32(1) << (exponents + 3)).astype(jnp.float32) * 0.125
    return powers.T


def cut_kernel(alone, cuts, tile, part_ref, queries_ref, codes_ref, exponents_ref, *refs):
    *chunk_refs, sent_ref, codes_buffer, sent_buffer, query_sems, fetch_sems, store_sems = refs
    part = part_ref[0]
    blocks = exponents_ref.shape[0]
    far = (blocks - alone) * BLOCK
    first = pl.multiple_of(part * far, BLOCK)
    rest = pl.multiple_of((1 - part) * far, BLOCK)
    wide = alone * BLOCK

    copies = []

    def copy_columns(out_ref, start, stop):
        if start < wide:
            width = min(stop, wide) - start
            copies.append((
                queries_ref.at[0, :, pl.ds(pl.multiple_of(first + start, BLOCK), width)],
                out_ref.at[:, pl.ds(0, width)],
            ))
        if stop > wide:
            begin = max(start, wide)
            copies.append((
                queries_ref.at[0, :, pl.ds(begin, stop - begin)],
                out_ref.at[:, pl.ds(begin - start, stop - begin)],
            ))

    for out_ref, start, stop in zip(chunk_refs, cuts[:-1], cuts[1:]):
        copy_columns(out_ref, start, stop)
    moves = [pltpu.make_async_copy(a, b, query_sems.at[i]) for i, (a, b) in enumerate(copies)]
    tiles = codes_buffer.shape[0]

    def fetch(i):
        return pltpu.make_async_copy(
            codes_ref.at[pl.ds(i * tile, tile), pl.ds(rest, wide)], codes_buffer.at[i], fetch_sems.at[i]
        )

    def store(i):
        return pltpu.make_async_copy(sent_buffer.at[i], sent_ref.at[pl.ds(i * tile, tile)], store_sems.at[i])

    for i in range(tiles):
        fetch(i).start()
    for move in moves:
        move.start()
    near = exponents_ref[0:alone, :]
    away = exponents_ref[blocks - alone : blocks, :]
    pad = jnp.zeros((-alone % 8, near.shape[1]), jnp.int32)
    scales = scales_of(jnp.concatenate([jnp.where(part == 0, away, near), pad], axis=0))
    for i in range(tiles):
        fetch(i).wait()
        for block in range(alone):
            columns = slice(block * BLOCK, (block + 1) * BLOCK)
            sent_buffer[i, :, columns] = scaled(
                codes_buffer[i, :, columns], scales[i * tile : (i + 1) * tile], block
            )
        store(i).start()
    for move in moves:
        move.wait()
    for i in range(tiles):
        store(i).wait()


def cut(part, queries, codes, exponents, alone, cuts):
    rows = queries.shape[1]
    count = codes.shape[0]
    blocks = exponents.shape[0]
    tile = min(count, 64)
    tiles = count // tile
    anywhere = pl.BlockSpec(memory_space=pl.ANY)
    wide = alone * BLOCK
    chunks = len(cuts) - 1
    return pl.pallas_call(
        functools.partial(cut_kernel, alone, cuts, tile),
        out_shape=[jax.ShapeDtypeStruct((rows, b - a), jnp.bfloat16) for a, b in zip(cuts[:-1], cuts[1:])]
        + [jax.ShapeDtypeStruct((count, wide), jnp.bfloat16)],
        in_specs=[SMEM, anywhere, anywhere, VMEM],
        out_specs=[anywhere] * (chunks + 1),
        scratch_shapes=[
            pltpu.VMEM((tiles, tile, wide), jnp.bfloat16),
            pltpu.VMEM((tiles, tile, wide), jnp.bfloat16),
            pltpu.SemaphoreType.DMA((2 * chunks,)),
            pltpu.SemaphoreType.DMA((tiles,)),
            pltpu.SemaphoreType.DMA((tiles,)),
        ],
        compiler_params=pltpu.CompilerParams(vmem_limit_bytes=FIRST_VMEM),
        cost_estimate=pl.CostEstimate(flops=codes.size, bytes_accessed=2 * codes.size, transcendentals=0),
        name="cut_queries",
    )(part, queries, codes, exponents)


def scale_kernel(alone, part_ref, codes_ref, exponents_ref, out_ref):
    part = part_ref[0]
    blocks = exponents_ref.shape[0]
    far = blocks - alone
    own = jnp.where(part == 0, exponents_ref[0:alone, :], exponents_ref[far:blocks, :])
    kept = jnp.concatenate([own, exponents_ref[alone:far, :]], axis=0)
    pad = jnp.zeros((-kept.shape[0] % 8, kept.shape[1]), jnp.int32)
    scales = scales_of(jnp.concatenate([kept, pad], axis=0))
    for block in range(far):
        start = pl.multiple_of((part * far + block) * BLOCK, BLOCK) if block < alone else block * BLOCK
        out_ref[:, block * BLOCK : (block + 1) * BLOCK] = scaled(codes_ref[:, pl.ds(start, BLOCK)], scales, block)


def scale(part, codes, exponents, alone):
    shape = (codes.shape[0], (exponents.shape[0] - alone) * BLOCK)
    return pl.pallas_call(
        functools.partial(scale_kernel, alone),
        out_shape=jax.ShapeDtypeStruct(shape, jnp.bfloat16),
        in_specs=[SMEM, VMEM, VMEM],
        out_specs=VMEM,
        compiler_params=pltpu.CompilerParams(vmem_limit_bytes=16 << 20),
        cost_estimate=pl.CostEstimate(flops=codes.size, bytes_accessed=4 * codes.size, transcendentals=0),
        name="scale_codes",
    )(part, codes, exponents)


def product(pieces, grads_ref):
    total = None
    first = 0
    for refs in pieces:
        width = min(refs[0].shape[1], grads_ref.shape[1] - first)
        if width <= 0:
            break
        rows = [ref[:, :width] for ref in refs]
        rows = jnp.concatenate(rows, axis=0) if len(rows) > 1 else rows[0]
        term = lax.dot_general(rows, grads_ref[:, first : first + width], NT, preferred_element_type=jnp.float32)
        total = term if total is None else total + term
        first += width
    return total


def unflatten(layout, refs):
    refs = list(refs)
    return [[refs.pop(0) for _ in range(arrays)] for arrays in layout]


def score_kernel(layout, rows, half_ref, *refs):
    *query_refs, grads_ref, keep_ref, send_ref = refs
    total = product(unflatten(layout, query_refs), grads_ref)
    for j in range(total.shape[0] // rows):
        low = total[j * rows : j * rows + rows // 2]
        high = total[j * rows + rows // 2 : (j + 1) * rows]
        keep_ref[j] = jnp.where(half_ref[0] == 0, low, high)
        send_ref[j] = jnp.where(half_ref[0] == 0, high, low)


def score(half, rows, pieces, grads):
    operands = [array for arrays in pieces for array in arrays]
    stacked = sum(array.shape[0] for array in pieces[0])
    shape = jax.ShapeDtypeStruct((stacked // rows, rows // 2, grads.shape[0]), jnp.float32)
    return pl.pallas_call(
        functools.partial(score_kernel, [len(arrays) for arrays in pieces], rows),
        out_shape=[shape, shape],
        in_specs=[SMEM] + [VMEM] * (len(operands) + 1),
        out_specs=[VMEM, VMEM],
        compiler_params=pltpu.CompilerParams(vmem_limit_bytes=16 << 20),
        cost_estimate=pl.CostEstimate(
            flops=2 * stacked * grads.size, bytes_accessed=2 * grads.size, transcendentals=0
        ),
        name="score",
    )(half, *operands, grads)


def place_kernel(rows, order_ref, ids_ref, *refs):
    *share_refs, out_ref = refs
    count = ids_ref.shape[1]
    slots = lax.broadcasted_iota(jnp.int32, (count, count), 0)
    table = (slots == jnp.broadcast_to(ids_ref[...], (count, count))).astype(jnp.float32)
    j = 0
    for first in range(0, len(share_refs), 4):
        a, b, c, d = (ref[...] for ref in share_refs[first : first + 4])
        raw = (d + c) + (b + a)
        placed = lax.dot_general(
            raw, table, NT, precision=lax.Precision.HIGHEST, preferred_element_type=jnp.float32
        )
        for i in range(raw.shape[0] // rows):
            out_ref[order_ref[j]] = placed[i * rows : (i + 1) * rows]
            j += 1


def place(order, ids, shares, rows):
    return pl.pallas_call(
        functools.partial(place_kernel, rows),
        out_shape=jax.ShapeDtypeStruct((order.shape[0], rows, ids.shape[1]), jnp.float32),
        in_specs=[SMEM] + [VMEM] * (len(shares) + 1),
        out_specs=VMEM,
        compiler_params=pltpu.CompilerParams(vmem_limit_bytes=16 << 20),
        name="place_scores",
    )(order, ids, *shares)


def shards(fast, parts, total, queries, codes, exponents, example_ids):
    part = lax.axis_index("groups")
    here = lax.axis_index("ex")
    half = lax.axis_index("dim")[None]
    slow = total // fast
    rows = queries.shape[1]
    count = codes.shape[0]
    blocks = exponents.shape[1]
    alone = blocks * ALONE // 64
    held = blocks - alone
    cuts = [i * held // CHUNKS * BLOCK for i in range(CHUNKS + 1)]

    def step(value, length, stride):
        pairs = [
            (i, i + stride if (i // stride) % length < length - 1 else i - (length - 1) * stride)
            for i in range(total)
        ]
        return lax.ppermute(value, "ex", pairs)

    def along_fast(value):
        values = [value]
        for _ in range(fast - 1):
            values.append(step(values[-1], fast, 1))
        return values

    swap = [(i, parts - 1 - i) for i in range(parts)]
    by_block = exponents.T
    *chunks, sent = cut(part[None], queries, codes, by_block, alone, cuts)
    theirs = lax.ppermute(sent, "groups", swap)
    ours = scale(part[None], codes, by_block, alone)
    near = [[] for _ in range(slow)]
    for c, chunk in enumerate(chunks):
        for s in range(slow):
            values = along_fast(chunk)
            if s < slow - 1:
                chunk, *values = lax.optimization_barrier([step(chunk, slow, fast)] + values)
                if c == CHUNKS - 1 and s == 0:
                    chunk, ours = lax.optimization_barrier((chunk, ours))
            near[s].append(values)

    def stack(arrays):
        return arrays if rows % 16 == 0 else [jnp.concatenate(arrays, axis=0)]

    def pieces_of(steps):
        return [[a for s in steps for a in stack(near[s][c])] for c in range(CHUNKS)]

    across = [(i, 3 - i) for i in range(4)]
    shares = []
    for steps in (range(slow - 1), [slow - 1]):
        pieces = pieces_of(steps)
        keep, send = score(half, rows, pieces, theirs)
        theirs, keep, send = lax.optimization_barrier((theirs, keep, send))
        shares += [lax.ppermute(send, ("groups", "dim"), across), lax.ppermute(keep, "groups", swap)]
        keep, send = score(half, rows, pieces, ours)
        shares += [lax.ppermute(send, "dim", [(0, 1), (1, 0)]), keep]
    shares = [share.reshape(-1, count) for share in shares]
    order = jnp.stack([
        lax.rem(here // fast + slow - s, slow) * fast + lax.rem(here % fast + fast - t, fast)
        for s in range(slow)
        for t in range(fast)
    ]).astype(jnp.int32)
    return place(order, example_ids, shares, rows // 2)


def solution(mesh):
    placed = (
        P("ex", None, "dim"),
        P(("groups", "ex"), "dim"),
        P(("groups", "ex"), "dim"),
        P(("groups", "ex"), None),
    )
    return jax.shard_map(
        functools.partial(shards, fast_length(mesh), mesh.shape["groups"], mesh.shape["ex"]),
        mesh=mesh,
        in_specs=placed,
        out_specs=P(None, "dim", ("groups", "ex")),
        check_vma=False,
    )
```

```python
import functools

import jax
import jax.numpy as jnp
from jax import lax
from jax.experimental import pallas as pl
from jax.experimental.pallas import tpu as pltpu
from jax.sharding import PartitionSpec as P

BLOCK = 128
ALONE = 28
CHUNKS = 2
VMEM = pl.BlockSpec(memory_space=pltpu.VMEM)
SMEM = pl.BlockSpec(memory_space=pltpu.SMEM)
NT = (((1,), (1,)), ((), ()))


def in_vmem(arrays):
    return [pltpu.with_memory_space_constraint(array, pltpu.VMEM) for array in arrays]


def in_hbm(array):
    return pltpu.with_memory_space_constraint(array, pltpu.HBM)


def fast_length(mesh):
    line = list(mesh.devices[0, :, 0])
    size = len(line)
    if size < 2 or not all(hasattr(device, "coords") for device in line):
        return 2 if size % 2 == 0 else size

    def moved(a, b):
        return tuple(i for i, (p, q) in enumerate(zip(a.coords, b.coords)) if p != q)

    along = moved(line[0], line[1])
    length = 2
    while length < size and moved(line[0], line[length]) == along:
        length += 1
    return length if size % length == 0 else size


def scaled(codes, scales, at):
    return codes * scales[:, at : at + 1].astype(jnp.bfloat16)


def scales_of(exponents):
    powers = (jnp.int32(1) << (exponents + 3)).astype(jnp.float32) * 0.125
    return powers.T


def cut_kernel(alone, cuts, tile, part_ref, queries_ref, codes_ref, exponents_ref, *refs):
    *chunk_refs, sent_ref, codes_buffer, powers, query_sems, fetch_sems, powers_sem = refs
    part = part_ref[0]
    blocks = exponents_ref.shape[0]
    far = (blocks - alone) * BLOCK
    first = pl.multiple_of(part * far, BLOCK)
    rest = pl.multiple_of((1 - part) * far, BLOCK)
    wide = alone * BLOCK

    copies = []

    def copy_columns(out_ref, start, stop):
        if start < wide:
            width = min(stop, wide) - start
            copies.append((
                queries_ref.at[0, :, pl.ds(pl.multiple_of(first + start, BLOCK), width)],
                out_ref.at[:, pl.ds(0, width)],
            ))
        if stop > wide:
            begin = max(start, wide)
            copies.append((
                queries_ref.at[0, :, pl.ds(begin, stop - begin)],
                out_ref.at[:, pl.ds(begin - start, stop - begin)],
            ))

    for out_ref, start, stop in zip(chunk_refs, cuts[:-1], cuts[1:]):
        copy_columns(out_ref, start, stop)
    moves = [pltpu.make_async_copy(a, b, query_sems.at[i]) for i, (a, b) in enumerate(copies)]
    tiles = codes_buffer.shape[0]

    def fetch(i):
        return pltpu.make_async_copy(
            codes_ref.at[pl.ds(i * tile, tile), pl.ds(rest, wide)], codes_buffer.at[i], fetch_sems.at[i]
        )

    powers_copy = pltpu.make_async_copy(exponents_ref, powers, powers_sem)
    powers_copy.start()
    for i in range(tiles):
        fetch(i).start()
    for move in moves:
        move.start()
    powers_copy.wait()
    near = powers[0:alone, :]
    away = powers[blocks - alone : blocks, :]
    pad = jnp.zeros((-alone % 8, near.shape[1]), jnp.int32)
    scales = scales_of(jnp.concatenate([jnp.where(part == 0, away, near), pad], axis=0))
    for i in range(tiles):
        fetch(i).wait()
        for block in range(alone):
            columns = slice(block * BLOCK, (block + 1) * BLOCK)
            sent_ref[i * tile : (i + 1) * tile, columns] = scaled(
                codes_buffer[i, :, columns], scales[i * tile : (i + 1) * tile], block
            )
    for move in moves:
        move.wait()


def cut(part, queries, codes, exponents, alone, cuts):
    rows = queries.shape[1]
    count = codes.shape[0]
    tile = min(count, 64)
    tiles = count // tile
    anywhere = pl.BlockSpec(memory_space=pl.ANY)
    wide = alone * BLOCK
    chunks = len(cuts) - 1
    return pl.pallas_call(
        functools.partial(cut_kernel, alone, cuts, tile),
        out_shape=[pltpu.VMEM((rows, b - a), jnp.bfloat16) for a, b in zip(cuts[:-1], cuts[1:])]
        + [pltpu.VMEM((count, wide), jnp.bfloat16)],
        in_specs=[SMEM, anywhere, anywhere, anywhere],
        out_specs=[VMEM] * (chunks + 1),
        scratch_shapes=[
            pltpu.VMEM((tiles, tile, wide), jnp.bfloat16),
            pltpu.VMEM(exponents.shape, exponents.dtype),
            pltpu.SemaphoreType.DMA((2 * chunks,)),
            pltpu.SemaphoreType.DMA((tiles,)),
            pltpu.SemaphoreType.DMA,
        ],
        compiler_params=pltpu.CompilerParams(vmem_limit_bytes=16 << 20),
        cost_estimate=pl.CostEstimate(flops=codes.size, bytes_accessed=2 * codes.size, transcendentals=0),
        name="cut_queries",
    )(part, in_hbm(queries), in_hbm(codes), in_hbm(exponents))


def scale_kernel(alone, tile, part_ref, codes_ref, exponents_ref, out_ref, buffer, powers, sems, powers_sem):
    part = part_ref[0]
    blocks = exponents_ref.shape[0]
    far = blocks - alone
    tiles = buffer.shape[0]

    def fetch(i):
        start = pl.multiple_of(part * alone * BLOCK, BLOCK)
        return pltpu.make_async_copy(
            codes_ref.at[pl.ds(i * tile, tile), pl.ds(start, far * BLOCK)], buffer.at[i], sems.at[i]
        )

    powers_copy = pltpu.make_async_copy(exponents_ref, powers, powers_sem)
    powers_copy.start()
    for i in range(tiles):
        fetch(i).start()
    powers_copy.wait()
    own = jnp.where(part == 0, powers[0:alone, :], powers[far:blocks, :])
    kept = jnp.concatenate([own, powers[alone:far, :]], axis=0)
    pad = jnp.zeros((-kept.shape[0] % 8, kept.shape[1]), jnp.int32)
    scales = scales_of(jnp.concatenate([kept, pad], axis=0))
    shared = far - alone
    for i in range(tiles):
        fetch(i).wait()
        rows = slice(i * tile, (i + 1) * tile)
        for block in range(far):
            at = block + part * shared if block < alone else block - part * alone
            columns = pl.ds(pl.multiple_of(at * BLOCK, BLOCK), BLOCK)
            out_ref[rows, block * BLOCK : (block + 1) * BLOCK] = scaled(buffer[i, :, columns], scales[rows], block)


def scale(part, codes, exponents, alone):
    count = codes.shape[0]
    width = (exponents.shape[0] - alone) * BLOCK
    tile = min(count, 64)
    return pl.pallas_call(
        functools.partial(scale_kernel, alone, tile),
        out_shape=pltpu.VMEM((count, width), jnp.bfloat16),
        in_specs=[SMEM] + [pl.BlockSpec(memory_space=pl.ANY)] * 2,
        out_specs=VMEM,
        scratch_shapes=[
            pltpu.VMEM((count // tile, tile, width), jnp.bfloat16),
            pltpu.VMEM(exponents.shape, exponents.dtype),
            pltpu.SemaphoreType.DMA((count // tile,)),
            pltpu.SemaphoreType.DMA,
        ],
        compiler_params=pltpu.CompilerParams(vmem_limit_bytes=16 << 20),
        cost_estimate=pl.CostEstimate(flops=codes.size, bytes_accessed=4 * codes.size, transcendentals=0),
        name="scale_codes",
    )(part, in_hbm(codes), in_hbm(exponents))


def product(pieces, grads_ref):
    total = None
    first = 0
    for refs in pieces:
        width = min(refs[0].shape[1], grads_ref.shape[1] - first)
        if width <= 0:
            break
        rows = [ref[:, :width] for ref in refs]
        rows = jnp.concatenate(rows, axis=0) if len(rows) > 1 else rows[0]
        term = lax.dot_general(rows, grads_ref[:, first : first + width], NT, preferred_element_type=jnp.float32)
        total = term if total is None else total + term
        first += width
    return total


def unflatten(layout, refs):
    refs = list(refs)
    return [[refs.pop(0) for _ in range(arrays)] for arrays in layout]


def score_kernel(layout, rows, half_ref, *refs):
    *query_refs, grads_ref, keep_ref, send_ref = refs
    total = product(unflatten(layout, query_refs), grads_ref)
    for j in range(total.shape[0] // rows):
        low = total[j * rows : j * rows + rows // 2]
        high = total[j * rows + rows // 2 : (j + 1) * rows]
        keep_ref[j] = jnp.where(half_ref[0] == 0, low, high)
        send_ref[j] = jnp.where(half_ref[0] == 0, high, low)


def score(half, rows, pieces, grads):
    operands = [array for arrays in pieces for array in arrays]
    stacked = sum(array.shape[0] for array in pieces[0])
    shape = pltpu.VMEM((stacked // rows, rows // 2, grads.shape[0]), jnp.float32)
    return pl.pallas_call(
        functools.partial(score_kernel, [len(arrays) for arrays in pieces], rows),
        out_shape=[shape, shape],
        in_specs=[SMEM] + [VMEM] * (len(operands) + 1),
        out_specs=[VMEM, VMEM],
        compiler_params=pltpu.CompilerParams(vmem_limit_bytes=16 << 20),
        cost_estimate=pl.CostEstimate(
            flops=2 * stacked * grads.size, bytes_accessed=2 * grads.size, transcendentals=0
        ),
        name="score",
    )(half, *in_vmem([*operands, grads]))


def place_kernel(rows, order_ref, ids_ref, *refs):
    *share_refs, out_ref = refs
    count = ids_ref.shape[1]
    slots = lax.broadcasted_iota(jnp.int32, (count, count), 0)
    table = (slots == jnp.broadcast_to(ids_ref[...], (count, count))).astype(jnp.float32)
    j = 0
    for first in range(0, len(share_refs), 4):
        a, b, c, d = (ref[...] for ref in share_refs[first : first + 4])
        raw = (d + c) + (b + a)
        placed = lax.dot_general(
            raw, table, NT, precision=lax.Precision.HIGHEST, preferred_element_type=jnp.float32
        )
        for i in range(raw.shape[0] // rows):
            out_ref[order_ref[j]] = placed[i * rows : (i + 1) * rows]
            j += 1


def place(order, ids, shares, rows):
    return pl.pallas_call(
        functools.partial(place_kernel, rows),
        out_shape=jax.ShapeDtypeStruct((order.shape[0], rows, ids.shape[1]), jnp.float32),
        in_specs=[SMEM] + [VMEM] * (len(shares) + 1),
        out_specs=VMEM,
        compiler_params=pltpu.CompilerParams(vmem_limit_bytes=16 << 20),
        name="place_scores",
    )(order, ids, *in_vmem(shares))


def shards(fast, parts, total, queries, codes, exponents, example_ids):
    part = lax.axis_index("groups")
    here = lax.axis_index("ex")
    half = lax.axis_index("dim")[None]
    slow = total // fast
    rows = queries.shape[1]
    count = codes.shape[0]
    blocks = exponents.shape[1]
    alone = blocks * ALONE // 64
    held = blocks - alone
    cuts = [i * held // CHUNKS * BLOCK for i in range(CHUNKS + 1)]

    def step(value, length, stride):
        pairs = [
            (i, i + stride if (i // stride) % length < length - 1 else i - (length - 1) * stride)
            for i in range(total)
        ]
        return lax.ppermute(value, "ex", pairs)

    def along_fast(value):
        values = [value]
        for _ in range(fast - 1):
            values.append(step(values[-1], fast, 1))
        return values

    swap = [(i, parts - 1 - i) for i in range(parts)]
    by_block = exponents.T
    *chunks, sent = cut(part[None], queries, codes, by_block, alone, cuts)
    theirs = lax.ppermute(sent, "groups", swap)
    ours = scale(part[None], codes, by_block, alone)
    near = [[] for _ in range(slow)]
    for c, chunk in enumerate(chunks):
        for s in range(slow):
            values = along_fast(chunk)
            if s < slow - 1:
                chunk, *values = lax.optimization_barrier([step(chunk, slow, fast)] + values)
                if c == CHUNKS - 1 and s == 0:
                    chunk, ours = lax.optimization_barrier((chunk, ours))
            near[s].append(values)

    def stack(arrays):
        return arrays if rows % 16 == 0 else [jnp.concatenate(arrays, axis=0)]

    def pieces_of(steps):
        return [[a for s in steps for a in stack(near[s][c])] for c in range(CHUNKS)]

    across = [(i, 3 - i) for i in range(4)]
    shares = []
    for steps in (range(slow - 1), [slow - 1]):
        pieces = pieces_of(steps)
        keep, send = score(half, rows, pieces, theirs)
        theirs, keep, send = lax.optimization_barrier((theirs, keep, send))
        shares += [lax.ppermute(send, ("groups", "dim"), across), lax.ppermute(keep, "groups", swap)]
        keep, send = score(half, rows, pieces, ours)
        shares += [lax.ppermute(send, "dim", [(0, 1), (1, 0)]), keep]
    shares = [share.reshape(-1, count) for share in shares]
    order = jnp.stack([
        lax.rem(here // fast + slow - s, slow) * fast + lax.rem(here % fast + fast - t, fast)
        for s in range(slow)
        for t in range(fast)
    ]).astype(jnp.int32)
    return place(order, example_ids, shares, rows // 2)


def solution(mesh):
    placed = (
        P("ex", None, "dim"),
        P(("groups", "ex"), "dim"),
        P(("groups", "ex"), "dim"),
        P(("groups", "ex"), None),
    )
    return jax.shard_map(
        functools.partial(shards, fast_length(mesh), mesh.shape["groups"], mesh.shape["ex"]),
        mesh=mesh,
        in_specs=placed,
        out_specs=P(None, "dim", ("groups", "ex")),
        check_vma=False,
    )
```

```python
import functools

import jax
import jax.numpy as jnp
from jax import lax
from jax.experimental import pallas as pl
from jax.experimental.pallas import tpu as pltpu
from jax.sharding import PartitionSpec as P

BLOCK = 128
ALONE = 28
RUN = 6 * BLOCK
CHUNKS = 2
VMEM = pl.BlockSpec(memory_space=pltpu.VMEM)
SMEM = pl.BlockSpec(memory_space=pltpu.SMEM)
NT = (((1,), (1,)), ((), ()))


def in_vmem(arrays):
    return [pltpu.with_memory_space_constraint(array, pltpu.VMEM) for array in arrays]


def in_hbm(array):
    return pltpu.with_memory_space_constraint(array, pltpu.HBM)


def fast_length(mesh):
    line = list(mesh.devices[0, :, 0])
    size = len(line)
    if size < 2 or not all(hasattr(device, "coords") for device in line):
        return 2 if size % 2 == 0 else size

    def moved(a, b):
        return tuple(i for i, (p, q) in enumerate(zip(a.coords, b.coords)) if p != q)

    along = moved(line[0], line[1])
    length = 2
    while length < size and moved(line[0], line[length]) == along:
        length += 1
    return length if size % length == 0 else size


def scaled(codes, scales, at):
    return codes * scales[:, at : at + 1].astype(jnp.bfloat16)


def scales_of(exponents):
    return (jnp.int32(1) << (exponents + 3)).astype(jnp.float32) * 0.125


def by_example(scales):
    pad = jnp.zeros((-scales.shape[0] % 8, scales.shape[1]), scales.dtype)
    return jnp.concatenate([scales, pad], axis=0).T


def cut_kernel(alone, cuts, part_ref, queries_ref, codes_ref, exponents_ref, *refs):
    *chunk_refs, sent_ref, sent_scales_ref, powers, sems = refs
    part = part_ref[0]
    blocks = exponents_ref.shape[0]
    far = (blocks - alone) * BLOCK
    first = pl.multiple_of(part * far, BLOCK)
    rest = pl.multiple_of((1 - part) * far, BLOCK)
    wide = alone * BLOCK
    copies = [(exponents_ref, powers)]
    for out_ref, start, stop in zip(chunk_refs, cuts[:-1], cuts[1:]):
        if start < wide:
            width = min(stop, wide) - start
            copies.append((
                queries_ref.at[0, :, pl.ds(pl.multiple_of(first + start, BLOCK), width)],
                out_ref.at[:, pl.ds(0, width)],
            ))
        if stop > wide:
            begin = max(start, wide)
            copies.append((
                queries_ref.at[0, :, pl.ds(begin, stop - begin)],
                out_ref.at[:, pl.ds(begin - start, stop - begin)],
            ))
    copies.append((codes_ref.at[:, pl.ds(rest, wide)], sent_ref))
    copies = [pltpu.make_async_copy(a, b, sems.at[i]) for i, (a, b) in enumerate(copies)]
    for copy in copies:
        copy.start()
    copies[0].wait()
    near = powers[0:alone, :]
    away = powers[blocks - alone : blocks, :]
    sent_scales_ref[...] = scales_of(jnp.where(part == 0, away, near))
    for copy in copies[1:]:
        copy.wait()


def cut(part, queries, codes, exponents, alone, cuts):
    rows = queries.shape[1]
    count = codes.shape[0]
    anywhere = pl.BlockSpec(memory_space=pl.ANY)
    wide = alone * BLOCK
    chunks = len(cuts) - 1
    return pl.pallas_call(
        functools.partial(cut_kernel, alone, cuts),
        out_shape=[pltpu.VMEM((rows, b - a), jnp.bfloat16) for a, b in zip(cuts[:-1], cuts[1:])]
        + [pltpu.VMEM((count, wide), jnp.bfloat16), pltpu.VMEM((alone, count), jnp.float32)],
        in_specs=[SMEM, anywhere, anywhere, anywhere],
        out_specs=[VMEM] * (chunks + 2),
        scratch_shapes=[
            pltpu.VMEM(exponents.shape, exponents.dtype),
            pltpu.SemaphoreType.DMA((2 * chunks + 2,)),
        ],
        compiler_params=pltpu.CompilerParams(vmem_limit_bytes=16 << 20),
        cost_estimate=pl.CostEstimate(flops=0, bytes_accessed=2 * codes.size, transcendentals=0),
        name="cut_queries",
    )(part, in_hbm(queries), in_hbm(codes), in_hbm(exponents))


def scale_kernel(alone, tile, part_ref, codes_ref, exponents_ref, out_ref, buffer, powers, sems, powers_sem):
    part = part_ref[0]
    blocks = exponents_ref.shape[0]
    far = blocks - alone
    tiles = buffer.shape[0]

    def fetch(i):
        start = pl.multiple_of(part * alone * BLOCK, BLOCK)
        return pltpu.make_async_copy(
            codes_ref.at[pl.ds(i * tile, tile), pl.ds(start, far * BLOCK)], buffer.at[i], sems.at[i]
        )

    powers_copy = pltpu.make_async_copy(exponents_ref, powers, powers_sem)
    powers_copy.start()
    for i in range(tiles):
        fetch(i).start()
    powers_copy.wait()
    own = jnp.where(part == 0, powers[0:alone, :], powers[far:blocks, :])
    kept = jnp.concatenate([own, powers[alone:far, :]], axis=0)
    scales = by_example(scales_of(kept))
    shared = far - alone
    for i in range(tiles):
        fetch(i).wait()
        rows = slice(i * tile, (i + 1) * tile)
        for block in range(far):
            at = block + part * shared if block < alone else block - part * alone
            columns = pl.ds(pl.multiple_of(at * BLOCK, BLOCK), BLOCK)
            out_ref[rows, block * BLOCK : (block + 1) * BLOCK] = scaled(buffer[i, :, columns], scales[rows], block)


def scale(part, codes, exponents, alone):
    count = codes.shape[0]
    width = (exponents.shape[0] - alone) * BLOCK
    tile = min(count, 64)
    return pl.pallas_call(
        functools.partial(scale_kernel, alone, tile),
        out_shape=pltpu.VMEM((count, width), jnp.bfloat16),
        in_specs=[SMEM] + [pl.BlockSpec(memory_space=pl.ANY)] * 2,
        out_specs=VMEM,
        scratch_shapes=[
            pltpu.VMEM((count // tile, tile, width), jnp.bfloat16),
            pltpu.VMEM(exponents.shape, exponents.dtype),
            pltpu.SemaphoreType.DMA((count // tile,)),
            pltpu.SemaphoreType.DMA,
        ],
        compiler_params=pltpu.CompilerParams(vmem_limit_bytes=16 << 20),
        cost_estimate=pl.CostEstimate(flops=codes.size, bytes_accessed=4 * codes.size, transcendentals=0),
        name="scale_codes",
    )(part, in_hbm(codes), in_hbm(exponents))


def stash_kernel(row, *refs):
    *array_refs, out_ref = refs
    array_refs = array_refs[1:] if row else array_refs
    for ref in array_refs:
        out_ref[row : row + ref.shape[0]] = ref[...]
        row += ref.shape[0]


def stash(held, arrays, row, rows):
    operands = ([held] if row else []) + arrays
    return pl.pallas_call(
        functools.partial(stash_kernel, row),
        out_shape=pltpu.VMEM((rows, arrays[0].shape[1]), arrays[0].dtype),
        in_specs=[VMEM] * len(operands),
        out_specs=VMEM,
        input_output_aliases={0: 0} if row else {},
        compiler_params=pltpu.CompilerParams(vmem_limit_bytes=16 << 20),
        cost_estimate=pl.CostEstimate(flops=0, bytes_accessed=4 * sum(a.size for a in arrays), transcendentals=0),
        name="stash",
    )(*in_vmem(operands))


def dot(rows, grads):
    return lax.dot_general(rows, grads, NT, preferred_element_type=jnp.float32)


def stacked(refs, columns):
    rows = [ref[:, columns] for ref in refs]
    return jnp.concatenate(rows, axis=0) if len(rows) > 1 else rows[0]


def halves(half, total, rows, keep_ref, send_ref):
    for j in range(total.shape[0] // rows):
        low = total[j * rows : j * rows + rows // 2]
        high = total[j * rows + rows // 2 : (j + 1) * rows]
        keep_ref[j] = jnp.where(half == 0, low, high)
        send_ref[j] = jnp.where(half == 0, high, low)


def product(pieces, grads_ref):
    total = None
    first = 0
    for refs in pieces:
        width = min(refs[0].shape[1], grads_ref.shape[1] - first)
        if width <= 0:
            break
        term = dot(stacked(refs, slice(0, width)), grads_ref[:, first : first + width])
        total = term if total is None else total + term
        first += width
    return total


def score_kernel(counts, grads_given, rows, half_ref, *refs):
    refs = list(refs)
    pieces = [[refs.pop(0) for _ in range(arrays)] for arrays in counts]
    grad_refs, outs = refs[:grads_given], refs[grads_given:]
    for i, grads_ref in enumerate(grad_refs):
        halves(half_ref[0], product(pieces, grads_ref), rows, *outs[2 * i : 2 * i + 2])


def score(half, rows, pieces, grads):
    operands = [array for arrays in pieces for array in arrays]
    height = sum(array.shape[0] for array in pieces[0])
    shape = pltpu.VMEM((height // rows, rows // 2, grads[0].shape[0]), jnp.float32)
    return pl.pallas_call(
        functools.partial(score_kernel, [len(arrays) for arrays in pieces], len(grads), rows),
        out_shape=[shape] * (2 * len(grads)),
        in_specs=[SMEM] + [VMEM] * (len(operands) + len(grads)),
        out_specs=[VMEM] * (2 * len(grads)),
        compiler_params=pltpu.CompilerParams(vmem_limit_bytes=16 << 20),
        cost_estimate=pl.CostEstimate(
            flops=2 * height * sum(g.size for g in grads), bytes_accessed=2 * grads[0].size, transcendentals=0
        ),
        name="score",
    )(half, *in_vmem([*operands, *grads]))


def received_kernel(pieces_given, runs, rows, half_ref, codes_ref, scales_ref, *refs):
    *piece_refs, grads_ref, keep_ref, send_ref, buffer, sems = refs

    def fetch(i):
        _, start, width, _ = runs[i]
        columns = pl.ds(start, width)
        return pltpu.make_async_copy(codes_ref.at[:, columns], buffer.at[:, columns], sems.at[i])

    for i in range(len(runs)):
        fetch(i).start()
    scales = by_example(scales_ref[...])
    total = None
    for i, (piece, start, width, at) in enumerate(runs):
        fetch(i).wait()
        for first in range(start, start + width, BLOCK):
            columns = slice(first, first + BLOCK)
            grads_ref[:, columns] = scaled(buffer[:, columns], scales, first // BLOCK)
        term = dot(piece_refs[piece][:, at : at + width], grads_ref[:, start : start + width])
        total = term if total is None else total + term
    halves(half_ref[0], total, rows, keep_ref, send_ref)


def score_received(half, rows, pieces, codes, scales):
    runs = []
    first = 0
    for i, piece in enumerate(pieces):
        width = min(piece.shape[1], codes.shape[1] - first)
        for at in range(0, max(width, 0), RUN):
            runs.append((i, first + at, min(RUN, width - at), at))
        first += max(width, 0)
    height = pieces[0].shape[0]
    shape = pltpu.VMEM((height // rows, rows // 2, codes.shape[0]), jnp.float32)
    return pl.pallas_call(
        functools.partial(received_kernel, len(pieces), runs, rows),
        out_shape=[pltpu.VMEM(codes.shape, codes.dtype), shape, shape],
        in_specs=[SMEM, pl.BlockSpec(memory_space=pl.ANY)] + [VMEM] * (len(pieces) + 1),
        out_specs=[VMEM] * 3,
        scratch_shapes=[pltpu.VMEM(codes.shape, codes.dtype), pltpu.SemaphoreType.DMA((len(runs),))],
        compiler_params=pltpu.CompilerParams(vmem_limit_bytes=16 << 20),
        cost_estimate=pl.CostEstimate(
            flops=2 * height * codes.size, bytes_accessed=2 * codes.size, transcendentals=0
        ),
        name="score_received",
    )(half, in_hbm(codes), *in_vmem([scales, *pieces]))


def place_kernel(rows, order_ref, ids_ref, *refs):
    *share_refs, out_ref = refs
    count = ids_ref.shape[1]
    slots = lax.broadcasted_iota(jnp.int32, (count, count), 0)
    table = (slots == jnp.broadcast_to(ids_ref[...], (count, count))).astype(jnp.float32)
    j = 0
    for first in range(0, len(share_refs), 4):
        a, b, c, d = (ref[...] for ref in share_refs[first : first + 4])
        raw = (d + c) + (b + a)
        placed = lax.dot_general(
            raw, table, NT, precision=lax.Precision.HIGHEST, preferred_element_type=jnp.float32
        )
        for i in range(raw.shape[0] // rows):
            out_ref[order_ref[j]] = placed[i * rows : (i + 1) * rows]
            j += 1


def place(order, ids, shares, rows):
    return pl.pallas_call(
        functools.partial(place_kernel, rows),
        out_shape=jax.ShapeDtypeStruct((order.shape[0], rows, ids.shape[1]), jnp.float32),
        in_specs=[SMEM] + [VMEM] * (len(shares) + 1),
        out_specs=VMEM,
        compiler_params=pltpu.CompilerParams(vmem_limit_bytes=16 << 20),
        name="place_scores",
    )(order, ids, *in_vmem(shares))


def shards(fast, parts, total, queries, codes, exponents, example_ids):
    part = lax.axis_index("groups")
    here = lax.axis_index("ex")
    half = lax.axis_index("dim")[None]
    slow = total // fast
    rows = queries.shape[1]
    count = codes.shape[0]
    blocks = exponents.shape[1]
    alone = blocks * ALONE // 64
    held = blocks - alone
    cuts = [i * held // CHUNKS * BLOCK for i in range(CHUNKS + 1)]

    def step(value, length, stride):
        pairs = [
            (i, i + stride if (i // stride) % length < length - 1 else i - (length - 1) * stride)
            for i in range(total)
        ]
        return lax.ppermute(value, "ex", pairs)

    def along_fast(value):
        values = [value]
        for _ in range(fast - 1):
            values.append(step(values[-1], fast, 1))
        return values

    swap = [(i, parts - 1 - i) for i in range(parts)]
    by_block = exponents.T
    *chunks, sent, sent_scales = cut(part[None], queries, codes, by_block, alone, cuts)
    theirs = lax.ppermute(sent, "groups", swap)
    their_scales = lax.ppermute(sent_scales, "groups", swap)
    ours = scale(part[None], codes, by_block, alone)

    def stack(arrays):
        return arrays if rows % 16 == 0 else [jnp.concatenate(arrays, axis=0)]

    early_rows = (slow - 1) * fast * rows
    early, late = [], []
    for c, chunk in enumerate(chunks):
        held = []
        for s in range(slow):
            values = along_fast(chunk)
            if s == slow - 1:
                late.append(stack(values))
                break
            tied = [step(chunk, slow, fast), *values] + held
            if c == CHUNKS - 1 and s == 0:
                *tied, ours, their_scales = lax.optimization_barrier(tied + [ours, their_scales])
            else:
                tied = lax.optimization_barrier(tied)
            chunk, values, held = tied[0], tied[1 : fast + 1], tied[fast + 1 :]
            held = [stash(held[0] if s else None, stack(values), s * fast * rows, early_rows)]
        early += held

    def shares_of(their_keep, their_send, keep, send):
        across = [(i, 3 - i) for i in range(4)]
        shares = [
            lax.ppermute(their_send, ("groups", "dim"), across),
            lax.ppermute(their_keep, "groups", swap),
            lax.ppermute(send, "dim", [(0, 1), (1, 0)]),
            keep,
        ]
        return [share.reshape(-1, count) for share in shares]

    theirs, *their_early = score_received(half, rows, early, theirs, their_scales)
    theirs, *their_early = lax.optimization_barrier((theirs, *their_early))
    shares = shares_of(*their_early, *score(half, rows, [[held] for held in early], [ours]))
    shares += shares_of(*score(half, rows, late, [theirs, ours]))
    order = jnp.stack([
        lax.rem(here // fast + slow - s, slow) * fast + lax.rem(here % fast + fast - t, fast)
        for s in range(slow)
        for t in range(fast)
    ]).astype(jnp.int32)
    return place(order, example_ids, shares, rows // 2)


def solution(mesh):
    placed = (
        P("ex", None, "dim"),
        P(("groups", "ex"), "dim"),
        P(("groups", "ex"), "dim"),
        P(("groups", "ex"), None),
    )
    return jax.shard_map(
        functools.partial(shards, fast_length(mesh), mesh.shape["groups"], mesh.shape["ex"]),
        mesh=mesh,
        in_specs=placed,
        out_specs=P(None, "dim", ("groups", "ex")),
        check_vma=False,
    )
```

```python
import functools

import jax
import jax.numpy as jnp
from jax import lax
from jax.experimental import pallas as pl
from jax.experimental.pallas import tpu as pltpu
from jax.sharding import PartitionSpec as P

BLOCK = 128
ALONE = 28
CHUNKS = 2
VMEM = pl.BlockSpec(memory_space=pltpu.VMEM)
SMEM = pl.BlockSpec(memory_space=pltpu.SMEM)
NT = (((1,), (1,)), ((), ()))


def in_vmem(arrays):
    return [pltpu.with_memory_space_constraint(array, pltpu.VMEM) for array in arrays]


def in_hbm(array):
    return pltpu.with_memory_space_constraint(array, pltpu.HBM)


def fast_length(mesh):
    line = list(mesh.devices[0, :, 0])
    size = len(line)
    if size < 2 or not all(hasattr(device, "coords") for device in line):
        return 2 if size % 2 == 0 else size

    def moved(a, b):
        return tuple(i for i, (p, q) in enumerate(zip(a.coords, b.coords)) if p != q)

    along = moved(line[0], line[1])
    length = 2
    while length < size and moved(line[0], line[length]) == along:
        length += 1
    return length if size % length == 0 else size


def scaled(codes, scales, at):
    return codes * scales[:, at : at + 1].astype(jnp.bfloat16)


def scales_of(exponents):
    return (jnp.int32(1) << (exponents + 3)).astype(jnp.float32) * 0.125


def by_example(scales):
    pad = jnp.zeros((-scales.shape[0] % 8, scales.shape[1]), scales.dtype)
    return jnp.concatenate([scales, pad], axis=0).T


def cut_kernel(alone, blocks, cuts, part_ref, queries_ref, *refs):
    *chunk_refs, sems = refs
    first = pl.multiple_of(part_ref[0] * (blocks - alone) * BLOCK, BLOCK)
    wide = alone * BLOCK
    copies = []
    for out_ref, start, stop in zip(chunk_refs, cuts[:-1], cuts[1:]):
        if start < wide:
            width = min(stop, wide) - start
            copies.append((
                queries_ref.at[0, :, pl.ds(pl.multiple_of(first + start, BLOCK), width)],
                out_ref.at[:, pl.ds(0, width)],
            ))
        if stop > wide:
            begin = max(start, wide)
            copies.append((
                queries_ref.at[0, :, pl.ds(begin, stop - begin)],
                out_ref.at[:, pl.ds(begin - start, stop - begin)],
            ))
    copies = [pltpu.make_async_copy(a, b, sems.at[i]) for i, (a, b) in enumerate(copies)]
    for copy in copies:
        copy.start()
    for copy in copies:
        copy.wait()


def cut(part, queries, alone, cuts):
    rows = queries.shape[1]
    chunks = len(cuts) - 1
    return pl.pallas_call(
        functools.partial(cut_kernel, alone, queries.shape[2] // BLOCK, cuts),
        out_shape=[pltpu.VMEM((rows, b - a), jnp.bfloat16) for a, b in zip(cuts[:-1], cuts[1:])],
        in_specs=[SMEM, pl.BlockSpec(memory_space=pl.ANY)],
        out_specs=[VMEM] * chunks,
        scratch_shapes=[pltpu.SemaphoreType.DMA((2 * chunks,))],
        compiler_params=pltpu.CompilerParams(vmem_limit_bytes=16 << 20),
        cost_estimate=pl.CostEstimate(flops=0, bytes_accessed=2 * queries.size, transcendentals=0),
        name="cut_queries",
    )(part, in_hbm(queries))


def scale_kernel(alone, tile, sent, part_ref, codes_ref, exponents_ref, out_ref, buffer, powers, sems, powers_sem):
    part = part_ref[0]
    blocks = exponents_ref.shape[0]
    far = blocks - alone
    shared = far - alone
    tiles, _, width = buffer.shape
    begin = (1 - part) * far if sent else part * alone

    def fetch(i):
        start = pl.multiple_of(begin * BLOCK, BLOCK)
        return pltpu.make_async_copy(
            codes_ref.at[pl.ds(i * tile, tile), pl.ds(start, width)], buffer.at[i], sems.at[i]
        )

    powers_copy = pltpu.make_async_copy(exponents_ref, powers, powers_sem)
    powers_copy.start()
    for i in range(tiles):
        fetch(i).start()
    powers_copy.wait()
    near, away = powers[0:alone, :], powers[far:blocks, :]
    if sent:
        scales = by_example(scales_of(jnp.where(part == 0, away, near)))
    else:
        own = jnp.where(part == 0, near, away)
        scales = by_example(scales_of(jnp.concatenate([own, powers[alone:far, :]], axis=0)))
    for i in range(tiles):
        fetch(i).wait()
        rows = slice(i * tile, (i + 1) * tile)
        for block in range(width // BLOCK):
            at = block
            if not sent:
                at = block + part * shared if block < alone else block - part * alone
            columns = pl.ds(pl.multiple_of(at * BLOCK, BLOCK), BLOCK)
            out_ref[rows, block * BLOCK : (block + 1) * BLOCK] = scaled(buffer[i, :, columns], scales[rows], block)


def scale(part, codes, exponents, alone, sent):
    count = codes.shape[0]
    width = (alone if sent else exponents.shape[0] - alone) * BLOCK
    tile = min(count, 64)
    return pl.pallas_call(
        functools.partial(scale_kernel, alone, tile, sent),
        out_shape=pltpu.VMEM((count, width), jnp.bfloat16),
        in_specs=[SMEM] + [pl.BlockSpec(memory_space=pl.ANY)] * 2,
        out_specs=VMEM,
        scratch_shapes=[
            pltpu.VMEM((count // tile, tile, width), jnp.bfloat16),
            pltpu.VMEM(exponents.shape, exponents.dtype),
            pltpu.SemaphoreType.DMA((count // tile,)),
            pltpu.SemaphoreType.DMA,
        ],
        compiler_params=pltpu.CompilerParams(vmem_limit_bytes=16 << 20),
        cost_estimate=pl.CostEstimate(flops=codes.size, bytes_accessed=4 * codes.size, transcendentals=0),
        name="scale_codes",
    )(part, in_hbm(codes), in_hbm(exponents))


def stash_kernel(row, *refs):
    *array_refs, out_ref = refs
    array_refs = array_refs[1:] if row else array_refs
    for ref in array_refs:
        out_ref[row : row + ref.shape[0]] = ref[...]
        row += ref.shape[0]


def stash(held, arrays, row, rows):
    operands = ([held] if row else []) + arrays
    return pl.pallas_call(
        functools.partial(stash_kernel, row),
        out_shape=pltpu.VMEM((rows, arrays[0].shape[1]), arrays[0].dtype),
        in_specs=[VMEM] * len(operands),
        out_specs=VMEM,
        input_output_aliases={0: 0} if row else {},
        compiler_params=pltpu.CompilerParams(vmem_limit_bytes=16 << 20),
        cost_estimate=pl.CostEstimate(flops=0, bytes_accessed=4 * sum(a.size for a in arrays), transcendentals=0),
        name="stash",
    )(*in_vmem(operands))


def dot(rows, grads):
    return lax.dot_general(rows, grads, NT, preferred_element_type=jnp.float32)


def stacked(refs, columns):
    rows = [ref[:, columns] for ref in refs]
    return jnp.concatenate(rows, axis=0) if len(rows) > 1 else rows[0]


def halves(half, total, rows, keep_ref, send_ref):
    for j in range(total.shape[0] // rows):
        low = total[j * rows : j * rows + rows // 2]
        high = total[j * rows + rows // 2 : (j + 1) * rows]
        keep_ref[j] = jnp.where(half == 0, low, high)
        send_ref[j] = jnp.where(half == 0, high, low)


def product(pieces, grads_ref):
    total = None
    first = 0
    for refs in pieces:
        width = min(refs[0].shape[1], grads_ref.shape[1] - first)
        if width <= 0:
            break
        term = dot(stacked(refs, slice(0, width)), grads_ref[:, first : first + width])
        total = term if total is None else total + term
        first += width
    return total


def score_kernel(counts, grads_given, rows, half_ref, *refs):
    refs = list(refs)
    pieces = [[refs.pop(0) for _ in range(arrays)] for arrays in counts]
    grad_refs, outs = refs[:grads_given], refs[grads_given:]
    for i, grads_ref in enumerate(grad_refs):
        halves(half_ref[0], product(pieces, grads_ref), rows, *outs[2 * i : 2 * i + 2])


def score(half, rows, pieces, grads):
    operands = [array for arrays in pieces for array in arrays]
    height = sum(array.shape[0] for array in pieces[0])
    shape = pltpu.VMEM((height // rows, rows // 2, grads[0].shape[0]), jnp.float32)
    return pl.pallas_call(
        functools.partial(score_kernel, [len(arrays) for arrays in pieces], len(grads), rows),
        out_shape=[shape] * (2 * len(grads)),
        in_specs=[SMEM] + [VMEM] * (len(operands) + len(grads)),
        out_specs=[VMEM] * (2 * len(grads)),
        compiler_params=pltpu.CompilerParams(vmem_limit_bytes=16 << 20),
        cost_estimate=pl.CostEstimate(
            flops=2 * height * sum(g.size for g in grads), bytes_accessed=2 * grads[0].size, transcendentals=0
        ),
        name="score",
    )(half, *in_vmem([*operands, *grads]))


def place_kernel(rows, order_ref, ids_ref, *refs):
    *share_refs, out_ref = refs
    count = ids_ref.shape[1]
    slots = lax.broadcasted_iota(jnp.int32, (count, count), 0)
    table = (slots == jnp.broadcast_to(ids_ref[...], (count, count))).astype(jnp.float32)
    j = 0
    for first in range(0, len(share_refs), 4):
        a, b, c, d = (ref[...] for ref in share_refs[first : first + 4])
        raw = (d + c) + (b + a)
        placed = lax.dot_general(
            raw, table, NT, precision=lax.Precision.HIGHEST, preferred_element_type=jnp.float32
        )
        for i in range(raw.shape[0] // rows):
            out_ref[order_ref[j]] = placed[i * rows : (i + 1) * rows]
            j += 1


def place(order, ids, shares, rows):
    return pl.pallas_call(
        functools.partial(place_kernel, rows),
        out_shape=jax.ShapeDtypeStruct((order.shape[0], rows, ids.shape[1]), jnp.float32),
        in_specs=[SMEM] + [VMEM] * (len(shares) + 1),
        out_specs=VMEM,
        compiler_params=pltpu.CompilerParams(vmem_limit_bytes=16 << 20),
        name="place_scores",
    )(order, ids, *in_vmem(shares))


def shards(fast, parts, total, queries, codes, exponents, example_ids):
    slow = total // fast
    here = lax.axis_index("ex")
    order = jnp.stack([
        lax.rem(here // fast + slow - s, slow) * fast + lax.rem(here % fast + fast - t, fast)
        for s in range(slow)
        for t in range(fast)
    ]).astype(jnp.int32)
    part, half, order = lax.optimization_barrier(
        (lax.axis_index("groups")[None], lax.axis_index("dim")[None], order)
    )
    rows = queries.shape[1]
    count = codes.shape[0]
    blocks = exponents.shape[1]
    alone = blocks * ALONE // 64
    held = blocks - alone
    cuts = [i * held // CHUNKS * BLOCK for i in range(CHUNKS + 1)]

    def step(value, length, stride):
        pairs = [
            (i, i + stride if (i // stride) % length < length - 1 else i - (length - 1) * stride)
            for i in range(total)
        ]
        return lax.ppermute(value, "ex", pairs)

    def along_fast(value):
        values = [value]
        for _ in range(fast - 1):
            values.append(step(values[-1], fast, 1))
        return values

    swap = [(i, parts - 1 - i) for i in range(parts)]
    by_block = exponents.T
    chunks = cut(part, queries, alone, cuts)
    theirs = lax.ppermute(scale(part, codes, by_block, alone, True), "groups", swap)
    ours = scale(part, codes, by_block, alone, False)

    def stack(arrays):
        return arrays if rows % 16 == 0 else [jnp.concatenate(arrays, axis=0)]

    early_rows = (slow - 1) * fast * rows
    early, late = [], []
    for c, chunk in enumerate(chunks):
        held = []
        for s in range(slow):
            values = along_fast(chunk)
            if s == slow - 1:
                late.append(stack(values))
                break
            tied = [step(chunk, slow, fast), *values] + held
            if c == CHUNKS - 1 and s == 0:
                *tied, ours = lax.optimization_barrier(tied + [ours])
            else:
                tied = lax.optimization_barrier(tied)
            chunk, values, held = tied[0], tied[1 : fast + 1], tied[fast + 1 :]
            held = [stash(held[0] if s else None, stack(values), s * fast * rows, early_rows)]
        early += held

    def shares_of(their_keep, their_send, keep, send):
        across = [(i, 3 - i) for i in range(4)]
        shares = [
            lax.ppermute(their_send, ("groups", "dim"), across),
            lax.ppermute(their_keep, "groups", swap),
            lax.ppermute(send, "dim", [(0, 1), (1, 0)]),
            keep,
        ]
        return [share.reshape(-1, count) for share in shares]

    early = [[held] for held in early]
    their_early = score(half, rows, early, [theirs])
    theirs, *their_early = lax.optimization_barrier((theirs, *their_early))
    shares = shares_of(*their_early, *score(half, rows, early, [ours]))
    shares += shares_of(*score(half, rows, late, [theirs, ours]))
    return place(order, example_ids, shares, rows // 2)


def solution(mesh):
    placed = (
        P("ex", None, "dim"),
        P(("groups", "ex"), "dim"),
        P(("groups", "ex"), "dim"),
        P(("groups", "ex"), None),
    )
    return jax.shard_map(
        functools.partial(shards, fast_length(mesh), mesh.shape["groups"], mesh.shape["ex"]),
        mesh=mesh,
        in_specs=placed,
        out_specs=P(None, "dim", ("groups", "ex")),
        check_vma=False,
    )
```

```python
import functools

import jax
import jax.numpy as jnp
from jax import lax
from jax.experimental import pallas as pl
from jax.experimental.pallas import tpu as pltpu
from jax.sharding import PartitionSpec as P

BLOCK = 128
ALONE = 30
CHUNKS = 2
VMEM = pl.BlockSpec(memory_space=pltpu.VMEM)
SMEM = pl.BlockSpec(memory_space=pltpu.SMEM)
NT = (((1,), (1,)), ((), ()))


def in_vmem(arrays):
    return [pltpu.with_memory_space_constraint(array, pltpu.VMEM) for array in arrays]


def in_hbm(array):
    return pltpu.with_memory_space_constraint(array, pltpu.HBM)


def fast_length(mesh):
    line = list(mesh.devices[0, :, 0])
    size = len(line)
    if size < 2 or not all(hasattr(device, "coords") for device in line):
        return 2 if size % 2 == 0 else size

    def moved(a, b):
        return tuple(i for i, (p, q) in enumerate(zip(a.coords, b.coords)) if p != q)

    along = moved(line[0], line[1])
    length = 2
    while length < size and moved(line[0], line[length]) == along:
        length += 1
    return length if size % length == 0 else size


def scaled(codes, scales, at):
    return codes * scales[:, at : at + 1].astype(jnp.bfloat16)


def scales_of(exponents):
    return (jnp.int32(1) << (exponents + 3)).astype(jnp.float32) * 0.125


def by_example(scales):
    pad = jnp.zeros((-scales.shape[0] % 8, scales.shape[1]), scales.dtype)
    return jnp.concatenate([scales, pad], axis=0).T


def cut_kernel(alone, blocks, cuts, part_ref, queries_ref, *refs):
    *chunk_refs, sems = refs
    first = pl.multiple_of(part_ref[0] * (blocks - alone) * BLOCK, BLOCK)
    wide = alone * BLOCK
    copies = []
    for out_ref, start, stop in zip(chunk_refs, cuts[:-1], cuts[1:]):
        if start < wide:
            width = min(stop, wide) - start
            copies.append((
                queries_ref.at[0, :, pl.ds(pl.multiple_of(first + start, BLOCK), width)],
                out_ref.at[:, pl.ds(0, width)],
            ))
        if stop > wide:
            begin = max(start, wide)
            copies.append((
                queries_ref.at[0, :, pl.ds(begin, stop - begin)],
                out_ref.at[:, pl.ds(begin - start, stop - begin)],
            ))
    copies = [pltpu.make_async_copy(a, b, sems.at[i]) for i, (a, b) in enumerate(copies)]
    for copy in copies:
        copy.start()
    for copy in copies:
        copy.wait()


def cut(part, queries, alone, cuts):
    rows = queries.shape[1]
    chunks = len(cuts) - 1
    return pl.pallas_call(
        functools.partial(cut_kernel, alone, queries.shape[2] // BLOCK, cuts),
        out_shape=[pltpu.VMEM((rows, b - a), jnp.bfloat16) for a, b in zip(cuts[:-1], cuts[1:])],
        in_specs=[SMEM, pl.BlockSpec(memory_space=pl.ANY)],
        out_specs=[VMEM] * chunks,
        scratch_shapes=[pltpu.SemaphoreType.DMA((2 * chunks,))],
        compiler_params=pltpu.CompilerParams(vmem_limit_bytes=16 << 20),
        cost_estimate=pl.CostEstimate(flops=0, bytes_accessed=2 * queries.size, transcendentals=0),
        name="cut_queries",
    )(part, in_hbm(queries))


def scale_kernel(alone, tile, sent, part_ref, codes_ref, exponents_ref, out_ref, buffer, powers, sems, powers_sem):
    part = part_ref[0]
    blocks = exponents_ref.shape[0]
    far = blocks - alone
    shared = far - alone
    tiles, _, width = buffer.shape
    begin = (1 - part) * far if sent else part * alone

    def fetch(i):
        start = pl.multiple_of(begin * BLOCK, BLOCK)
        return pltpu.make_async_copy(
            codes_ref.at[pl.ds(i * tile, tile), pl.ds(start, width)], buffer.at[i], sems.at[i]
        )

    powers_copy = pltpu.make_async_copy(exponents_ref, powers, powers_sem)
    powers_copy.start()
    for i in range(tiles):
        fetch(i).start()
    powers_copy.wait()
    near, away = powers[0:alone, :], powers[far:blocks, :]
    if sent:
        scales = by_example(scales_of(jnp.where(part == 0, away, near)))
    else:
        own = jnp.where(part == 0, near, away)
        scales = by_example(scales_of(jnp.concatenate([own, powers[alone:far, :]], axis=0)))
    for i in range(tiles):
        fetch(i).wait()
        rows = slice(i * tile, (i + 1) * tile)
        for block in range(width // BLOCK):
            at = block
            if not sent:
                at = block + part * shared if block < alone else block - part * alone
            columns = pl.ds(pl.multiple_of(at * BLOCK, BLOCK), BLOCK)
            out_ref[rows, block * BLOCK : (block + 1) * BLOCK] = scaled(buffer[i, :, columns], scales[rows], block)


def scale(part, codes, exponents, alone, sent):
    count = codes.shape[0]
    width = (alone if sent else exponents.shape[0] - alone) * BLOCK
    tile = min(count, 64)
    return pl.pallas_call(
        functools.partial(scale_kernel, alone, tile, sent),
        out_shape=pltpu.VMEM((count, width), jnp.bfloat16),
        in_specs=[SMEM] + [pl.BlockSpec(memory_space=pl.ANY)] * 2,
        out_specs=VMEM,
        scratch_shapes=[
            pltpu.VMEM((count // tile, tile, width), jnp.bfloat16),
            pltpu.VMEM(exponents.shape, exponents.dtype),
            pltpu.SemaphoreType.DMA((count // tile,)),
            pltpu.SemaphoreType.DMA,
        ],
        compiler_params=pltpu.CompilerParams(vmem_limit_bytes=16 << 20),
        cost_estimate=pl.CostEstimate(flops=codes.size, bytes_accessed=4 * codes.size, transcendentals=0),
        name="scale_codes",
    )(part, in_hbm(codes), in_hbm(exponents))


def stash_kernel(row, *refs):
    *array_refs, out_ref = refs
    array_refs = array_refs[1:] if row else array_refs
    for ref in array_refs:
        out_ref[row : row + ref.shape[0]] = ref[...]
        row += ref.shape[0]


def stash(held, arrays, row, rows):
    operands = ([held] if row else []) + arrays
    return pl.pallas_call(
        functools.partial(stash_kernel, row),
        out_shape=pltpu.VMEM((rows, arrays[0].shape[1]), arrays[0].dtype),
        in_specs=[VMEM] * len(operands),
        out_specs=VMEM,
        input_output_aliases={0: 0} if row else {},
        compiler_params=pltpu.CompilerParams(vmem_limit_bytes=16 << 20),
        cost_estimate=pl.CostEstimate(flops=0, bytes_accessed=4 * sum(a.size for a in arrays), transcendentals=0),
        name="stash",
    )(*in_vmem(operands))


def dot(rows, grads):
    return lax.dot_general(rows, grads, NT, preferred_element_type=jnp.float32)


def stacked(refs, columns):
    rows = [ref[:, columns] for ref in refs]
    return jnp.concatenate(rows, axis=0) if len(rows) > 1 else rows[0]


def halves(half, total, rows, keep_ref, send_ref):
    for j in range(total.shape[0] // rows):
        low = total[j * rows : j * rows + rows // 2]
        high = total[j * rows + rows // 2 : (j + 1) * rows]
        keep_ref[j] = jnp.where(half == 0, low, high)
        send_ref[j] = jnp.where(half == 0, high, low)


def product(pieces, grads_ref, first):
    total = None
    for refs in pieces:
        width = min(refs[0].shape[1], grads_ref.shape[1] - first)
        if width <= 0:
            break
        term = dot(stacked(refs, slice(0, width)), grads_ref[:, first : first + width])
        total = term if total is None else total + term
        first += width
    return total


def score_kernel(counts, grads_given, first, rows, begun, half_ref, *refs):
    refs = list(refs)
    pieces = [[refs.pop(0) for _ in range(arrays)] for arrays in counts]
    grad_refs, outs = refs[:grads_given], refs[grads_given:]
    base_refs, outs = (outs[:grads_given], outs[grads_given:]) if begun else (None, outs)
    for i, grads_ref in enumerate(grad_refs):
        total = product(pieces, grads_ref, first)
        if begun:
            total = total + base_refs[i][...]
        if rows:
            halves(half_ref[0], total, rows, *outs[2 * i : 2 * i + 2])
        else:
            outs[i][...] = total


def score(half, rows, pieces, grads, first=0, base=()):
    operands = [array for arrays in pieces for array in arrays] + list(grads) + list(base)
    height = sum(array.shape[0] for array in pieces[0])
    count = grads[0].shape[0]
    if rows:
        shapes = [pltpu.VMEM((height // rows, rows // 2, count), jnp.float32)] * (2 * len(grads))
    else:
        shapes = [pltpu.VMEM((height, count), jnp.float32)] * len(grads)
    return pl.pallas_call(
        functools.partial(score_kernel, [len(arrays) for arrays in pieces], len(grads), first, rows, bool(base)),
        out_shape=shapes,
        in_specs=[SMEM] + [VMEM] * len(operands),
        out_specs=[VMEM] * len(shapes),
        compiler_params=pltpu.CompilerParams(vmem_limit_bytes=16 << 20),
        cost_estimate=pl.CostEstimate(
            flops=2 * height * sum(g.size for g in grads), bytes_accessed=2 * grads[0].size, transcendentals=0
        ),
        name="score",
    )(half, *in_vmem(operands))


def place_kernel(rows, first, order_ref, ids_ref, *refs):
    *share_refs, out_ref, placed_ref, sems = refs
    share_refs = share_refs[1:] if first else share_refs
    count = ids_ref.shape[1]
    slots = lax.broadcasted_iota(jnp.int32, (count, count), 0)
    table = (slots == jnp.broadcast_to(ids_ref[...], (count, count))).astype(jnp.float32)
    copies = []
    for at in range(0, len(share_refs), 4):
        a, b, c, d = (ref[...] for ref in share_refs[at : at + 4])
        raw = (d + c) + (b + a)
        placed = lax.dot_general(
            raw, table, NT, precision=lax.Precision.HIGHEST, preferred_element_type=jnp.float32
        )
        for i in range(raw.shape[0] // rows):
            j = len(copies)
            placed_ref[j] = placed[i * rows : (i + 1) * rows]
            copies.append(
                pltpu.make_async_copy(placed_ref.at[j], out_ref.at[order_ref[first + j]], sems.at[j])
            )
            copies[-1].start()
    for copy in copies:
        copy.wait()


def place(order, ids, out, first, shares, rows):
    count = ids.shape[1]
    blocks = sum(share.shape[0] for share in shares[::4]) // rows
    anywhere = pl.BlockSpec(memory_space=pl.ANY)
    given = [in_hbm(out)] if first else []
    return pl.pallas_call(
        functools.partial(place_kernel, rows, first),
        out_shape=pltpu.HBM((order.shape[0], rows, count), jnp.float32),
        in_specs=[SMEM, VMEM] + [anywhere] * len(given) + [VMEM] * len(shares),
        out_specs=anywhere,
        input_output_aliases={2: 0} if given else {},
        scratch_shapes=[pltpu.VMEM((blocks, rows, count), jnp.float32), pltpu.SemaphoreType.DMA((blocks,))],
        compiler_params=pltpu.CompilerParams(vmem_limit_bytes=16 << 20),
        name="place_scores",
    )(order, ids, *given, *in_vmem(shares))


def shards(fast, parts, total, queries, codes, exponents, example_ids):
    slow = total // fast
    here = lax.axis_index("ex")
    order = jnp.stack([
        lax.rem(here // fast + slow - s, slow) * fast + lax.rem(here % fast + fast - t, fast)
        for s in range(slow)
        for t in range(fast)
    ]).astype(jnp.int32)
    part, half, order = lax.optimization_barrier(
        (lax.axis_index("groups")[None], lax.axis_index("dim")[None], order)
    )
    rows = queries.shape[1]
    count = codes.shape[0]
    blocks = exponents.shape[1]
    alone = blocks * ALONE // 64
    held = blocks - alone
    cuts = [i * held // CHUNKS * BLOCK for i in range(CHUNKS + 1)]

    def step(value, length, stride):
        pairs = [
            (i, i + stride if (i // stride) % length < length - 1 else i - (length - 1) * stride)
            for i in range(total)
        ]
        return lax.ppermute(value, "ex", pairs)

    def along_fast(value):
        values = [value]
        for _ in range(fast - 1):
            values.append(step(values[-1], fast, 1))
        return values

    swap = [(i, parts - 1 - i) for i in range(parts)]
    by_block = exponents.T
    chunks = cut(part, queries, alone, cuts)
    theirs = lax.ppermute(scale(part, codes, by_block, alone, True), "groups", swap)
    ours = scale(part, codes, by_block, alone, False)

    def stack(arrays):
        return arrays if rows % 16 == 0 else [jnp.concatenate(arrays, axis=0)]

    first_steps = max(slow - 2, 1)
    early_rows = first_steps * fast * rows
    early, middle, late = [], [], []
    for c, chunk in enumerate(chunks):
        held, between = [], []
        for s in range(slow - 1):
            tied = [step(chunk, slow, fast), *along_fast(chunk)] + held
            if c == CHUNKS - 1 and s == 0:
                *tied, ours = lax.optimization_barrier(tied + [ours])
            elif c == CHUNKS - 1 and s == slow - 2:
                their_early = list(score(half, rows, early + [held], [theirs]))
                *tied, keep, send = lax.optimization_barrier(tied + their_early)
                their_early = [keep, send]
            else:
                tied = lax.optimization_barrier(tied)
            chunk, values, held = tied[0], tied[1 : fast + 1], tied[fast + 1 :]
            if s < first_steps:
                held = [stash(held[0] if s else None, stack(values), s * fast * rows, early_rows)]
            else:
                between += values
        early.append(held)
        middle.append(stack(between + [chunk]))
        along = along_fast(chunk)[1:] if c < CHUNKS - 1 else [step(value, slow, fast) for value in values[1:]]
        late.append(stack(along))

    def shares_of(their_keep, their_send, keep, send):
        across = [(i, 3 - i) for i in range(4)]
        shares = [
            lax.ppermute(their_send, ("groups", "dim"), across),
            lax.ppermute(their_keep, "groups", swap),
            lax.ppermute(send, "dim", [(0, 1), (1, 0)]),
            keep,
        ]
        return [share.reshape(-1, count) for share in shares]

    shares = shares_of(*their_early, *score(half, rows, early, [ours]))
    out = place(order, example_ids, None, 0, shares, rows // 2)
    shares = shares_of(*score(half, rows, middle, [theirs, ours]))
    begun = score(half, 0, late[:-1], [theirs, ours])
    *begun, out = lax.optimization_barrier((*begun, out))
    shares += shares_of(*score(half, rows, late[-1:], [theirs, ours], cuts[-2], begun))
    return place(order, example_ids, out, first_steps * fast, shares, rows // 2)


def solution(mesh):
    placed = (
        P("ex", None, "dim"),
        P(("groups", "ex"), "dim"),
        P(("groups", "ex"), "dim"),
        P(("groups", "ex"), None),
    )
    return jax.shard_map(
        functools.partial(shards, fast_length(mesh), mesh.shape["groups"], mesh.shape["ex"]),
        mesh=mesh,
        in_specs=placed,
        out_specs=P(None, "dim", ("groups", "ex")),
        check_vma=False,
    )
```

```python
import functools

import jax
import jax.numpy as jnp
from jax import lax
from jax.experimental import pallas as pl
from jax.experimental.pallas import tpu as pltpu
from jax.sharding import PartitionSpec as P

BLOCK = 128
ALONE = 29
LATE_WEIGHT = 10
CHUNKS = 2
VMEM = pl.BlockSpec(memory_space=pltpu.VMEM)
SMEM = pl.BlockSpec(memory_space=pltpu.SMEM)
NT = (((1,), (1,)), ((), ()))


def in_vmem(arrays):
    return [pltpu.with_memory_space_constraint(array, pltpu.VMEM) for array in arrays]


def in_hbm(array):
    return pltpu.with_memory_space_constraint(array, pltpu.HBM)


def fast_length(mesh):
    line = list(mesh.devices[0, :, 0])
    size = len(line)
    if size < 2 or not all(hasattr(device, "coords") for device in line):
        return 2 if size % 2 == 0 else size

    def moved(a, b):
        return tuple(i for i, (p, q) in enumerate(zip(a.coords, b.coords)) if p != q)

    along = moved(line[0], line[1])
    length = 2
    while length < size and moved(line[0], line[length]) == along:
        length += 1
    return length if size % length == 0 else size


def scaled(codes, scales, at):
    return codes * scales[:, at : at + 1].astype(jnp.bfloat16)


def scales_of(exponents):
    return (jnp.int32(1) << (exponents + 3)).astype(jnp.float32) * 0.125


def by_example(scales):
    pad = jnp.zeros((-scales.shape[0] % 8, scales.shape[1]), scales.dtype)
    return jnp.concatenate([scales, pad], axis=0).T


def scale_tiles(codes_ref, begin, buffer, sems, scales, order, out_ref):
    tiles, tile, width = buffer.shape

    def fetch(i):
        start = pl.multiple_of(begin * BLOCK, BLOCK)
        return pltpu.make_async_copy(
            codes_ref.at[pl.ds(i * tile, tile), pl.ds(start, width)], buffer.at[i], sems.at[i]
        )

    for i in range(tiles):
        fetch(i).start()
    scales = scales()
    for i in range(tiles):
        fetch(i).wait()
        rows = slice(i * tile, (i + 1) * tile)
        for block, at in enumerate(order):
            columns = pl.ds(pl.multiple_of(at * BLOCK, BLOCK), BLOCK)
            out_ref[rows, block * BLOCK : (block + 1) * BLOCK] = scaled(buffer[i, :, columns], scales[rows], block)


def cut_kernel(alone, cuts, part_ref, queries_ref, codes_ref, exponents_ref, *refs):
    *chunk_refs, sent_ref, buffer, powers, code_sems, sems = refs
    part = part_ref[0]
    blocks = exponents_ref.shape[0]
    far = blocks - alone
    first = pl.multiple_of(part * far * BLOCK, BLOCK)
    wide = alone * BLOCK
    copies = [(exponents_ref, powers)]
    for out_ref, start, stop in zip(chunk_refs, cuts[:-1], cuts[1:]):
        if start < wide:
            width = min(stop, wide) - start
            copies.append((
                queries_ref.at[0, :, pl.ds(pl.multiple_of(first + start, BLOCK), width)],
                out_ref.at[:, pl.ds(0, width)],
            ))
        if stop > wide:
            begin = max(start, wide)
            copies.append((
                queries_ref.at[0, :, pl.ds(begin, stop - begin)],
                out_ref.at[:, pl.ds(begin - start, stop - begin)],
            ))
    copies = [pltpu.make_async_copy(a, b, sems.at[i]) for i, (a, b) in enumerate(copies)]
    copies[0].start()

    def scales():
        for copy in copies[1:]:
            copy.start()
        copies[0].wait()
        near, away = powers[0:alone, :], powers[far:blocks, :]
        return by_example(scales_of(jnp.where(part == 0, away, near)))

    scale_tiles(codes_ref, (1 - part) * far, buffer, code_sems, scales, range(alone), sent_ref)
    for copy in copies[1:]:
        copy.wait()


def cut(part, queries, codes, exponents, alone, cuts):
    rows = queries.shape[1]
    count = codes.shape[0]
    wide = alone * BLOCK
    tile = min(count, 64)
    chunks = len(cuts) - 1
    return pl.pallas_call(
        functools.partial(cut_kernel, alone, cuts),
        out_shape=[pltpu.VMEM((rows, b - a), jnp.bfloat16) for a, b in zip(cuts[:-1], cuts[1:])]
        + [pltpu.VMEM((count, wide), jnp.bfloat16)],
        in_specs=[SMEM] + [pl.BlockSpec(memory_space=pl.ANY)] * 3,
        out_specs=[VMEM] * (chunks + 1),
        scratch_shapes=[
            pltpu.VMEM((count // tile, tile, wide), jnp.bfloat16),
            pltpu.VMEM(exponents.shape, exponents.dtype),
            pltpu.SemaphoreType.DMA((count // tile,)),
            pltpu.SemaphoreType.DMA((2 * chunks + 1,)),
        ],
        compiler_params=pltpu.CompilerParams(vmem_limit_bytes=16 << 20),
        cost_estimate=pl.CostEstimate(flops=codes.size, bytes_accessed=2 * codes.size, transcendentals=0),
        name="cut_queries",
    )(part, in_hbm(queries), in_hbm(codes), in_hbm(exponents))


def scale_kernel(alone, part_ref, codes_ref, exponents_ref, out_ref, buffer, powers, code_sems, sem):
    part = part_ref[0]
    blocks = exponents_ref.shape[0]
    far = blocks - alone
    copy = pltpu.make_async_copy(exponents_ref, powers, sem)
    copy.start()

    def scales():
        copy.wait()
        own = jnp.where(part == 0, powers[0:alone, :], powers[far:blocks, :])
        return by_example(scales_of(jnp.concatenate([own, powers[alone:far, :]], axis=0)))

    order = [i + part * (far - alone) if i < alone else i - part * alone for i in range(far)]
    scale_tiles(codes_ref, part * alone, buffer, code_sems, scales, order, out_ref)


def scale(part, codes, exponents, alone):
    count = codes.shape[0]
    width = (exponents.shape[0] - alone) * BLOCK
    tile = min(count, 64)
    return pl.pallas_call(
        functools.partial(scale_kernel, alone),
        out_shape=pltpu.VMEM((count, width), jnp.bfloat16),
        in_specs=[SMEM] + [pl.BlockSpec(memory_space=pl.ANY)] * 2,
        out_specs=VMEM,
        scratch_shapes=[
            pltpu.VMEM((count // tile, tile, width), jnp.bfloat16),
            pltpu.VMEM(exponents.shape, exponents.dtype),
            pltpu.SemaphoreType.DMA((count // tile,)),
            pltpu.SemaphoreType.DMA,
        ],
        compiler_params=pltpu.CompilerParams(vmem_limit_bytes=16 << 20),
        cost_estimate=pl.CostEstimate(flops=codes.size, bytes_accessed=4 * codes.size, transcendentals=0),
        name="scale_codes",
    )(part, in_hbm(codes), in_hbm(exponents))


def stash_kernel(row, *refs):
    *array_refs, out_ref = refs
    array_refs = array_refs[1:] if row else array_refs
    for ref in array_refs:
        out_ref[row : row + ref.shape[0]] = ref[...]
        row += ref.shape[0]


def stash(held, arrays, row, rows):
    operands = ([held] if row else []) + arrays
    return pl.pallas_call(
        functools.partial(stash_kernel, row),
        out_shape=pltpu.VMEM((rows, arrays[0].shape[1]), arrays[0].dtype),
        in_specs=[VMEM] * len(operands),
        out_specs=VMEM,
        input_output_aliases={0: 0} if row else {},
        compiler_params=pltpu.CompilerParams(vmem_limit_bytes=16 << 20),
        cost_estimate=pl.CostEstimate(flops=0, bytes_accessed=4 * sum(a.size for a in arrays), transcendentals=0),
        name="stash",
    )(*in_vmem(operands))


def dot(rows, grads):
    return lax.dot_general(rows, grads, NT, preferred_element_type=jnp.float32)


def stacked(refs, columns):
    rows = [ref[:, columns] for ref in refs]
    return jnp.concatenate(rows, axis=0) if len(rows) > 1 else rows[0]


def halves(half, total, rows, keep_ref, send_ref):
    for j in range(total.shape[0] // rows):
        low = total[j * rows : j * rows + rows // 2]
        high = total[j * rows + rows // 2 : (j + 1) * rows]
        keep_ref[j] = jnp.where(half == 0, low, high)
        send_ref[j] = jnp.where(half == 0, high, low)


def product(pieces, grads_ref, first):
    total = None
    for refs in pieces:
        width = min(refs[0].shape[1], grads_ref.shape[1] - first)
        if width <= 0:
            break
        term = dot(stacked(refs, slice(0, width)), grads_ref[:, first : first + width])
        total = term if total is None else total + term
        first += width
    return total


def score_kernel(counts, grads_given, first, rows, begun, half_ref, *refs):
    refs = list(refs)
    pieces = [[refs.pop(0) for _ in range(arrays)] for arrays in counts]
    grad_refs, outs = refs[:grads_given], refs[grads_given:]
    base_refs, outs = (outs[:grads_given], outs[grads_given:]) if begun else (None, outs)
    for i, grads_ref in enumerate(grad_refs):
        total = product(pieces, grads_ref, first)
        if begun:
            total = total + base_refs[i][...]
        if rows:
            halves(half_ref[0], total, rows, *outs[2 * i : 2 * i + 2])
        else:
            outs[i][...] = total


def score(half, rows, pieces, grads, first=0, base=(), weight=1):
    operands = [array for arrays in pieces for array in arrays] + list(grads) + list(base)
    height = sum(array.shape[0] for array in pieces[0])
    count = grads[0].shape[0]
    if rows:
        shapes = [pltpu.VMEM((height // rows, rows // 2, count), jnp.float32)] * (2 * len(grads))
    else:
        shapes = [pltpu.VMEM((height, count), jnp.float32)] * len(grads)
    return pl.pallas_call(
        functools.partial(score_kernel, [len(arrays) for arrays in pieces], len(grads), first, rows, bool(base)),
        out_shape=shapes,
        in_specs=[SMEM] + [VMEM] * len(operands),
        out_specs=[VMEM] * len(shapes),
        compiler_params=pltpu.CompilerParams(vmem_limit_bytes=16 << 20),
        cost_estimate=pl.CostEstimate(
            flops=2 * height * sum(g.size for g in grads) * weight, bytes_accessed=2 * grads[0].size, transcendentals=0
        ),
        name="score",
    )(half, *in_vmem(operands))


def add_kernel(a_ref, b_ref, out_ref):
    out_ref[...] = a_ref[...] + b_ref[...]


def add(a, b):
    return pl.pallas_call(
        add_kernel,
        out_shape=pltpu.VMEM(a.shape, a.dtype),
        in_specs=[VMEM, VMEM],
        out_specs=VMEM,
        compiler_params=pltpu.CompilerParams(vmem_limit_bytes=16 << 20),
        name="add",
    )(*in_vmem([a, b]))


def place_kernel(first, order_ref, ids_ref, *refs):
    *share_refs, out_ref, placed_ref, sems = refs
    share_refs = share_refs[1:] if first else share_refs
    blocks, rows, count = placed_ref.shape
    slots = lax.broadcasted_iota(jnp.int32, (count, count), 0)
    table = (slots == jnp.broadcast_to(ids_ref[...], (count, count))).astype(jnp.float32).astype(jnp.bfloat16)
    raw = functools.reduce(jnp.add, [ref[...] for ref in share_refs])
    high = raw.astype(jnp.bfloat16)
    rest = raw - high.astype(jnp.float32)
    middle = rest.astype(jnp.bfloat16)
    low = (rest - middle.astype(jnp.float32)).astype(jnp.bfloat16)
    placed = (dot(high, table) + dot(middle, table)) + dot(low, table)
    copies = []
    for j in range(blocks):
        placed_ref[j] = placed[j * rows : (j + 1) * rows]
        copies.append(pltpu.make_async_copy(placed_ref.at[j], out_ref.at[order_ref[first + j]], sems.at[j]))
        copies[-1].start()
    for copy in copies:
        copy.wait()


def place(order, ids, out, first, shares, rows):
    count = ids.shape[1]
    shares = [share.reshape(-1, count) for share in shares]
    blocks = shares[0].shape[0] // rows
    anywhere = pl.BlockSpec(memory_space=pl.ANY)
    given = [in_hbm(out)] if first else []
    return pl.pallas_call(
        functools.partial(place_kernel, first),
        out_shape=pltpu.HBM((order.shape[0], rows, count), jnp.float32),
        in_specs=[SMEM, VMEM] + [anywhere] * len(given) + [VMEM] * len(shares),
        out_specs=anywhere,
        input_output_aliases={2: 0} if given else {},
        scratch_shapes=[pltpu.VMEM((blocks, rows, count), jnp.float32), pltpu.SemaphoreType.DMA((blocks,))],
        compiler_params=pltpu.CompilerParams(vmem_limit_bytes=16 << 20),
        name="place_scores",
    )(order, ids, *given, *in_vmem(shares))


def shards(fast, parts, total, queries, codes, exponents, example_ids):
    slow = total // fast
    here = lax.axis_index("ex")
    order = jnp.stack([
        lax.rem(here // fast + slow - s, slow) * fast + lax.rem(here % fast + fast - t, fast)
        for s in range(slow)
        for t in range(fast)
    ]).astype(jnp.int32)
    part, half, order = lax.optimization_barrier(
        (lax.axis_index("groups")[None], lax.axis_index("dim")[None], order)
    )
    rows = queries.shape[1]
    count = codes.shape[0]
    blocks = exponents.shape[1]
    alone = blocks * ALONE // 64
    held = blocks - alone
    cuts = [i * held // CHUNKS * BLOCK for i in range(CHUNKS + 1)]

    def step(value, length, stride):
        pairs = [
            (i, i + stride if (i // stride) % length < length - 1 else i - (length - 1) * stride)
            for i in range(total)
        ]
        return lax.ppermute(value, "ex", pairs)

    def along_fast(value):
        values = [value]
        for _ in range(fast - 1):
            values.append(step(values[-1], fast, 1))
        return values

    swap = [(i, parts - 1 - i) for i in range(parts)]
    by_block = exponents.T
    *chunks, sent = cut(part, queries, codes, by_block, alone, cuts)
    theirs = lax.ppermute(sent, "groups", swap)
    ours = scale(part, codes, by_block, alone)

    def stack(arrays):
        return arrays if rows % 16 == 0 else [jnp.concatenate(arrays, axis=0)]

    kept_rows = (slow - 2) * fast * rows
    early, late = [], []
    for c, chunk in enumerate(chunks):
        held = []
        for s in range(slow - 1):
            tied = [step(chunk, slow, fast), *along_fast(chunk)] + held
            if c == CHUNKS - 1 and s == 0:
                *tied, ours = lax.optimization_barrier(tied + [ours])
            else:
                tied = lax.optimization_barrier(tied)
            chunk, values, held = tied[0], tied[1 : fast + 1], tied[fast + 1 :]
            if s < slow - 2:
                held = [stash(held[0] if s else None, stack(values), s * fast * rows, kept_rows)]
        early.append(held + stack(values + [chunk]))
        along = along_fast(chunk)[1:] if c < CHUNKS - 1 else [step(value, slow, fast) for value in values[1:]]
        late.append(stack(along))

    def over_dim(value):
        return lax.ppermute(value, "dim", [(0, 1), (1, 0)])

    keep, send = score(half, rows, early, [theirs])
    added, theirs = lax.optimization_barrier((add(keep, over_dim(send)), theirs))
    given = lax.ppermute(added, "groups", swap)
    keep, send = score(half, rows, early, [ours])
    shares = [given, keep, over_dim(send)]

    begun = score(half, 0, late[:-1], [theirs, ours])
    last = score(half, rows, late[-1:], [theirs, ours], cuts[-2], begun, LATE_WEIGHT)
    *last, shares[1] = lax.optimization_barrier((*last, shares[1]))
    out = place(order, example_ids, None, 0, shares, rows // 2)
    their_keep, their_send, keep, send = last
    across = [(i, 3 - i) for i in range(4)]
    shares = [
        lax.ppermute(their_send, ("groups", "dim"), across),
        lax.ppermute(their_keep, "groups", swap),
        over_dim(send),
        keep,
    ]
    return place(order, example_ids, out, total - fast + 1, shares, rows // 2)


def solution(mesh):
    placed = (
        P("ex", None, "dim"),
        P(("groups", "ex"), "dim"),
        P(("groups", "ex"), "dim"),
        P(("groups", "ex"), None),
    )
    return jax.shard_map(
        functools.partial(shards, fast_length(mesh), mesh.shape["groups"], mesh.shape["ex"]),
        mesh=mesh,
        in_specs=placed,
        out_specs=P(None, "dim", ("groups", "ex")),
        check_vma=False,
    )
```

```python
import functools

import jax
import jax.numpy as jnp
from jax import lax
from jax.experimental import pallas as pl
from jax.experimental.pallas import tpu as pltpu
from jax.sharding import PartitionSpec as P

BLOCK = 128
ALONE = 29
LATE_WEIGHT = 10
LEAD = 0
CHUNKS = 2
VMEM = pl.BlockSpec(memory_space=pltpu.VMEM)
SMEM = pl.BlockSpec(memory_space=pltpu.SMEM)
NT = (((1,), (1,)), ((), ()))


def in_vmem(arrays):
    return [pltpu.with_memory_space_constraint(array, pltpu.VMEM) for array in arrays]


def in_hbm(array):
    return pltpu.with_memory_space_constraint(array, pltpu.HBM)


def fast_length(mesh):
    line = list(mesh.devices[0, :, 0])
    size = len(line)
    if size < 2 or not all(hasattr(device, "coords") for device in line):
        return 2 if size % 2 == 0 else size

    def moved(a, b):
        return tuple(i for i, (p, q) in enumerate(zip(a.coords, b.coords)) if p != q)

    along = moved(line[0], line[1])
    length = 2
    while length < size and moved(line[0], line[length]) == along:
        length += 1
    return length if size % length == 0 else size


def scaled(codes, scales, at):
    return codes * scales[:, at : at + 1].astype(jnp.bfloat16)


def scales_of(exponents):
    return (jnp.int32(1) << (exponents + 3)).astype(jnp.float32) * 0.125


def by_example(scales):
    pad = jnp.zeros((-scales.shape[0] % 8, scales.shape[1]), scales.dtype)
    return jnp.concatenate([scales, pad], axis=0).T


def scale_tiles(codes_ref, begin, buffer, sems, scales, order, out_ref):
    tiles, tile, width = buffer.shape

    def fetch(i):
        start = pl.multiple_of(begin * BLOCK, BLOCK)
        return pltpu.make_async_copy(
            codes_ref.at[pl.ds(i * tile, tile), pl.ds(start, width)], buffer.at[i], sems.at[i]
        )

    for i in range(tiles):
        fetch(i).start()
    scales = scales()
    for i in range(tiles):
        fetch(i).wait()
        rows = slice(i * tile, (i + 1) * tile)
        for block, at in enumerate(order):
            columns = pl.ds(pl.multiple_of(at * BLOCK, BLOCK), BLOCK)
            out_ref[rows, block * BLOCK : (block + 1) * BLOCK] = scaled(buffer[i, :, columns], scales[rows], block)


def cut_kernel(alone, cuts, part_ref, queries_ref, codes_ref, exponents_ref, *refs):
    *chunk_refs, sent_ref, buffer, powers, code_sems, sems = refs
    part = part_ref[0]
    blocks = exponents_ref.shape[0]
    far = blocks - alone
    first = pl.multiple_of(part * far * BLOCK, BLOCK)
    wide = alone * BLOCK
    copies = [(exponents_ref, powers)]
    for out_ref, start, stop in zip(chunk_refs, cuts[:-1], cuts[1:]):
        if start < wide:
            width = min(stop, wide) - start
            copies.append((
                queries_ref.at[0, :, pl.ds(pl.multiple_of(first + start, BLOCK), width)],
                out_ref.at[:, pl.ds(0, width)],
            ))
        if stop > wide:
            begin = max(start, wide)
            copies.append((
                queries_ref.at[0, :, pl.ds(begin, stop - begin)],
                out_ref.at[:, pl.ds(begin - start, stop - begin)],
            ))
    copies = [pltpu.make_async_copy(a, b, sems.at[i]) for i, (a, b) in enumerate(copies)]
    copies[0].start()

    def scales():
        for copy in copies[1:]:
            copy.start()
        copies[0].wait()
        near, away = powers[0:alone, :], powers[far:blocks, :]
        return by_example(scales_of(jnp.where(part == 0, away, near)))

    scale_tiles(codes_ref, (1 - part) * far, buffer, code_sems, scales, range(alone), sent_ref)
    for copy in copies[1:]:
        copy.wait()


def cut(part, queries, codes, exponents, alone, cuts):
    rows = queries.shape[1]
    count = codes.shape[0]
    wide = alone * BLOCK
    tile = min(count, 64)
    chunks = len(cuts) - 1
    return pl.pallas_call(
        functools.partial(cut_kernel, alone, cuts),
        out_shape=[pltpu.VMEM((rows, b - a), jnp.bfloat16) for a, b in zip(cuts[:-1], cuts[1:])]
        + [pltpu.VMEM((count, wide), jnp.bfloat16)],
        in_specs=[SMEM] + [pl.BlockSpec(memory_space=pl.ANY)] * 3,
        out_specs=[VMEM] * (chunks + 1),
        scratch_shapes=[
            pltpu.VMEM((count // tile, tile, wide), jnp.bfloat16),
            pltpu.VMEM(exponents.shape, exponents.dtype),
            pltpu.SemaphoreType.DMA((count // tile,)),
            pltpu.SemaphoreType.DMA((2 * chunks + 1,)),
        ],
        compiler_params=pltpu.CompilerParams(vmem_limit_bytes=16 << 20),
        cost_estimate=pl.CostEstimate(flops=codes.size, bytes_accessed=2 * codes.size, transcendentals=0),
        name="cut_queries",
    )(part, in_hbm(queries), in_hbm(codes), in_hbm(exponents))


def scale_kernel(alone, part_ref, codes_ref, exponents_ref, out_ref, buffer, powers, code_sems, sem):
    part = part_ref[0]
    blocks = exponents_ref.shape[0]
    far = blocks - alone
    copy = pltpu.make_async_copy(exponents_ref, powers, sem)
    copy.start()

    def scales():
        copy.wait()
        own = jnp.where(part == 0, powers[0:alone, :], powers[far:blocks, :])
        return by_example(scales_of(jnp.concatenate([own, powers[alone:far, :]], axis=0)))

    order = [i + part * (far - alone) if i < alone else i - part * alone for i in range(far)]
    scale_tiles(codes_ref, part * alone, buffer, code_sems, scales, order, out_ref)


def scale(part, codes, exponents, alone):
    count = codes.shape[0]
    width = (exponents.shape[0] - alone) * BLOCK
    tile = min(count, 64)
    return pl.pallas_call(
        functools.partial(scale_kernel, alone),
        out_shape=pltpu.VMEM((count, width), jnp.bfloat16),
        in_specs=[SMEM] + [pl.BlockSpec(memory_space=pl.ANY)] * 2,
        out_specs=VMEM,
        scratch_shapes=[
            pltpu.VMEM((count // tile, tile, width), jnp.bfloat16),
            pltpu.VMEM(exponents.shape, exponents.dtype),
            pltpu.SemaphoreType.DMA((count // tile,)),
            pltpu.SemaphoreType.DMA,
        ],
        compiler_params=pltpu.CompilerParams(vmem_limit_bytes=16 << 20),
        cost_estimate=pl.CostEstimate(flops=codes.size, bytes_accessed=4 * codes.size, transcendentals=0),
        name="scale_codes",
    )(part, in_hbm(codes), in_hbm(exponents))


def stash_kernel(row, *refs):
    *array_refs, out_ref = refs
    array_refs = array_refs[1:] if row else array_refs
    for ref in array_refs:
        out_ref[row : row + ref.shape[0]] = ref[...]
        row += ref.shape[0]


def stash(held, arrays, row, rows):
    operands = ([held] if row else []) + arrays
    return pl.pallas_call(
        functools.partial(stash_kernel, row),
        out_shape=pltpu.VMEM((rows, arrays[0].shape[1]), arrays[0].dtype),
        in_specs=[VMEM] * len(operands),
        out_specs=VMEM,
        input_output_aliases={0: 0} if row else {},
        compiler_params=pltpu.CompilerParams(vmem_limit_bytes=16 << 20),
        cost_estimate=pl.CostEstimate(flops=0, bytes_accessed=4 * sum(a.size for a in arrays), transcendentals=0),
        name="stash",
    )(*in_vmem(operands))


def dot(rows, grads):
    return lax.dot_general(rows, grads, NT, preferred_element_type=jnp.float32)


def stacked(refs, columns):
    rows = [ref[:, columns] for ref in refs]
    return jnp.concatenate(rows, axis=0) if len(rows) > 1 else rows[0]


def halves(half, total, rows, keep_ref, send_ref):
    for j in range(total.shape[0] // rows):
        low = total[j * rows : j * rows + rows // 2]
        high = total[j * rows + rows // 2 : (j + 1) * rows]
        keep_ref[j] = jnp.where(half == 0, low, high)
        send_ref[j] = jnp.where(half == 0, high, low)


def product(pieces, grads_ref, first):
    total = None
    for refs in pieces:
        width = min(refs[0].shape[1], grads_ref.shape[1] - first)
        if width <= 0:
            break
        term = dot(stacked(refs, slice(0, width)), grads_ref[:, first : first + width])
        total = term if total is None else total + term
        first += width
    return total


def score_kernel(counts, grads_given, first, rows, begun, half_ref, *refs):
    refs = list(refs)
    pieces = [[refs.pop(0) for _ in range(arrays)] for arrays in counts]
    grad_refs, outs = refs[:grads_given], refs[grads_given:]
    base_refs, outs = (outs[:grads_given], outs[grads_given:]) if begun else (None, outs)
    for i, grads_ref in enumerate(grad_refs):
        total = product(pieces, grads_ref, first)
        if begun:
            total = total + base_refs[i][...]
        if rows:
            halves(half_ref[0], total, rows, *outs[2 * i : 2 * i + 2])
        else:
            outs[i][...] = total


def score(half, rows, pieces, grads, first=0, base=(), weight=1):
    operands = [array for arrays in pieces for array in arrays] + list(grads) + list(base)
    height = sum(array.shape[0] for array in pieces[0])
    count = grads[0].shape[0]
    if rows:
        shapes = [pltpu.VMEM((height // rows, rows // 2, count), jnp.float32)] * (2 * len(grads))
    else:
        shapes = [pltpu.VMEM((height, count), jnp.float32)] * len(grads)
    return pl.pallas_call(
        functools.partial(score_kernel, [len(arrays) for arrays in pieces], len(grads), first, rows, bool(base)),
        out_shape=shapes,
        in_specs=[SMEM] + [VMEM] * len(operands),
        out_specs=[VMEM] * len(shapes),
        compiler_params=pltpu.CompilerParams(vmem_limit_bytes=16 << 20),
        cost_estimate=pl.CostEstimate(
            flops=2 * height * sum(g.size for g in grads) * weight, bytes_accessed=2 * grads[0].size, transcendentals=0
        ),
        name="score",
    )(half, *in_vmem(operands))


def add_kernel(a_ref, b_ref, out_ref):
    out_ref[...] = a_ref[...] + b_ref[...]


def add(a, b):
    return pl.pallas_call(
        add_kernel,
        out_shape=pltpu.VMEM(a.shape, a.dtype),
        in_specs=[VMEM, VMEM],
        out_specs=VMEM,
        compiler_params=pltpu.CompilerParams(vmem_limit_bytes=16 << 20),
        name="add",
    )(*in_vmem([a, b]))


def place_kernel(groups, order_ref, ids_ref, *refs):
    *share_refs, out_ref = refs
    share_refs = list(share_refs)
    _, rows, count = out_ref.shape
    slots = lax.broadcasted_iota(jnp.int32, (count, count), 0)
    table = (slots == jnp.broadcast_to(ids_ref[...], (count, count))).astype(jnp.float32).astype(jnp.bfloat16)
    raw = [functools.reduce(jnp.add, [share_refs.pop(0)[...] for _ in range(shares)]) for shares in groups]
    raw = jnp.concatenate(raw, axis=0)
    high = raw.astype(jnp.bfloat16)
    rest = raw - high.astype(jnp.float32)
    middle = rest.astype(jnp.bfloat16)
    low = (rest - middle.astype(jnp.float32)).astype(jnp.bfloat16)
    placed = (dot(high, table) + dot(middle, table)) + dot(low, table)
    for j in range(raw.shape[0] // rows):
        out_ref[order_ref[j]] = placed[j * rows : (j + 1) * rows]


def place(order, ids, groups, rows):
    count = ids.shape[1]
    shares = [share.reshape(-1, count) for group in groups for share in group]
    return pl.pallas_call(
        functools.partial(place_kernel, [len(group) for group in groups]),
        out_shape=jax.ShapeDtypeStruct((order.shape[0], rows, count), jnp.float32),
        in_specs=[SMEM, VMEM] + [VMEM] * len(shares),
        out_specs=VMEM,
        compiler_params=pltpu.CompilerParams(vmem_limit_bytes=16 << 20),
        name="place_scores",
    )(order, ids, *in_vmem(shares))


def shards(fast, parts, total, queries, codes, exponents, example_ids):
    slow = total // fast
    here = lax.axis_index("ex")
    order = jnp.stack([
        lax.rem(here // fast + slow - s, slow) * fast + lax.rem(here % fast + fast - t, fast)
        for s in range(slow)
        for t in range(fast)
    ]).astype(jnp.int32)
    part, half, order = lax.optimization_barrier(
        (lax.axis_index("groups")[None], lax.axis_index("dim")[None], order)
    )
    rows = queries.shape[1]
    count = codes.shape[0]
    blocks = exponents.shape[1]
    alone = blocks * ALONE // 64
    held = blocks - alone
    cuts = [-(-i * held // CHUNKS) * BLOCK for i in range(CHUNKS + 1)]

    def step(value, length, stride):
        pairs = [
            (i, i + stride if (i // stride) % length < length - 1 else i - (length - 1) * stride)
            for i in range(total)
        ]
        return lax.ppermute(value, "ex", pairs)

    def along_fast(value):
        values = [value]
        for _ in range(fast - 1):
            values.append(step(values[-1], fast, 1))
        return values

    swap = [(i, parts - 1 - i) for i in range(parts)]
    by_block = exponents.T
    *chunks, sent = cut(part, queries, codes, by_block, alone, cuts)
    theirs = lax.ppermute(sent, "groups", swap)
    ours = scale(part, codes, by_block, alone)

    def stack(arrays):
        return arrays if rows % 16 == 0 else [jnp.concatenate(arrays, axis=0)]

    kept_rows = (slow - 2) * fast * rows
    early, late = [None] * CHUNKS, [None] * CHUNKS
    held = [[] for _ in range(CHUNKS)]
    for s in range(slow - 1):
        for c in (LEAD, 1 - LEAD):
            tied = [step(chunks[c], slow, fast), *along_fast(chunks[c])] + held[c]
            if s == 0 and c == LEAD:
                *tied, ours = lax.optimization_barrier(tied + [ours])
            elif s == slow - 2 and c != LEAD:
                begun_own = score(half, 0, early[LEAD:LEAD + 1], [ours], cuts[LEAD])
                *tied, begun_own = lax.optimization_barrier(tied + list(begun_own))
            else:
                tied = lax.optimization_barrier(tied)
            chunks[c], values, kept = tied[0], tied[1 : fast + 1], tied[fast + 1 :]
            if s < slow - 2:
                held[c] = [stash(kept[0] if s else None, stack(values), s * fast * rows, kept_rows)]
                continue
            early[c] = kept + stack(values + [chunks[c]])
            late[c] = stack(
                along_fast(chunks[c])[1:] if c == LEAD else [step(value, slow, fast) for value in values[1:]]
            )

    def over_dim(value):
        return lax.ppermute(value, "dim", [(0, 1), (1, 0)])

    lead, trail = slice(LEAD, LEAD + 1), slice(1 - LEAD, 2 - LEAD)
    keep, send = score(half, rows, early, [theirs])
    added, theirs = lax.optimization_barrier((add(keep, over_dim(send)), theirs))
    given = lax.ppermute(added, "groups", swap)
    keep, send = score(half, rows, early[trail], [ours], cuts[1 - LEAD], [begun_own])
    shares = [given, keep, over_dim(send)]

    begun = score(half, 0, late[lead], [theirs, ours], cuts[LEAD])
    their_keep, their_send, own_keep, own_send = score(
        half, rows, late[trail], [theirs, ours], cuts[1 - LEAD], begun, LATE_WEIGHT
    )
    across = [(i, 3 - i) for i in range(4)]
    last = [
        lax.ppermute(their_send, ("groups", "dim"), across),
        lax.ppermute(their_keep, "groups", swap),
        over_dim(own_send),
        own_keep,
    ]
    return place(order, example_ids, [shares, last], rows // 2)


def solution(mesh):
    placed = (
        P("ex", None, "dim"),
        P(("groups", "ex"), "dim"),
        P(("groups", "ex"), "dim"),
        P(("groups", "ex"), None),
    )
    return jax.shard_map(
        functools.partial(shards, fast_length(mesh), mesh.shape["groups"], mesh.shape["ex"]),
        mesh=mesh,
        in_specs=placed,
        out_specs=P(None, "dim", ("groups", "ex")),
        check_vma=False,
    )
```

```python
import functools

import jax
import jax.numpy as jnp
from jax import lax
from jax.experimental import pallas as pl
from jax.experimental.pallas import tpu as pltpu
from jax.sharding import PartitionSpec as P

BLOCK = 128
ALONE = 28
LATE_WEIGHT = 10
BEGUN_WEIGHT = 10
LEAD = 0
CHUNKS = 2
VMEM = pl.BlockSpec(memory_space=pltpu.VMEM)
SMEM = pl.BlockSpec(memory_space=pltpu.SMEM)
NT = (((1,), (1,)), ((), ()))


def in_vmem(arrays):
    return [pltpu.with_memory_space_constraint(array, pltpu.VMEM) for array in arrays]


def in_hbm(array):
    return pltpu.with_memory_space_constraint(array, pltpu.HBM)


def fast_length(mesh):
    line = list(mesh.devices[0, :, 0])
    size = len(line)
    if size < 2 or not all(hasattr(device, "coords") for device in line):
        return 2 if size % 2 == 0 else size

    def moved(a, b):
        return tuple(i for i, (p, q) in enumerate(zip(a.coords, b.coords)) if p != q)

    along = moved(line[0], line[1])
    length = 2
    while length < size and moved(line[0], line[length]) == along:
        length += 1
    return length if size % length == 0 else size


def scaled(codes, scales, at):
    return codes * scales[:, at : at + 1].astype(jnp.bfloat16)


def scales_of(exponents):
    return (jnp.int32(1) << (exponents + 3)).astype(jnp.float32) * 0.125


def by_example(scales):
    pad = jnp.zeros((-scales.shape[0] % 8, scales.shape[1]), scales.dtype)
    return jnp.concatenate([scales, pad], axis=0).T


def scale_tiles(codes_ref, begin, buffer, sems, scales, order, out_ref):
    tiles, tile, width = buffer.shape

    def fetch(i):
        start = pl.multiple_of(begin * BLOCK, BLOCK)
        return pltpu.make_async_copy(
            codes_ref.at[pl.ds(i * tile, tile), pl.ds(start, width)], buffer.at[i], sems.at[i]
        )

    for i in range(tiles):
        fetch(i).start()
    scales = scales()
    for i in range(tiles):
        fetch(i).wait()
        rows = slice(i * tile, (i + 1) * tile)
        for block, at in enumerate(order):
            columns = pl.ds(pl.multiple_of(at * BLOCK, BLOCK), BLOCK)
            out_ref[rows, block * BLOCK : (block + 1) * BLOCK] = scaled(buffer[i, :, columns], scales[rows], block)


def cut_kernel(alone, cuts, part_ref, queries_ref, codes_ref, exponents_ref, *refs):
    *chunk_refs, sent_ref, buffer, powers, code_sems, sems = refs
    part = part_ref[0]
    blocks = exponents_ref.shape[0]
    far = blocks - alone
    first = pl.multiple_of(part * far * BLOCK, BLOCK)
    wide = alone * BLOCK
    copies = [(exponents_ref, powers)]
    for out_ref, start, stop in zip(chunk_refs, cuts[:-1], cuts[1:]):
        if start < wide:
            width = min(stop, wide) - start
            copies.append((
                queries_ref.at[0, :, pl.ds(pl.multiple_of(first + start, BLOCK), width)],
                out_ref.at[:, pl.ds(0, width)],
            ))
        if stop > wide:
            begin = max(start, wide)
            copies.append((
                queries_ref.at[0, :, pl.ds(begin, stop - begin)],
                out_ref.at[:, pl.ds(begin - start, stop - begin)],
            ))
    copies = [pltpu.make_async_copy(a, b, sems.at[i]) for i, (a, b) in enumerate(copies)]
    copies[0].start()

    def scales():
        for copy in copies[1:]:
            copy.start()
        copies[0].wait()
        near, away = powers[0:alone, :], powers[far:blocks, :]
        return by_example(scales_of(jnp.where(part == 0, away, near)))

    scale_tiles(codes_ref, (1 - part) * far, buffer, code_sems, scales, range(alone), sent_ref)
    for copy in copies[1:]:
        copy.wait()


def cut(part, queries, codes, exponents, alone, cuts):
    rows = queries.shape[1]
    count = codes.shape[0]
    wide = alone * BLOCK
    tile = min(count, 64)
    chunks = len(cuts) - 1
    return pl.pallas_call(
        functools.partial(cut_kernel, alone, cuts),
        out_shape=[pltpu.VMEM((rows, b - a), jnp.bfloat16) for a, b in zip(cuts[:-1], cuts[1:])]
        + [pltpu.VMEM((count, wide), jnp.bfloat16)],
        in_specs=[SMEM] + [pl.BlockSpec(memory_space=pl.ANY)] * 3,
        out_specs=[VMEM] * (chunks + 1),
        scratch_shapes=[
            pltpu.VMEM((count // tile, tile, wide), jnp.bfloat16),
            pltpu.VMEM(exponents.shape, exponents.dtype),
            pltpu.SemaphoreType.DMA((count // tile,)),
            pltpu.SemaphoreType.DMA((2 * chunks + 1,)),
        ],
        compiler_params=pltpu.CompilerParams(vmem_limit_bytes=16 << 20),
        cost_estimate=pl.CostEstimate(flops=codes.size, bytes_accessed=2 * codes.size, transcendentals=0),
        name="cut_queries",
    )(part, in_hbm(queries), in_hbm(codes), in_hbm(exponents))


def scale_kernel(alone, part_ref, codes_ref, exponents_ref, out_ref, buffer, powers, code_sems, sem):
    part = part_ref[0]
    blocks = exponents_ref.shape[0]
    far = blocks - alone
    copy = pltpu.make_async_copy(exponents_ref, powers, sem)
    copy.start()

    def scales():
        copy.wait()
        own = jnp.where(part == 0, powers[0:alone, :], powers[far:blocks, :])
        return by_example(scales_of(jnp.concatenate([own, powers[alone:far, :]], axis=0)))

    order = [i + part * (far - alone) if i < alone else i - part * alone for i in range(far)]
    scale_tiles(codes_ref, part * alone, buffer, code_sems, scales, order, out_ref)


def scale(part, codes, exponents, alone):
    count = codes.shape[0]
    width = (exponents.shape[0] - alone) * BLOCK
    tile = min(count, 64)
    return pl.pallas_call(
        functools.partial(scale_kernel, alone),
        out_shape=pltpu.VMEM((count, width), jnp.bfloat16),
        in_specs=[SMEM] + [pl.BlockSpec(memory_space=pl.ANY)] * 2,
        out_specs=VMEM,
        scratch_shapes=[
            pltpu.VMEM((count // tile, tile, width), jnp.bfloat16),
            pltpu.VMEM(exponents.shape, exponents.dtype),
            pltpu.SemaphoreType.DMA((count // tile,)),
            pltpu.SemaphoreType.DMA,
        ],
        compiler_params=pltpu.CompilerParams(vmem_limit_bytes=16 << 20),
        cost_estimate=pl.CostEstimate(flops=codes.size, bytes_accessed=4 * codes.size, transcendentals=0),
        name="scale_codes",
    )(part, in_hbm(codes), in_hbm(exponents))


def stash_kernel(row, *refs):
    *array_refs, out_ref = refs
    array_refs = array_refs[1:] if row else array_refs
    for ref in array_refs:
        out_ref[row : row + ref.shape[0]] = ref[...]
        row += ref.shape[0]


def stash(held, arrays, row, rows):
    operands = ([held] if row else []) + arrays
    return pl.pallas_call(
        functools.partial(stash_kernel, row),
        out_shape=pltpu.VMEM((rows, arrays[0].shape[1]), arrays[0].dtype),
        in_specs=[VMEM] * len(operands),
        out_specs=VMEM,
        input_output_aliases={0: 0} if row else {},
        compiler_params=pltpu.CompilerParams(vmem_limit_bytes=16 << 20),
        cost_estimate=pl.CostEstimate(flops=0, bytes_accessed=4 * sum(a.size for a in arrays), transcendentals=0),
        name="stash",
    )(*in_vmem(operands))


def dot(rows, grads):
    return lax.dot_general(rows, grads, NT, preferred_element_type=jnp.float32)


def stacked(refs, columns):
    rows = [ref[:, columns] for ref in refs]
    return jnp.concatenate(rows, axis=0) if len(rows) > 1 else rows[0]


def halves(half, total, rows, keep_ref, send_ref):
    for j in range(total.shape[0] // rows):
        low = total[j * rows : j * rows + rows // 2]
        high = total[j * rows + rows // 2 : (j + 1) * rows]
        keep_ref[j] = jnp.where(half == 0, low, high)
        send_ref[j] = jnp.where(half == 0, high, low)


def product(pieces, grads_ref, first):
    total = None
    for refs in pieces:
        width = min(refs[0].shape[1], grads_ref.shape[1] - first)
        if width <= 0:
            break
        term = dot(stacked(refs, slice(0, width)), grads_ref[:, first : first + width])
        total = term if total is None else total + term
        first += width
    return total


def score_kernel(counts, grads_given, first, rows, begun, half_ref, *refs):
    refs = list(refs)
    pieces = [[refs.pop(0) for _ in range(arrays)] for arrays in counts]
    grad_refs, outs = refs[:grads_given], refs[grads_given:]
    base_refs, outs = (outs[:grads_given], outs[grads_given:]) if begun else (None, outs)
    for i, grads_ref in enumerate(grad_refs):
        total = product(pieces, grads_ref, first)
        if begun:
            total = total + base_refs[i][...]
        if rows:
            halves(half_ref[0], total, rows, *outs[2 * i : 2 * i + 2])
        else:
            outs[i][...] = total


def score(half, rows, pieces, grads, first=0, base=(), weight=1):
    operands = [array for arrays in pieces for array in arrays] + list(grads) + list(base)
    height = sum(array.shape[0] for array in pieces[0])
    count = grads[0].shape[0]
    if rows:
        shapes = [pltpu.VMEM((height // rows, rows // 2, count), jnp.float32)] * (2 * len(grads))
    else:
        shapes = [pltpu.VMEM((height, count), jnp.float32)] * len(grads)
    return pl.pallas_call(
        functools.partial(score_kernel, [len(arrays) for arrays in pieces], len(grads), first, rows, bool(base)),
        out_shape=shapes,
        in_specs=[SMEM] + [VMEM] * len(operands),
        out_specs=[VMEM] * len(shapes),
        compiler_params=pltpu.CompilerParams(vmem_limit_bytes=16 << 20),
        cost_estimate=pl.CostEstimate(
            flops=2 * height * sum(g.size for g in grads) * weight, bytes_accessed=2 * grads[0].size, transcendentals=0
        ),
        name="score",
    )(half, *in_vmem(operands))


def add_kernel(a_ref, b_ref, out_ref):
    out_ref[...] = a_ref[...] + b_ref[...]


def add(a, b):
    return pl.pallas_call(
        add_kernel,
        out_shape=pltpu.VMEM(a.shape, a.dtype),
        in_specs=[VMEM, VMEM],
        out_specs=VMEM,
        compiler_params=pltpu.CompilerParams(vmem_limit_bytes=16 << 20),
        name="add",
    )(*in_vmem([a, b]))


def place_kernel(groups, order_ref, ids_ref, *refs):
    *share_refs, out_ref = refs
    share_refs = list(share_refs)

    def stacked_share(arrays):
        given = [share_refs.pop(0)[...] for _ in range(arrays)]
        return jnp.concatenate(given, axis=0) if arrays > 1 else given[0]

    _, rows, count = out_ref.shape
    slots = lax.broadcasted_iota(jnp.int32, (count, count), 0)
    table = (slots == jnp.broadcast_to(ids_ref[...], (count, count))).astype(jnp.float32).astype(jnp.bfloat16)
    raw = [functools.reduce(jnp.add, [stacked_share(arrays) for arrays in shares]) for shares in groups]
    raw = jnp.concatenate(raw, axis=0)
    high = raw.astype(jnp.bfloat16)
    rest = raw - high.astype(jnp.float32)
    middle = rest.astype(jnp.bfloat16)
    low = (rest - middle.astype(jnp.float32)).astype(jnp.bfloat16)
    placed = (dot(high, table) + dot(middle, table)) + dot(low, table)
    for j in range(raw.shape[0] // rows):
        out_ref[order_ref[j]] = placed[j * rows : (j + 1) * rows]


def place(order, ids, groups, rows):
    count = ids.shape[1]
    shares = [array.reshape(-1, count) for group in groups for share in group for array in share]
    return pl.pallas_call(
        functools.partial(place_kernel, [[len(share) for share in group] for group in groups]),
        out_shape=jax.ShapeDtypeStruct((order.shape[0], rows, count), jnp.float32),
        in_specs=[SMEM, VMEM] + [VMEM] * len(shares),
        out_specs=VMEM,
        compiler_params=pltpu.CompilerParams(vmem_limit_bytes=16 << 20),
        name="place_scores",
    )(order, ids, *in_vmem(shares))


def shards(fast, parts, total, queries, codes, exponents, example_ids):
    slow = total // fast
    here = lax.axis_index("ex")
    order = jnp.stack([
        lax.rem(here // fast + slow - s, slow) * fast + lax.rem(here % fast + fast - t, fast)
        for s in range(slow)
        for t in range(fast)
    ]).astype(jnp.int32)
    part, half, order = lax.optimization_barrier(
        (lax.axis_index("groups")[None], lax.axis_index("dim")[None], order)
    )
    rows = queries.shape[1]
    count = codes.shape[0]
    blocks = exponents.shape[1]
    alone = blocks * ALONE // 64
    held = blocks - alone
    cuts = [-(-i * held // CHUNKS) * BLOCK for i in range(CHUNKS + 1)]

    def step(value, length, stride):
        pairs = [
            (i, i + stride if (i // stride) % length < length - 1 else i - (length - 1) * stride)
            for i in range(total)
        ]
        return lax.ppermute(value, "ex", pairs)

    def along_fast(value):
        values = [value]
        for _ in range(fast - 1):
            values.append(step(values[-1], fast, 1))
        return values

    swap = [(i, parts - 1 - i) for i in range(parts)]
    by_block = exponents.T
    *chunks, sent = cut(part, queries, codes, by_block, alone, cuts)
    theirs = lax.ppermute(sent, "groups", swap)
    ours = scale(part, codes, by_block, alone)

    def stack(arrays):
        return arrays if rows % 16 == 0 else [jnp.concatenate(arrays, axis=0)]

    kept_rows = (slow - 2) * fast * rows
    first, second, last = ([None] * CHUNKS for _ in range(3))
    held = [[] for _ in range(CHUNKS)]
    lead, trail = slice(LEAD, LEAD + 1), slice(1 - LEAD, 2 - LEAD)
    for s in range(slow - 1):
        for c in (LEAD, 1 - LEAD):
            if s == slow - 2:
                first[c] = held[c] + [chunks[c]]
            tied = [step(chunks[c], slow, fast), *along_fast(chunks[c])] + held[c]
            if s == 0 and c == LEAD:
                *tied, ours = lax.optimization_barrier(tied + [ours])
            elif s == slow - 2 and c != LEAD:
                begun_own = score(half, 0, [first[LEAD] + second[LEAD]], [ours], cuts[LEAD])
                ready, *begun_own = lax.optimization_barrier((chunks[LEAD], *begun_own))
                last[LEAD] = stack(along_fast(ready)[1:])
                their_first = score(half, rows, first, [theirs])
                *tied, keep, send = lax.optimization_barrier(tied + list(their_first))
                their_first = keep, send
            else:
                tied = lax.optimization_barrier(tied)
            chunks[c], values, kept = tied[0], tied[1 : fast + 1], tied[fast + 1 :]
            if s < slow - 2:
                held[c] = [stash(kept[0] if s else None, stack(values), s * fast * rows, kept_rows)]
                continue
            second[c] = stack(values[1:] + [chunks[c]])
            if c != LEAD:
                last[c] = stack([step(value, slow, fast) for value in values[1:]])

    def over_dim(value):
        return lax.ppermute(value, "dim", [(0, 1), (1, 0)])

    keep, send = their_first
    added, theirs = lax.optimization_barrier((add(keep, over_dim(send)), theirs))
    given = [lax.ppermute(added, "groups", swap)]
    keep, send = score(half, rows, second, [theirs])
    added, *begun_own = lax.optimization_barrier((add(keep, over_dim(send)), *begun_own))
    given.append(lax.ppermute(added, "groups", swap))
    early = [a + b for a, b in zip(first, second)]
    keep, send = score(half, rows, early[trail], [ours], cuts[1 - LEAD], begun_own)
    shares = [given, [keep], [over_dim(send)]]

    begun = score(half, 0, last[lead], [theirs, ours], cuts[LEAD], (), BEGUN_WEIGHT)
    their_keep, their_send, own_keep, own_send = score(
        half, rows, last[trail], [theirs, ours], cuts[1 - LEAD], begun, LATE_WEIGHT
    )
    across = [(i, 3 - i) for i in range(4)]
    late = [
        [lax.ppermute(their_send, ("groups", "dim"), across)],
        [lax.ppermute(their_keep, "groups", swap)],
        [over_dim(own_send)],
        [own_keep],
    ]
    return place(order, example_ids, [shares, late], rows // 2)


def solution(mesh):
    placed = (
        P("ex", None, "dim"),
        P(("groups", "ex"), "dim"),
        P(("groups", "ex"), "dim"),
        P(("groups", "ex"), None),
    )
    return jax.shard_map(
        functools.partial(shards, fast_length(mesh), mesh.shape["groups"], mesh.shape["ex"]),
        mesh=mesh,
        in_specs=placed,
        out_specs=P(None, "dim", ("groups", "ex")),
        check_vma=False,
    )
```

```python
import functools

import jax
import jax.numpy as jnp
from jax import lax
from jax.experimental import pallas as pl
from jax.experimental.pallas import tpu as pltpu
from jax.sharding import PartitionSpec as P

BLOCK = 128
ALONE = 29
LATE_WEIGHT = 30
LEAD = 0
LEAD_PART = 19
CHUNKS = 2
VMEM = pl.BlockSpec(memory_space=pltpu.VMEM)
SMEM = pl.BlockSpec(memory_space=pltpu.SMEM)
NT = (((1,), (1,)), ((), ()))


def in_vmem(arrays):
    return [pltpu.with_memory_space_constraint(array, pltpu.VMEM) for array in arrays]


def in_hbm(array):
    return pltpu.with_memory_space_constraint(array, pltpu.HBM)


def fast_length(mesh):
    line = list(mesh.devices[0, :, 0])
    size = len(line)
    if size < 2 or not all(hasattr(device, "coords") for device in line):
        return 2 if size % 2 == 0 else size

    def moved(a, b):
        return tuple(i for i, (p, q) in enumerate(zip(a.coords, b.coords)) if p != q)

    along = moved(line[0], line[1])
    length = 2
    while length < size and moved(line[0], line[length]) == along:
        length += 1
    return length if size % length == 0 else size


def scaled(codes, scales, at):
    return codes * scales[:, at : at + 1].astype(jnp.bfloat16)


def scales_of(exponents):
    return (jnp.int32(1) << (exponents + 3)).astype(jnp.float32) * 0.125


def by_example(scales):
    pad = jnp.zeros((-scales.shape[0] % 8, scales.shape[1]), scales.dtype)
    return jnp.concatenate([scales, pad], axis=0).T


def scale_tiles(codes_ref, begin, buffer, sems, scales, order, out_ref):
    tiles, tile, width = buffer.shape

    def fetch(i):
        start = pl.multiple_of(begin * BLOCK, BLOCK)
        return pltpu.make_async_copy(
            codes_ref.at[pl.ds(i * tile, tile), pl.ds(start, width)], buffer.at[i], sems.at[i]
        )

    for i in range(tiles):
        fetch(i).start()
    scales = scales()
    for i in range(tiles):
        fetch(i).wait()
        rows = slice(i * tile, (i + 1) * tile)
        for block, at in enumerate(order):
            columns = pl.ds(pl.multiple_of(at * BLOCK, BLOCK), BLOCK)
            out_ref[rows, block * BLOCK : (block + 1) * BLOCK] = scaled(buffer[i, :, columns], scales[rows], block)


def cut_kernel(alone, cuts, part_ref, queries_ref, codes_ref, exponents_ref, *refs):
    *chunk_refs, sent_ref, buffer, powers, code_sems, sems = refs
    part = part_ref[0]
    blocks = exponents_ref.shape[0]
    far = blocks - alone
    first = pl.multiple_of(part * far * BLOCK, BLOCK)
    wide = alone * BLOCK
    copies = [(exponents_ref, powers)]
    for out_ref, start, stop in zip(chunk_refs, cuts[:-1], cuts[1:]):
        if start < wide:
            width = min(stop, wide) - start
            copies.append((
                queries_ref.at[0, :, pl.ds(pl.multiple_of(first + start, BLOCK), width)],
                out_ref.at[:, pl.ds(0, width)],
            ))
        if stop > wide:
            begin = max(start, wide)
            copies.append((
                queries_ref.at[0, :, pl.ds(begin, stop - begin)],
                out_ref.at[:, pl.ds(begin - start, stop - begin)],
            ))
    copies = [pltpu.make_async_copy(a, b, sems.at[i]) for i, (a, b) in enumerate(copies)]
    copies[0].start()

    def scales():
        for copy in copies[1:]:
            copy.start()
        copies[0].wait()
        near, away = powers[0:alone, :], powers[far:blocks, :]
        return by_example(scales_of(jnp.where(part == 0, away, near)))

    scale_tiles(codes_ref, (1 - part) * far, buffer, code_sems, scales, range(alone), sent_ref)
    for copy in copies[1:]:
        copy.wait()


def cut(part, queries, codes, exponents, alone, cuts):
    rows = queries.shape[1]
    count = codes.shape[0]
    wide = alone * BLOCK
    tile = min(count, 64)
    chunks = len(cuts) - 1
    return pl.pallas_call(
        functools.partial(cut_kernel, alone, cuts),
        out_shape=[pltpu.VMEM((rows, b - a), jnp.bfloat16) for a, b in zip(cuts[:-1], cuts[1:])]
        + [pltpu.VMEM((count, wide), jnp.bfloat16)],
        in_specs=[SMEM] + [pl.BlockSpec(memory_space=pl.ANY)] * 3,
        out_specs=[VMEM] * (chunks + 1),
        scratch_shapes=[
            pltpu.VMEM((count // tile, tile, wide), jnp.bfloat16),
            pltpu.VMEM(exponents.shape, exponents.dtype),
            pltpu.SemaphoreType.DMA((count // tile,)),
            pltpu.SemaphoreType.DMA((2 * chunks + 1,)),
        ],
        compiler_params=pltpu.CompilerParams(vmem_limit_bytes=16 << 20),
        cost_estimate=pl.CostEstimate(flops=codes.size, bytes_accessed=2 * codes.size, transcendentals=0),
        name="cut_queries",
    )(part, in_hbm(queries), in_hbm(codes), in_hbm(exponents))


def scale_kernel(alone, part_ref, codes_ref, exponents_ref, out_ref, buffer, powers, code_sems, sem):
    part = part_ref[0]
    blocks = exponents_ref.shape[0]
    far = blocks - alone
    copy = pltpu.make_async_copy(exponents_ref, powers, sem)
    copy.start()

    def scales():
        copy.wait()
        own = jnp.where(part == 0, powers[0:alone, :], powers[far:blocks, :])
        return by_example(scales_of(jnp.concatenate([own, powers[alone:far, :]], axis=0)))

    order = [i + part * (far - alone) if i < alone else i - part * alone for i in range(far)]
    scale_tiles(codes_ref, part * alone, buffer, code_sems, scales, order, out_ref)


def scale(part, codes, exponents, alone):
    count = codes.shape[0]
    width = (exponents.shape[0] - alone) * BLOCK
    tile = min(count, 64)
    return pl.pallas_call(
        functools.partial(scale_kernel, alone),
        out_shape=pltpu.VMEM((count, width), jnp.bfloat16),
        in_specs=[SMEM] + [pl.BlockSpec(memory_space=pl.ANY)] * 2,
        out_specs=VMEM,
        scratch_shapes=[
            pltpu.VMEM((count // tile, tile, width), jnp.bfloat16),
            pltpu.VMEM(exponents.shape, exponents.dtype),
            pltpu.SemaphoreType.DMA((count // tile,)),
            pltpu.SemaphoreType.DMA,
        ],
        compiler_params=pltpu.CompilerParams(vmem_limit_bytes=16 << 20),
        cost_estimate=pl.CostEstimate(flops=codes.size, bytes_accessed=4 * codes.size, transcendentals=0),
        name="scale_codes",
    )(part, in_hbm(codes), in_hbm(exponents))


def stash_kernel(row, *refs):
    *array_refs, out_ref = refs
    array_refs = array_refs[1:] if row else array_refs
    for ref in array_refs:
        out_ref[row : row + ref.shape[0]] = ref[...]
        row += ref.shape[0]


def stash(held, arrays, row, rows):
    operands = ([held] if row else []) + arrays
    return pl.pallas_call(
        functools.partial(stash_kernel, row),
        out_shape=pltpu.VMEM((rows, arrays[0].shape[1]), arrays[0].dtype),
        in_specs=[VMEM] * len(operands),
        out_specs=VMEM,
        input_output_aliases={0: 0} if row else {},
        compiler_params=pltpu.CompilerParams(vmem_limit_bytes=16 << 20),
        cost_estimate=pl.CostEstimate(flops=0, bytes_accessed=4 * sum(a.size for a in arrays), transcendentals=0),
        name="stash",
    )(*in_vmem(operands))


def dot(rows, grads):
    return lax.dot_general(rows, grads, NT, preferred_element_type=jnp.float32)


def stacked(refs, columns):
    rows = [ref[:, columns] for ref in refs]
    return jnp.concatenate(rows, axis=0) if len(rows) > 1 else rows[0]


def halves(half, total, rows, keep_ref, send_ref):
    for j in range(total.shape[0] // rows):
        low = total[j * rows : j * rows + rows // 2]
        high = total[j * rows + rows // 2 : (j + 1) * rows]
        keep_ref[j] = jnp.where(half == 0, low, high)
        send_ref[j] = jnp.where(half == 0, high, low)


def product(pieces, grads_ref, first):
    total = None
    for refs in pieces:
        width = min(refs[0].shape[1], grads_ref.shape[1] - first)
        if width <= 0:
            break
        term = dot(stacked(refs, slice(0, width)), grads_ref[:, first : first + width])
        total = term if total is None else total + term
        first += width
    return total


def score_kernel(counts, grads_given, first, rows, begun, half_ref, *refs):
    refs = list(refs)
    pieces = [[refs.pop(0) for _ in range(arrays)] for arrays in counts]
    grad_refs, outs = refs[:grads_given], refs[grads_given:]
    base_refs, outs = (outs[:grads_given], outs[grads_given:]) if begun else (None, outs)
    for i, grads_ref in enumerate(grad_refs):
        total = product(pieces, grads_ref, first)
        if begun:
            total = total + base_refs[i][...]
        if rows:
            halves(half_ref[0], total, rows, *outs[2 * i : 2 * i + 2])
        else:
            outs[i][...] = total


def score(half, rows, pieces, grads, first=0, base=(), weight=1):
    operands = [array for arrays in pieces for array in arrays] + list(grads) + list(base)
    height = sum(array.shape[0] for array in pieces[0])
    count = grads[0].shape[0]
    if rows:
        shapes = [pltpu.VMEM((height // rows, rows // 2, count), jnp.float32)] * (2 * len(grads))
    else:
        shapes = [pltpu.VMEM((height, count), jnp.float32)] * len(grads)
    return pl.pallas_call(
        functools.partial(score_kernel, [len(arrays) for arrays in pieces], len(grads), first, rows, bool(base)),
        out_shape=shapes,
        in_specs=[SMEM] + [VMEM] * len(operands),
        out_specs=[VMEM] * len(shapes),
        compiler_params=pltpu.CompilerParams(vmem_limit_bytes=16 << 20),
        cost_estimate=pl.CostEstimate(
            flops=2 * height * sum(g.size for g in grads) * weight, bytes_accessed=2 * grads[0].size, transcendentals=0
        ),
        name="score",
    )(half, *in_vmem(operands))


def add_kernel(a_ref, b_ref, out_ref):
    out_ref[...] = a_ref[...] + b_ref[...]


def add(a, b):
    return pl.pallas_call(
        add_kernel,
        out_shape=pltpu.VMEM(a.shape, a.dtype),
        in_specs=[VMEM, VMEM],
        out_specs=VMEM,
        compiler_params=pltpu.CompilerParams(vmem_limit_bytes=16 << 20),
        name="add",
    )(*in_vmem([a, b]))


def place_kernel(groups, order_ref, ids_ref, *refs):
    *share_refs, out_ref = refs
    share_refs = list(share_refs)
    _, rows, count = out_ref.shape
    slots = lax.broadcasted_iota(jnp.int32, (count, count), 0)
    table = (slots == jnp.broadcast_to(ids_ref[...], (count, count))).astype(jnp.float32).astype(jnp.bfloat16)
    raw = [functools.reduce(jnp.add, [share_refs.pop(0)[...] for _ in range(shares)]) for shares in groups]
    raw = jnp.concatenate(raw, axis=0)
    high = raw.astype(jnp.bfloat16)
    rest = raw - high.astype(jnp.float32)
    middle = rest.astype(jnp.bfloat16)
    low = (rest - middle.astype(jnp.float32)).astype(jnp.bfloat16)
    placed = (dot(high, table) + dot(middle, table)) + dot(low, table)
    for j in range(raw.shape[0] // rows):
        out_ref[order_ref[j]] = placed[j * rows : (j + 1) * rows]


def place(order, ids, groups, rows):
    count = ids.shape[1]
    shares = [share.reshape(-1, count) for group in groups for share in group]
    return pl.pallas_call(
        functools.partial(place_kernel, [len(group) for group in groups]),
        out_shape=jax.ShapeDtypeStruct((order.shape[0], rows, count), jnp.float32),
        in_specs=[SMEM, VMEM] + [VMEM] * len(shares),
        out_specs=VMEM,
        compiler_params=pltpu.CompilerParams(vmem_limit_bytes=16 << 20),
        name="place_scores",
    )(order, ids, *in_vmem(shares))


def shards(fast, parts, total, queries, codes, exponents, example_ids):
    slow = total // fast
    here = lax.axis_index("ex")
    order = jnp.stack([
        lax.rem(here // fast + slow - s, slow) * fast + lax.rem(here % fast + fast - t, fast)
        for s in range(slow)
        for t in range(fast)
    ]).astype(jnp.int32)
    part, half, order = lax.optimization_barrier(
        (lax.axis_index("groups")[None], lax.axis_index("dim")[None], order)
    )
    rows = queries.shape[1]
    count = codes.shape[0]
    blocks = exponents.shape[1]
    alone = blocks * ALONE // 64
    held = blocks - alone
    cuts = [0, held * LEAD_PART // 35 * BLOCK, held * BLOCK]

    def step(value, length, stride):
        pairs = [
            (i, i + stride if (i // stride) % length < length - 1 else i - (length - 1) * stride)
            for i in range(total)
        ]
        return lax.ppermute(value, "ex", pairs)

    def along_fast(value):
        values = [value]
        for _ in range(fast - 1):
            values.append(step(values[-1], fast, 1))
        return values

    swap = [(i, parts - 1 - i) for i in range(parts)]
    by_block = exponents.T
    *chunks, sent = cut(part, queries, codes, by_block, alone, cuts)
    theirs = lax.ppermute(sent, "groups", swap)
    ours = scale(part, codes, by_block, alone)

    def stack(arrays):
        return arrays if rows % 16 == 0 else [jnp.concatenate(arrays, axis=0)]

    kept_rows = (slow - 2) * fast * rows
    early, late = [None] * CHUNKS, [None] * CHUNKS
    held = [[] for _ in range(CHUNKS)]
    for s in range(slow - 1):
        for c in (LEAD, 1 - LEAD):
            tied = [step(chunks[c], slow, fast), *along_fast(chunks[c])] + held[c]
            if s == 0 and c == LEAD:
                *tied, ours = lax.optimization_barrier(tied + [ours])
            elif s == slow - 2 and c != LEAD:
                begun_own = score(half, 0, early[LEAD : LEAD + 1], [ours], cuts[LEAD])
                ready, *begun_own = lax.optimization_barrier((chunks[LEAD], *begun_own))
                late[LEAD] = stack(along_fast(ready)[1:])
                *tied, begun_own = lax.optimization_barrier(tied + begun_own)
            else:
                tied = lax.optimization_barrier(tied)
            chunks[c], values, kept = tied[0], tied[1 : fast + 1], tied[fast + 1 :]
            if s < slow - 2:
                held[c] = [stash(kept[0] if s else None, stack(values), s * fast * rows, kept_rows)]
                continue
            early[c] = kept + stack(values + [chunks[c]])
            if c != LEAD:
                late[c] = stack([step(value, slow, fast) for value in values[1:]])

    def over_dim(value):
        return lax.ppermute(value, "dim", [(0, 1), (1, 0)])

    lead, trail = slice(LEAD, LEAD + 1), slice(1 - LEAD, 2 - LEAD)
    keep, send = score(half, rows, early, [theirs])
    added, theirs = lax.optimization_barrier((add(keep, over_dim(send)), theirs))
    given = lax.ppermute(added, "groups", swap)
    keep, send = score(half, rows, early[trail], [ours], cuts[1 - LEAD], [begun_own])
    shares = [given, keep, over_dim(send)]

    begun = score(half, 0, late[lead], [theirs, ours], cuts[LEAD])
    their_keep, their_send, own_keep, own_send = score(
        half, rows, late[trail], [theirs, ours], cuts[1 - LEAD], begun, LATE_WEIGHT
    )
    across = [(i, 3 - i) for i in range(4)]
    last = [
        lax.ppermute(their_send, ("groups", "dim"), across),
        lax.ppermute(their_keep, "groups", swap),
        over_dim(own_send),
        own_keep,
    ]
    return place(order, example_ids, [shares, last], rows // 2)


def solution(mesh):
    placed = (
        P("ex", None, "dim"),
        P(("groups", "ex"), "dim"),
        P(("groups", "ex"), "dim"),
        P(("groups", "ex"), None),
    )
    return jax.shard_map(
        functools.partial(shards, fast_length(mesh), mesh.shape["groups"], mesh.shape["ex"]),
        mesh=mesh,
        in_specs=placed,
        out_specs=P(None, "dim", ("groups", "ex")),
        check_vma=False,
    )
```

```python
import functools

import jax
import jax.numpy as jnp
from jax import lax
from jax.experimental import pallas as pl
from jax.experimental.pallas import tpu as pltpu
from jax.sharding import PartitionSpec as P

BLOCK = 128
ALONE = 29
LATE_WEIGHT = 30
LEAD = 0
LEAD_PART = 19
CHUNKS = 2
VMEM = pl.BlockSpec(memory_space=pltpu.VMEM)
SMEM = pl.BlockSpec(memory_space=pltpu.SMEM)
NT = (((1,), (1,)), ((), ()))


def in_vmem(arrays):
    return [pltpu.with_memory_space_constraint(array, pltpu.VMEM) for array in arrays]


def in_hbm(array):
    return pltpu.with_memory_space_constraint(array, pltpu.HBM)


def fast_length(mesh):
    line = list(mesh.devices[0, :, 0])
    size = len(line)
    if size < 2 or not all(hasattr(device, "coords") for device in line):
        return 2 if size % 2 == 0 else size

    def moved(a, b):
        return tuple(i for i, (p, q) in enumerate(zip(a.coords, b.coords)) if p != q)

    along = moved(line[0], line[1])
    length = 2
    while length < size and moved(line[0], line[length]) == along:
        length += 1
    return length if size % length == 0 else size


def scaled(codes, scales, at):
    return codes * scales[:, at : at + 1].astype(jnp.bfloat16)


def scales_of(exponents):
    return (jnp.int32(1) << (exponents + 3)).astype(jnp.float32) * 0.125


def by_example(scales):
    pad = jnp.zeros((-scales.shape[0] % 8, scales.shape[1]), scales.dtype)
    return jnp.concatenate([scales, pad], axis=0).T


def scale_tiles(codes_ref, begin, buffer, sems, scales, order, out_ref):
    tiles, tile, width = buffer.shape

    def fetch(i):
        start = pl.multiple_of(begin * BLOCK, BLOCK)
        return pltpu.make_async_copy(
            codes_ref.at[pl.ds(i * tile, tile), pl.ds(start, width)], buffer.at[i], sems.at[i]
        )

    for i in range(tiles):
        fetch(i).start()
    scales = scales()
    for i in range(tiles):
        fetch(i).wait()
        rows = slice(i * tile, (i + 1) * tile)
        for block, at in enumerate(order):
            columns = pl.ds(pl.multiple_of(at * BLOCK, BLOCK), BLOCK)
            out_ref[rows, block * BLOCK : (block + 1) * BLOCK] = scaled(buffer[i, :, columns], scales[rows], block)


def cut_kernel(alone, cuts, part_ref, queries_ref, codes_ref, exponents_ref, *refs):
    *chunk_refs, sent_ref, buffer, powers, code_sems, sems = refs
    part = part_ref[0]
    blocks = exponents_ref.shape[0]
    far = blocks - alone
    first = pl.multiple_of(part * far * BLOCK, BLOCK)
    wide = alone * BLOCK
    copies = [(exponents_ref, powers)]
    for out_ref, start, stop in zip(chunk_refs, cuts[:-1], cuts[1:]):
        if start < wide:
            width = min(stop, wide) - start
            copies.append((
                queries_ref.at[0, :, pl.ds(pl.multiple_of(first + start, BLOCK), width)],
                out_ref.at[:, pl.ds(0, width)],
            ))
        if stop > wide:
            begin = max(start, wide)
            copies.append((
                queries_ref.at[0, :, pl.ds(begin, stop - begin)],
                out_ref.at[:, pl.ds(begin - start, stop - begin)],
            ))
    copies = [pltpu.make_async_copy(a, b, sems.at[i]) for i, (a, b) in enumerate(copies)]
    copies[0].start()

    def scales():
        for copy in copies[1:]:
            copy.start()
        copies[0].wait()
        near, away = powers[0:alone, :], powers[far:blocks, :]
        return by_example(scales_of(jnp.where(part == 0, away, near)))

    scale_tiles(codes_ref, (1 - part) * far, buffer, code_sems, scales, range(alone), sent_ref)
    for copy in copies[1:]:
        copy.wait()


def cut(part, queries, codes, exponents, alone, cuts):
    rows = queries.shape[1]
    count = codes.shape[0]
    wide = alone * BLOCK
    tile = min(count, 64)
    chunks = len(cuts) - 1
    return pl.pallas_call(
        functools.partial(cut_kernel, alone, cuts),
        out_shape=[pltpu.VMEM((rows, b - a), jnp.bfloat16) for a, b in zip(cuts[:-1], cuts[1:])]
        + [pltpu.VMEM((count, wide), jnp.bfloat16)],
        in_specs=[SMEM] + [pl.BlockSpec(memory_space=pl.ANY)] * 3,
        out_specs=[VMEM] * (chunks + 1),
        scratch_shapes=[
            pltpu.VMEM((count // tile, tile, wide), jnp.bfloat16),
            pltpu.VMEM(exponents.shape, exponents.dtype),
            pltpu.SemaphoreType.DMA((count // tile,)),
            pltpu.SemaphoreType.DMA((2 * chunks + 1,)),
        ],
        compiler_params=pltpu.CompilerParams(vmem_limit_bytes=16 << 20),
        cost_estimate=pl.CostEstimate(flops=codes.size, bytes_accessed=2 * codes.size, transcendentals=0),
        name="cut_queries",
    )(part, in_hbm(queries), in_hbm(codes), in_hbm(exponents))


def scale_kernel(alone, part_ref, codes_ref, exponents_ref, out_ref, buffer, powers, code_sems, sem):
    part = part_ref[0]
    blocks = exponents_ref.shape[0]
    far = blocks - alone
    copy = pltpu.make_async_copy(exponents_ref, powers, sem)
    copy.start()

    def scales():
        copy.wait()
        own = jnp.where(part == 0, powers[0:alone, :], powers[far:blocks, :])
        return by_example(scales_of(jnp.concatenate([own, powers[alone:far, :]], axis=0)))

    order = [i + part * (far - alone) if i < alone else i - part * alone for i in range(far)]
    scale_tiles(codes_ref, part * alone, buffer, code_sems, scales, order, out_ref)


def scale(part, codes, exponents, alone):
    count = codes.shape[0]
    width = (exponents.shape[0] - alone) * BLOCK
    tile = min(count, 64)
    return pl.pallas_call(
        functools.partial(scale_kernel, alone),
        out_shape=pltpu.VMEM((count, width), jnp.bfloat16),
        in_specs=[SMEM] + [pl.BlockSpec(memory_space=pl.ANY)] * 2,
        out_specs=VMEM,
        scratch_shapes=[
            pltpu.VMEM((count // tile, tile, width), jnp.bfloat16),
            pltpu.VMEM(exponents.shape, exponents.dtype),
            pltpu.SemaphoreType.DMA((count // tile,)),
            pltpu.SemaphoreType.DMA,
        ],
        compiler_params=pltpu.CompilerParams(vmem_limit_bytes=16 << 20),
        cost_estimate=pl.CostEstimate(flops=codes.size, bytes_accessed=4 * codes.size, transcendentals=0),
        name="scale_codes",
    )(part, in_hbm(codes), in_hbm(exponents))


def stash_kernel(row, *refs):
    *array_refs, out_ref = refs
    array_refs = array_refs[1:] if row else array_refs
    for ref in array_refs:
        out_ref[row : row + ref.shape[0]] = ref[...]
        row += ref.shape[0]


def stash(held, arrays, row, rows):
    operands = ([held] if row else []) + arrays
    return pl.pallas_call(
        functools.partial(stash_kernel, row),
        out_shape=pltpu.VMEM((rows, arrays[0].shape[1]), arrays[0].dtype),
        in_specs=[VMEM] * len(operands),
        out_specs=VMEM,
        input_output_aliases={0: 0} if row else {},
        compiler_params=pltpu.CompilerParams(vmem_limit_bytes=16 << 20),
        cost_estimate=pl.CostEstimate(flops=0, bytes_accessed=4 * sum(a.size for a in arrays), transcendentals=0),
        name="stash",
    )(*in_vmem(operands))


def dot(rows, grads):
    return lax.dot_general(rows, grads, NT, preferred_element_type=jnp.float32)


def stacked(refs, columns):
    rows = [ref[:, columns] for ref in refs]
    return jnp.concatenate(rows, axis=0) if len(rows) > 1 else rows[0]


def halves(half, total, rows, keep_ref, send_ref):
    for j in range(total.shape[0] // rows):
        low = total[j * rows : j * rows + rows // 2]
        high = total[j * rows + rows // 2 : (j + 1) * rows]
        keep_ref[j] = jnp.where(half == 0, low, high)
        send_ref[j] = jnp.where(half == 0, high, low)


def product(pieces, grads_ref, first):
    total = None
    for refs in pieces:
        width = min(refs[0].shape[1], grads_ref.shape[1] - first)
        if width <= 0:
            break
        term = dot(stacked(refs, slice(0, width)), grads_ref[:, first : first + width])
        total = term if total is None else total + term
        first += width
    return total


def score_kernel(counts, grads_given, first, rows, begun, half_ref, *refs):
    refs = list(refs)
    pieces = [[refs.pop(0) for _ in range(arrays)] for arrays in counts]
    grad_refs, outs = refs[:grads_given], refs[grads_given:]
    base_refs, outs = (outs[:grads_given], outs[grads_given:]) if begun else (None, outs)
    for i, grads_ref in enumerate(grad_refs):
        total = product(pieces, grads_ref, first)
        if begun:
            total = total + base_refs[i][...]
        if rows:
            halves(half_ref[0], total, rows, *outs[2 * i : 2 * i + 2])
        else:
            outs[i][...] = total


def score(half, rows, pieces, grads, first=0, base=(), weight=1):
    operands = [array for arrays in pieces for array in arrays] + list(grads) + list(base)
    height = sum(array.shape[0] for array in pieces[0])
    count = grads[0].shape[0]
    if rows:
        shapes = [pltpu.VMEM((height // rows, rows // 2, count), jnp.float32)] * (2 * len(grads))
    else:
        shapes = [pltpu.VMEM((height, count), jnp.float32)] * len(grads)
    return pl.pallas_call(
        functools.partial(score_kernel, [len(arrays) for arrays in pieces], len(grads), first, rows, bool(base)),
        out_shape=shapes,
        in_specs=[SMEM] + [VMEM] * len(operands),
        out_specs=[VMEM] * len(shapes),
        compiler_params=pltpu.CompilerParams(vmem_limit_bytes=16 << 20),
        cost_estimate=pl.CostEstimate(
            flops=2 * height * sum(g.size for g in grads) * weight, bytes_accessed=2 * grads[0].size, transcendentals=0
        ),
        name="score",
    )(half, *in_vmem(operands))


def add_kernel(a_ref, b_ref, out_ref):
    out_ref[...] = a_ref[...] + b_ref[...]


def add(a, b):
    return pl.pallas_call(
        add_kernel,
        out_shape=pltpu.VMEM(a.shape, a.dtype),
        in_specs=[VMEM, VMEM],
        out_specs=VMEM,
        compiler_params=pltpu.CompilerParams(vmem_limit_bytes=16 << 20),
        name="add",
    )(*in_vmem([a, b]))


def place_kernel(groups, order_ref, ids_ref, *refs):
    *share_refs, out_ref = refs
    share_refs = list(share_refs)
    _, rows, count = out_ref.shape
    slots = lax.broadcasted_iota(jnp.int32, (count, count), 0)
    table = (slots == jnp.broadcast_to(ids_ref[...], (count, count))).astype(jnp.float32).astype(jnp.bfloat16)
    raw = [functools.reduce(jnp.add, [share_refs.pop(0)[...] for _ in range(shares)]) for shares in groups]
    raw = jnp.concatenate(raw, axis=0)
    high = raw.astype(jnp.bfloat16)
    rest = raw - high.astype(jnp.float32)
    middle = rest.astype(jnp.bfloat16)
    low = (rest - middle.astype(jnp.float32)).astype(jnp.bfloat16)
    placed = (dot(high, table) + dot(middle, table)) + dot(low, table)
    for j in range(raw.shape[0] // rows):
        out_ref[order_ref[j]] = placed[j * rows : (j + 1) * rows]


def place(order, ids, groups, rows):
    count = ids.shape[1]
    shares = [share.reshape(-1, count) for group in groups for share in group]
    return pl.pallas_call(
        functools.partial(place_kernel, [len(group) for group in groups]),
        out_shape=jax.ShapeDtypeStruct((order.shape[0], rows, count), jnp.float32),
        in_specs=[SMEM, VMEM] + [VMEM] * len(shares),
        out_specs=VMEM,
        compiler_params=pltpu.CompilerParams(vmem_limit_bytes=16 << 20),
        name="place_scores",
    )(order, ids, *in_vmem(shares))


def shards(fast, parts, total, queries, codes, exponents, example_ids):
    slow = total // fast
    here = lax.axis_index("ex")
    order = jnp.stack([
        lax.rem(here // fast + slow - s, slow) * fast + lax.rem(here % fast + fast - t, fast)
        for s in range(slow)
        for t in range(fast)
    ]).astype(jnp.int32)
    part, half, order = lax.optimization_barrier(
        (lax.axis_index("groups")[None], lax.axis_index("dim")[None], order)
    )
    rows = queries.shape[1]
    count = codes.shape[0]
    blocks = exponents.shape[1]
    alone = blocks * ALONE // 64
    held = blocks - alone
    cuts = [0, held * LEAD_PART // 35 * BLOCK, held * BLOCK]

    def step(value, length, stride):
        pairs = [
            (i, i + stride if (i // stride) % length < length - 1 else i - (length - 1) * stride)
            for i in range(total)
        ]
        return lax.ppermute(value, "ex", pairs)

    def along_fast(value):
        values = [value]
        for _ in range(fast - 1):
            values.append(step(values[-1], fast, 1))
        return values

    swap = [(i, parts - 1 - i) for i in range(parts)]
    by_block = exponents.T
    *chunks, sent = cut(part, queries, codes, by_block, alone, cuts)
    theirs = lax.ppermute(sent, "groups", swap)
    ours = scale(part, codes, by_block, alone)

    def stack(arrays):
        return arrays if rows % 16 == 0 else [jnp.concatenate(arrays, axis=0)]

    kept_rows = (slow - 2) * fast * rows
    early, late = [None] * CHUNKS, [None] * CHUNKS
    held = [[] for _ in range(CHUNKS)]
    for s in range(slow - 1):
        for c in (LEAD, 1 - LEAD):
            tied = [step(chunks[c], slow, fast), *along_fast(chunks[c])] + held[c]
            if s == 0 and c == LEAD:
                *tied, ours = lax.optimization_barrier(tied + [ours])
            elif s == slow - 2 and c != LEAD:
                begun_own = score(half, 0, early[LEAD : LEAD + 1], [ours], cuts[LEAD])
                ready, *begun_own = lax.optimization_barrier((chunks[LEAD], *begun_own))
                late[LEAD] = stack(along_fast(ready)[1:])
                *tied, begun_own = lax.optimization_barrier(tied + begun_own)
            else:
                tied = lax.optimization_barrier(tied)
            chunks[c], values, kept = tied[0], tied[1 : fast + 1], tied[fast + 1 :]
            if s < slow - 2:
                held[c] = [stash(kept[0] if s else None, stack(values), s * fast * rows, kept_rows)]
                continue
            early[c] = kept + stack(values + [chunks[c]])
            if c != LEAD:
                late[c] = stack([step(value, slow, fast) for value in values[1:]])

    def over_dim(value):
        return lax.ppermute(value, "dim", [(0, 1), (1, 0)])

    lead, trail = slice(LEAD, LEAD + 1), slice(1 - LEAD, 2 - LEAD)
    keep, send = score(half, rows, early, [theirs])
    added, theirs = lax.optimization_barrier((add(keep, over_dim(send)), theirs))
    given = lax.ppermute(added, "groups", swap)
    keep, send = score(half, rows, early[trail], [ours], cuts[1 - LEAD], [begun_own])
    shares = [given, keep, over_dim(send)]

    begun = score(half, 0, late[lead], [theirs, ours], cuts[LEAD])
    their_keep, their_send, own_keep, own_send = score(
        half, rows, late[trail], [theirs, ours], cuts[1 - LEAD], begun, LATE_WEIGHT
    )
    given = lax.ppermute(add(their_keep, over_dim(their_send)), "groups", swap)
    last = [given, own_keep, over_dim(own_send)]
    return place(order, example_ids, [shares, last], rows // 2)


def solution(mesh):
    placed = (
        P("ex", None, "dim"),
        P(("groups", "ex"), "dim"),
        P(("groups", "ex"), "dim"),
        P(("groups", "ex"), None),
    )
    return jax.shard_map(
        functools.partial(shards, fast_length(mesh), mesh.shape["groups"], mesh.shape["ex"]),
        mesh=mesh,
        in_specs=placed,
        out_specs=P(None, "dim", ("groups", "ex")),
        check_vma=False,
    )
```

```python
import functools

import jax
import jax.numpy as jnp
from jax import lax
from jax.experimental import pallas as pl
from jax.experimental.pallas import tpu as pltpu
from jax.sharding import PartitionSpec as P

BLOCK = 128
ALONE = 30
LATE_WEIGHT = 30
LEAD = 0
LEAD_PART = 19
CHUNKS = 2
VMEM = pl.BlockSpec(memory_space=pltpu.VMEM)
SMEM = pl.BlockSpec(memory_space=pltpu.SMEM)
NT = (((1,), (1,)), ((), ()))


def in_vmem(arrays):
    return [pltpu.with_memory_space_constraint(array, pltpu.VMEM) for array in arrays]


def in_hbm(array):
    return pltpu.with_memory_space_constraint(array, pltpu.HBM)


def fast_length(mesh):
    line = list(mesh.devices[0, :, 0])
    size = len(line)
    if size < 2 or not all(hasattr(device, "coords") for device in line):
        return 2 if size % 2 == 0 else size

    def moved(a, b):
        return tuple(i for i, (p, q) in enumerate(zip(a.coords, b.coords)) if p != q)

    along = moved(line[0], line[1])
    length = 2
    while length < size and moved(line[0], line[length]) == along:
        length += 1
    return length if size % length == 0 else size


def scaled(codes, scales, at):
    return codes * scales[:, at : at + 1].astype(jnp.bfloat16)


def scales_of(exponents):
    return (jnp.int32(1) << (exponents + 3)).astype(jnp.float32) * 0.125


def by_example(scales):
    pad = jnp.zeros((-scales.shape[0] % 8, scales.shape[1]), scales.dtype)
    return jnp.concatenate([scales, pad], axis=0).T


def scale_tiles(codes_ref, begin, buffer, sems, scales, order, out_ref):
    tiles, tile, width = buffer.shape

    def fetch(i):
        start = pl.multiple_of(begin * BLOCK, BLOCK)
        return pltpu.make_async_copy(
            codes_ref.at[pl.ds(i * tile, tile), pl.ds(start, width)], buffer.at[i], sems.at[i]
        )

    for i in range(tiles):
        fetch(i).start()
    scales = scales()
    for i in range(tiles):
        fetch(i).wait()
        rows = slice(i * tile, (i + 1) * tile)
        for block, at in enumerate(order):
            columns = pl.ds(pl.multiple_of(at * BLOCK, BLOCK), BLOCK)
            out_ref[rows, block * BLOCK : (block + 1) * BLOCK] = scaled(buffer[i, :, columns], scales[rows], block)


def cut_kernel(alone, cuts, part_ref, queries_ref, codes_ref, exponents_ref, *refs):
    *chunk_refs, sent_ref, buffer, powers, code_sems, sems = refs
    part = part_ref[0]
    blocks = exponents_ref.shape[0]
    far = blocks - alone
    first = pl.multiple_of(part * far * BLOCK, BLOCK)
    wide = alone * BLOCK
    copies = [(exponents_ref, powers)]
    for out_ref, start, stop in zip(chunk_refs, cuts[:-1], cuts[1:]):
        if start < wide:
            width = min(stop, wide) - start
            copies.append((
                queries_ref.at[0, :, pl.ds(pl.multiple_of(first + start, BLOCK), width)],
                out_ref.at[:, pl.ds(0, width)],
            ))
        if stop > wide:
            begin = max(start, wide)
            copies.append((
                queries_ref.at[0, :, pl.ds(begin, stop - begin)],
                out_ref.at[:, pl.ds(begin - start, stop - begin)],
            ))
    copies = [pltpu.make_async_copy(a, b, sems.at[i]) for i, (a, b) in enumerate(copies)]
    copies[0].start()

    def scales():
        for copy in copies[1:]:
            copy.start()
        copies[0].wait()
        near, away = powers[0:alone, :], powers[far:blocks, :]
        return by_example(scales_of(jnp.where(part == 0, away, near)))

    scale_tiles(codes_ref, (1 - part) * far, buffer, code_sems, scales, range(alone), sent_ref)
    for copy in copies[1:]:
        copy.wait()


def cut(part, queries, codes, exponents, alone, cuts):
    rows = queries.shape[1]
    count = codes.shape[0]
    wide = alone * BLOCK
    tile = min(count, 64)
    chunks = len(cuts) - 1
    return pl.pallas_call(
        functools.partial(cut_kernel, alone, cuts),
        out_shape=[pltpu.VMEM((rows, b - a), jnp.bfloat16) for a, b in zip(cuts[:-1], cuts[1:])]
        + [pltpu.VMEM((count, wide), jnp.bfloat16)],
        in_specs=[SMEM] + [pl.BlockSpec(memory_space=pl.ANY)] * 3,
        out_specs=[VMEM] * (chunks + 1),
        scratch_shapes=[
            pltpu.VMEM((count // tile, tile, wide), jnp.bfloat16),
            pltpu.VMEM(exponents.shape, exponents.dtype),
            pltpu.SemaphoreType.DMA((count // tile,)),
            pltpu.SemaphoreType.DMA((2 * chunks + 1,)),
        ],
        compiler_params=pltpu.CompilerParams(vmem_limit_bytes=16 << 20),
        cost_estimate=pl.CostEstimate(flops=codes.size, bytes_accessed=2 * codes.size, transcendentals=0),
        name="cut_queries",
    )(part, in_hbm(queries), in_hbm(codes), in_hbm(exponents))


def scale_kernel(alone, part_ref, codes_ref, exponents_ref, out_ref, buffer, powers, code_sems, sem):
    part = part_ref[0]
    blocks = exponents_ref.shape[0]
    far = blocks - alone
    copy = pltpu.make_async_copy(exponents_ref, powers, sem)
    copy.start()

    def scales():
        copy.wait()
        own = jnp.where(part == 0, powers[0:alone, :], powers[far:blocks, :])
        return by_example(scales_of(jnp.concatenate([own, powers[alone:far, :]], axis=0)))

    order = [i + part * (far - alone) if i < alone else i - part * alone for i in range(far)]
    scale_tiles(codes_ref, part * alone, buffer, code_sems, scales, order, out_ref)


def scale(part, codes, exponents, alone):
    count = codes.shape[0]
    width = (exponents.shape[0] - alone) * BLOCK
    tile = min(count, 64)
    return pl.pallas_call(
        functools.partial(scale_kernel, alone),
        out_shape=pltpu.VMEM((count, width), jnp.bfloat16),
        in_specs=[SMEM] + [pl.BlockSpec(memory_space=pl.ANY)] * 2,
        out_specs=VMEM,
        scratch_shapes=[
            pltpu.VMEM((count // tile, tile, width), jnp.bfloat16),
            pltpu.VMEM(exponents.shape, exponents.dtype),
            pltpu.SemaphoreType.DMA((count // tile,)),
            pltpu.SemaphoreType.DMA,
        ],
        compiler_params=pltpu.CompilerParams(vmem_limit_bytes=16 << 20),
        cost_estimate=pl.CostEstimate(flops=codes.size, bytes_accessed=4 * codes.size, transcendentals=0),
        name="scale_codes",
    )(part, in_hbm(codes), in_hbm(exponents))


def stash_kernel(row, *refs):
    *array_refs, out_ref = refs
    array_refs = array_refs[1:] if row else array_refs
    for ref in array_refs:
        out_ref[row : row + ref.shape[0]] = ref[...]
        row += ref.shape[0]


def stash(held, arrays, row, rows):
    operands = ([held] if row else []) + arrays
    return pl.pallas_call(
        functools.partial(stash_kernel, row),
        out_shape=pltpu.VMEM((rows, arrays[0].shape[1]), arrays[0].dtype),
        in_specs=[VMEM] * len(operands),
        out_specs=VMEM,
        input_output_aliases={0: 0} if row else {},
        compiler_params=pltpu.CompilerParams(vmem_limit_bytes=16 << 20),
        cost_estimate=pl.CostEstimate(flops=0, bytes_accessed=4 * sum(a.size for a in arrays), transcendentals=0),
        name="stash",
    )(*in_vmem(operands))


def dot(rows, grads):
    return lax.dot_general(rows, grads, NT, preferred_element_type=jnp.float32)


def stacked(refs, columns):
    rows = [ref[:, columns] for ref in refs]
    return jnp.concatenate(rows, axis=0) if len(rows) > 1 else rows[0]


def halves(half, total, rows, keep_ref, send_ref):
    for j in range(total.shape[0] // rows):
        low = total[j * rows : j * rows + rows // 2]
        high = total[j * rows + rows // 2 : (j + 1) * rows]
        keep_ref[j] = jnp.where(half == 0, low, high)
        send_ref[j] = jnp.where(half == 0, high, low)


def product(pieces, grads_ref, first):
    total = None
    for refs in pieces:
        width = min(refs[0].shape[1], grads_ref.shape[1] - first)
        if width <= 0:
            break
        term = dot(stacked(refs, slice(0, width)), grads_ref[:, first : first + width])
        total = term if total is None else total + term
        first += width
    return total


def score_kernel(counts, grads_given, first, rows, begun, half_ref, *refs):
    refs = list(refs)
    pieces = [[refs.pop(0) for _ in range(arrays)] for arrays in counts]
    grad_refs, outs = refs[:grads_given], refs[grads_given:]
    base_refs, outs = (outs[:grads_given], outs[grads_given:]) if begun else (None, outs)
    for i, grads_ref in enumerate(grad_refs):
        total = product(pieces, grads_ref, first)
        if begun:
            total = total + base_refs[i][...]
        if rows:
            halves(half_ref[0], total, rows, *outs[2 * i : 2 * i + 2])
        else:
            outs[i][...] = total


def score(half, rows, pieces, grads, first=0, base=(), weight=1):
    operands = [array for arrays in pieces for array in arrays] + list(grads) + list(base)
    height = sum(array.shape[0] for array in pieces[0])
    count = grads[0].shape[0]
    if rows:
        shapes = [pltpu.VMEM((height // rows, rows // 2, count), jnp.float32)] * (2 * len(grads))
    else:
        shapes = [pltpu.VMEM((height, count), jnp.float32)] * len(grads)
    return pl.pallas_call(
        functools.partial(score_kernel, [len(arrays) for arrays in pieces], len(grads), first, rows, bool(base)),
        out_shape=shapes,
        in_specs=[SMEM] + [VMEM] * len(operands),
        out_specs=[VMEM] * len(shapes),
        compiler_params=pltpu.CompilerParams(vmem_limit_bytes=16 << 20),
        cost_estimate=pl.CostEstimate(
            flops=2 * height * sum(g.size for g in grads) * weight, bytes_accessed=2 * grads[0].size, transcendentals=0
        ),
        name="score",
    )(half, *in_vmem(operands))


def add_kernel(a_ref, b_ref, out_ref):
    out_ref[...] = a_ref[...] + b_ref[...]


def add(a, b):
    return pl.pallas_call(
        add_kernel,
        out_shape=pltpu.VMEM(a.shape, a.dtype),
        in_specs=[VMEM, VMEM],
        out_specs=VMEM,
        compiler_params=pltpu.CompilerParams(vmem_limit_bytes=16 << 20),
        name="add",
    )(*in_vmem([a, b]))


def place_kernel(groups, order_ref, ids_ref, *refs):
    *share_refs, out_ref = refs
    share_refs = list(share_refs)
    _, rows, count = out_ref.shape
    slots = lax.broadcasted_iota(jnp.int32, (count, count), 0)
    table = (slots == jnp.broadcast_to(ids_ref[...], (count, count))).astype(jnp.float32).astype(jnp.bfloat16)
    raw = [functools.reduce(jnp.add, [share_refs.pop(0)[...] for _ in range(shares)]) for shares in groups]
    raw = jnp.concatenate(raw, axis=0)
    high = raw.astype(jnp.bfloat16)
    rest = raw - high.astype(jnp.float32)
    middle = rest.astype(jnp.bfloat16)
    low = (rest - middle.astype(jnp.float32)).astype(jnp.bfloat16)
    placed = (dot(high, table) + dot(middle, table)) + dot(low, table)
    for j in range(raw.shape[0] // rows):
        out_ref[order_ref[j]] = placed[j * rows : (j + 1) * rows]


def place(order, ids, groups, rows):
    count = ids.shape[1]
    shares = [share.reshape(-1, count) for group in groups for share in group]
    return pl.pallas_call(
        functools.partial(place_kernel, [len(group) for group in groups]),
        out_shape=jax.ShapeDtypeStruct((order.shape[0], rows, count), jnp.float32),
        in_specs=[SMEM, VMEM] + [VMEM] * len(shares),
        out_specs=VMEM,
        compiler_params=pltpu.CompilerParams(vmem_limit_bytes=16 << 20),
        name="place_scores",
    )(order, ids, *in_vmem(shares))


def shards(fast, parts, total, queries, codes, exponents, example_ids):
    slow = total // fast
    here = lax.axis_index("ex")
    order = jnp.stack([
        lax.rem(here // fast + slow - s, slow) * fast + lax.rem(here % fast + fast - t, fast)
        for s in range(slow)
        for t in range(fast)
    ]).astype(jnp.int32)
    part, half, order = lax.optimization_barrier(
        (lax.axis_index("groups")[None], lax.axis_index("dim")[None], order)
    )
    rows = queries.shape[1]
    count = codes.shape[0]
    blocks = exponents.shape[1]
    alone = blocks * ALONE // 64
    held = blocks - alone
    cuts = [0, held * LEAD_PART // 35 * BLOCK, held * BLOCK]

    def step(value, length, stride):
        pairs = [
            (i, i + stride if (i // stride) % length < length - 1 else i - (length - 1) * stride)
            for i in range(total)
        ]
        return lax.ppermute(value, "ex", pairs)

    def along_fast(value):
        values = [value]
        for _ in range(fast - 1):
            values.append(step(values[-1], fast, 1))
        return values

    swap = [(i, parts - 1 - i) for i in range(parts)]
    by_block = exponents.T
    *chunks, sent = cut(part, queries, codes, by_block, alone, cuts)
    theirs = lax.ppermute(sent, "groups", swap)
    ours = scale(part, codes, by_block, alone)

    def stack(arrays):
        return arrays if rows % 16 == 0 else [jnp.concatenate(arrays, axis=0)]

    kept_rows = (slow - 2) * fast * rows
    early, late = [None] * CHUNKS, [None] * CHUNKS
    held = [[] for _ in range(CHUNKS)]
    for s in range(slow - 1):
        for c in (LEAD, 1 - LEAD):
            tied = [step(chunks[c], slow, fast), *along_fast(chunks[c])] + held[c]
            if s == 0 and c == LEAD:
                *tied, ours = lax.optimization_barrier(tied + [ours])
            elif s == slow - 2 and c != LEAD:
                begun_own = score(half, 0, early[LEAD : LEAD + 1], [ours], cuts[LEAD])
                late[LEAD] = stack(along_fast(chunks[LEAD])[1:])
                *tied, begun_own = lax.optimization_barrier(tied + list(begun_own))
            else:
                tied = lax.optimization_barrier(tied)
            chunks[c], values, kept = tied[0], tied[1 : fast + 1], tied[fast + 1 :]
            if s < slow - 2:
                held[c] = [stash(kept[0] if s else None, stack(values), s * fast * rows, kept_rows)]
                continue
            early[c] = kept + stack(values + [chunks[c]])
            if c != LEAD:
                late[c] = stack([step(value, slow, fast) for value in values[1:]])

    def over_dim(value):
        return lax.ppermute(value, "dim", [(0, 1), (1, 0)])

    lead, trail = slice(LEAD, LEAD + 1), slice(1 - LEAD, 2 - LEAD)
    keep, send = score(half, rows, early, [theirs])
    added, theirs = lax.optimization_barrier((add(keep, over_dim(send)), theirs))
    given = lax.ppermute(added, "groups", swap)
    keep, send = score(half, rows, early[trail], [ours], cuts[1 - LEAD], [begun_own])
    shares = [given, keep, over_dim(send)]

    begun = score(half, 0, late[lead], [theirs, ours], cuts[LEAD])
    their_keep, their_send, own_keep, own_send = score(
        half, rows, late[trail], [theirs, ours], cuts[1 - LEAD], begun, LATE_WEIGHT
    )
    given = lax.ppermute(add(their_keep, over_dim(their_send)), "groups", swap)
    last = [given, own_keep, over_dim(own_send)]
    return place(order, example_ids, [shares, last], rows // 2)


def solution(mesh):
    placed = (
        P("ex", None, "dim"),
        P(("groups", "ex"), "dim"),
        P(("groups", "ex"), "dim"),
        P(("groups", "ex"), None),
    )
    return jax.shard_map(
        functools.partial(shards, fast_length(mesh), mesh.shape["groups"], mesh.shape["ex"]),
        mesh=mesh,
        in_specs=placed,
        out_specs=P(None, "dim", ("groups", "ex")),
        check_vma=False,
    )
```

```python
import functools

import jax
import jax.numpy as jnp
from jax import lax
from jax.experimental import pallas as pl
from jax.experimental.pallas import tpu as pltpu
from jax.sharding import PartitionSpec as P

BLOCK = 128
ALONE = 30
LATE_WEIGHT = 30
LEAD = 0
LEAD_PART = 19
CHUNKS = 2
VMEM = pl.BlockSpec(memory_space=pltpu.VMEM)
SMEM = pl.BlockSpec(memory_space=pltpu.SMEM)
NT = (((1,), (1,)), ((), ()))


def in_vmem(arrays):
    return [pltpu.with_memory_space_constraint(array, pltpu.VMEM) for array in arrays]


def in_hbm(array):
    return pltpu.with_memory_space_constraint(array, pltpu.HBM)


def fast_length(mesh):
    line = list(mesh.devices[0, :, 0])
    size = len(line)
    if size < 2 or not all(hasattr(device, "coords") for device in line):
        return 2 if size % 2 == 0 else size

    def moved(a, b):
        return tuple(i for i, (p, q) in enumerate(zip(a.coords, b.coords)) if p != q)

    along = moved(line[0], line[1])
    length = 2
    while length < size and moved(line[0], line[length]) == along:
        length += 1
    return length if size % length == 0 else size


def scaled(codes, scales, at):
    return codes * scales[:, at : at + 1]


def scales_of(exponents):
    return (jnp.int32(1) << (exponents + 3)).astype(jnp.float32) * 0.125


def by_example(scales):
    pad = jnp.zeros((-scales.shape[0] % 8, scales.shape[1]), scales.dtype)
    return jnp.concatenate([scales, pad], axis=0).T.astype(jnp.bfloat16)


def scale_tiles(codes_ref, begin, buffer, sems, scales, order, out_ref):
    tiles, tile, width = buffer.shape

    def fetch(i):
        start = pl.multiple_of(begin * BLOCK, BLOCK)
        return pltpu.make_async_copy(
            codes_ref.at[pl.ds(i * tile, tile), pl.ds(start, width)], buffer.at[i], sems.at[i]
        )

    for i in range(tiles):
        fetch(i).start()
    scales = scales()
    for i in range(tiles):
        fetch(i).wait()
        rows = slice(i * tile, (i + 1) * tile)
        for block, at in enumerate(order):
            columns = pl.ds(pl.multiple_of(at * BLOCK, BLOCK), BLOCK)
            out_ref[rows, block * BLOCK : (block + 1) * BLOCK] = scaled(buffer[i, :, columns], scales[rows], block)


def cut_kernel(alone, cuts, part_ref, queries_ref, codes_ref, exponents_ref, *refs):
    *chunk_refs, sent_ref, buffer, powers, code_sems, sems = refs
    part = part_ref[0]
    blocks = exponents_ref.shape[0]
    far = blocks - alone
    first = pl.multiple_of(part * far * BLOCK, BLOCK)
    wide = alone * BLOCK
    copies = [(exponents_ref, powers)]
    for out_ref, start, stop in zip(chunk_refs, cuts[:-1], cuts[1:]):
        if start < wide:
            width = min(stop, wide) - start
            copies.append((
                queries_ref.at[0, :, pl.ds(pl.multiple_of(first + start, BLOCK), width)],
                out_ref.at[:, pl.ds(0, width)],
            ))
        if stop > wide:
            begin = max(start, wide)
            copies.append((
                queries_ref.at[0, :, pl.ds(begin, stop - begin)],
                out_ref.at[:, pl.ds(begin - start, stop - begin)],
            ))
    copies = [pltpu.make_async_copy(a, b, sems.at[i]) for i, (a, b) in enumerate(copies)]
    copies[0].start()

    def scales():
        for copy in copies[1:]:
            copy.start()
        copies[0].wait()
        near, away = powers[0:alone, :], powers[far:blocks, :]
        return by_example(scales_of(jnp.where(part == 0, away, near)))

    scale_tiles(codes_ref, (1 - part) * far, buffer, code_sems, scales, range(alone), sent_ref)
    for copy in copies[1:]:
        copy.wait()


def cut(part, queries, codes, exponents, alone, cuts):
    rows = queries.shape[1]
    count = codes.shape[0]
    wide = alone * BLOCK
    tile = min(count, 32)
    chunks = len(cuts) - 1
    return pl.pallas_call(
        functools.partial(cut_kernel, alone, cuts),
        out_shape=[pltpu.VMEM((rows, b - a), jnp.bfloat16) for a, b in zip(cuts[:-1], cuts[1:])]
        + [pltpu.VMEM((count, wide), jnp.bfloat16)],
        in_specs=[SMEM] + [pl.BlockSpec(memory_space=pl.ANY)] * 3,
        out_specs=[VMEM] * (chunks + 1),
        scratch_shapes=[
            pltpu.VMEM((count // tile, tile, wide), jnp.bfloat16),
            pltpu.VMEM(exponents.shape, exponents.dtype),
            pltpu.SemaphoreType.DMA((count // tile,)),
            pltpu.SemaphoreType.DMA((2 * chunks + 1,)),
        ],
        compiler_params=pltpu.CompilerParams(vmem_limit_bytes=16 << 20),
        cost_estimate=pl.CostEstimate(flops=codes.size, bytes_accessed=2 * codes.size, transcendentals=0),
        name="cut_queries",
    )(part, in_hbm(queries), in_hbm(codes), in_hbm(exponents))


def scale_kernel(alone, part_ref, codes_ref, exponents_ref, out_ref, buffer, powers, code_sems, sem):
    part = part_ref[0]
    blocks = exponents_ref.shape[0]
    far = blocks - alone
    copy = pltpu.make_async_copy(exponents_ref, powers, sem)
    copy.start()

    def scales():
        copy.wait()
        own = jnp.where(part == 0, powers[0:alone, :], powers[far:blocks, :])
        return by_example(scales_of(jnp.concatenate([own, powers[alone:far, :]], axis=0)))

    order = [i + part * (far - alone) if i < alone else i - part * alone for i in range(far)]
    scale_tiles(codes_ref, part * alone, buffer, code_sems, scales, order, out_ref)


def scale(part, codes, exponents, alone):
    count = codes.shape[0]
    width = (exponents.shape[0] - alone) * BLOCK
    tile = min(count, 64)
    return pl.pallas_call(
        functools.partial(scale_kernel, alone),
        out_shape=pltpu.VMEM((count, width), jnp.bfloat16),
        in_specs=[SMEM] + [pl.BlockSpec(memory_space=pl.ANY)] * 2,
        out_specs=VMEM,
        scratch_shapes=[
            pltpu.VMEM((count // tile, tile, width), jnp.bfloat16),
            pltpu.VMEM(exponents.shape, exponents.dtype),
            pltpu.SemaphoreType.DMA((count // tile,)),
            pltpu.SemaphoreType.DMA,
        ],
        compiler_params=pltpu.CompilerParams(vmem_limit_bytes=16 << 20),
        cost_estimate=pl.CostEstimate(flops=codes.size, bytes_accessed=4 * codes.size, transcendentals=0),
        name="scale_codes",
    )(part, in_hbm(codes), in_hbm(exponents))


def stash_kernel(row, *refs):
    *array_refs, out_ref = refs
    array_refs = array_refs[1:] if row else array_refs
    for ref in array_refs:
        out_ref[row : row + ref.shape[0]] = ref[...]
        row += ref.shape[0]


def stash(held, arrays, row, rows):
    operands = ([held] if row else []) + arrays
    return pl.pallas_call(
        functools.partial(stash_kernel, row),
        out_shape=pltpu.VMEM((rows, arrays[0].shape[1]), arrays[0].dtype),
        in_specs=[VMEM] * len(operands),
        out_specs=VMEM,
        input_output_aliases={0: 0} if row else {},
        compiler_params=pltpu.CompilerParams(vmem_limit_bytes=16 << 20),
        cost_estimate=pl.CostEstimate(flops=0, bytes_accessed=4 * sum(a.size for a in arrays), transcendentals=0),
        name="stash",
    )(*in_vmem(operands))


def dot(rows, grads):
    return lax.dot_general(rows, grads, NT, preferred_element_type=jnp.float32)


def stacked(refs, columns):
    rows = [ref[:, columns] for ref in refs]
    return jnp.concatenate(rows, axis=0) if len(rows) > 1 else rows[0]


def halves(half, total, rows, keep_ref, send_ref):
    for j in range(total.shape[0] // rows):
        low = total[j * rows : j * rows + rows // 2]
        high = total[j * rows + rows // 2 : (j + 1) * rows]
        keep_ref[j] = jnp.where(half == 0, low, high)
        send_ref[j] = jnp.where(half == 0, high, low)


def product(pieces, grads_ref, first):
    total = None
    for refs in pieces:
        width = min(refs[0].shape[1], grads_ref.shape[1] - first)
        if width <= 0:
            break
        term = dot(stacked(refs, slice(0, width)), grads_ref[:, first : first + width])
        total = term if total is None else total + term
        first += width
    return total


def score_kernel(counts, grads_given, first, rows, begun, half_ref, *refs):
    refs = list(refs)
    pieces = [[refs.pop(0) for _ in range(arrays)] for arrays in counts]
    grad_refs, outs = refs[:grads_given], refs[grads_given:]
    base_refs, outs = (outs[:grads_given], outs[grads_given:]) if begun else (None, outs)
    for i, grads_ref in enumerate(grad_refs):
        total = product(pieces, grads_ref, first)
        if begun:
            total = total + base_refs[i][...]
        if rows:
            halves(half_ref[0], total, rows, *outs[2 * i : 2 * i + 2])
        else:
            outs[i][...] = total


def score(half, rows, pieces, grads, first=0, base=(), weight=1):
    operands = [array for arrays in pieces for array in arrays] + list(grads) + list(base)
    height = sum(array.shape[0] for array in pieces[0])
    count = grads[0].shape[0]
    if rows:
        shapes = [pltpu.VMEM((height // rows, rows // 2, count), jnp.float32)] * (2 * len(grads))
    else:
        shapes = [pltpu.VMEM((height, count), jnp.float32)] * len(grads)
    return pl.pallas_call(
        functools.partial(score_kernel, [len(arrays) for arrays in pieces], len(grads), first, rows, bool(base)),
        out_shape=shapes,
        in_specs=[SMEM] + [VMEM] * len(operands),
        out_specs=[VMEM] * len(shapes),
        compiler_params=pltpu.CompilerParams(vmem_limit_bytes=16 << 20),
        cost_estimate=pl.CostEstimate(
            flops=2 * height * sum(g.size for g in grads) * weight, bytes_accessed=2 * grads[0].size, transcendentals=0
        ),
        name="score",
    )(half, *in_vmem(operands))


def add_kernel(a_ref, b_ref, out_ref):
    out_ref[...] = a_ref[...] + b_ref[...]


def add(a, b):
    return pl.pallas_call(
        add_kernel,
        out_shape=pltpu.VMEM(a.shape, a.dtype),
        in_specs=[VMEM, VMEM],
        out_specs=VMEM,
        compiler_params=pltpu.CompilerParams(vmem_limit_bytes=16 << 20),
        name="add",
    )(*in_vmem([a, b]))


def place_kernel(groups, order_ref, ids_ref, *refs):
    *share_refs, out_ref = refs
    share_refs = list(share_refs)
    _, rows, count = out_ref.shape
    slots = lax.broadcasted_iota(jnp.int32, (count, count), 0)
    table = (slots == jnp.broadcast_to(ids_ref[...], (count, count))).astype(jnp.float32).astype(jnp.bfloat16)
    raw = [functools.reduce(jnp.add, [share_refs.pop(0)[...] for _ in range(shares)]) for shares in groups]
    raw = jnp.concatenate(raw, axis=0)
    high = raw.astype(jnp.bfloat16)
    rest = raw - high.astype(jnp.float32)
    middle = rest.astype(jnp.bfloat16)
    low = (rest - middle.astype(jnp.float32)).astype(jnp.bfloat16)
    placed = (dot(high, table) + dot(middle, table)) + dot(low, table)
    for j in range(raw.shape[0] // rows):
        out_ref[order_ref[j]] = placed[j * rows : (j + 1) * rows]


def place(order, ids, groups, rows):
    count = ids.shape[1]
    shares = [share.reshape(-1, count) for group in groups for share in group]
    return pl.pallas_call(
        functools.partial(place_kernel, [len(group) for group in groups]),
        out_shape=jax.ShapeDtypeStruct((order.shape[0], rows, count), jnp.float32),
        in_specs=[SMEM, VMEM] + [VMEM] * len(shares),
        out_specs=VMEM,
        compiler_params=pltpu.CompilerParams(vmem_limit_bytes=16 << 20),
        name="place_scores",
    )(order, ids, *in_vmem(shares))


def shards(fast, parts, total, queries, codes, exponents, example_ids):
    slow = total // fast
    here = lax.axis_index("ex")
    order = jnp.stack([
        lax.rem(here // fast + slow - s, slow) * fast + lax.rem(here % fast + fast - t, fast)
        for s in range(slow)
        for t in range(fast)
    ]).astype(jnp.int32)
    part, half, order = lax.optimization_barrier(
        (lax.axis_index("groups")[None], lax.axis_index("dim")[None], order)
    )
    rows = queries.shape[1]
    count = codes.shape[0]
    blocks = exponents.shape[1]
    alone = blocks * ALONE // 64
    held = blocks - alone
    cuts = [0, held * LEAD_PART // 35 * BLOCK, held * BLOCK]

    def step(value, length, stride):
        pairs = [
            (i, i + stride if (i // stride) % length < length - 1 else i - (length - 1) * stride)
            for i in range(total)
        ]
        return lax.ppermute(value, "ex", pairs)

    def along_fast(value):
        values = [value]
        for _ in range(fast - 1):
            values.append(step(values[-1], fast, 1))
        return values

    swap = [(i, parts - 1 - i) for i in range(parts)]
    by_block = exponents.T
    *chunks, sent = cut(part, queries, codes, by_block, alone, cuts)
    theirs = lax.ppermute(sent, "groups", swap)
    ours = scale(part, codes, by_block, alone)

    def stack(arrays):
        return arrays if rows % 16 == 0 else [jnp.concatenate(arrays, axis=0)]

    kept_rows = (slow - 2) * fast * rows
    early, late = [None] * CHUNKS, [None] * CHUNKS
    held = [[] for _ in range(CHUNKS)]
    for s in range(slow - 1):
        for c in (LEAD, 1 - LEAD):
            tied = [step(chunks[c], slow, fast), *along_fast(chunks[c])] + held[c]
            if s == 0 and c == LEAD:
                *tied, ours = lax.optimization_barrier(tied + [ours])
            elif s == slow - 2 and c != LEAD:
                begun_own = score(half, 0, early[LEAD : LEAD + 1], [ours], cuts[LEAD])
                late[LEAD] = stack(along_fast(chunks[LEAD])[1:])
                *tied, begun_own = lax.optimization_barrier(tied + list(begun_own))
            else:
                tied = lax.optimization_barrier(tied)
            chunks[c], values, kept = tied[0], tied[1 : fast + 1], tied[fast + 1 :]
            if s < slow - 2:
                held[c] = [stash(kept[0] if s else None, stack(values), s * fast * rows, kept_rows)]
                continue
            early[c] = kept + stack(values + [chunks[c]])
            if c != LEAD:
                late[c] = stack([step(value, slow, fast) for value in values[1:]])

    def over_dim(value):
        return lax.ppermute(value, "dim", [(0, 1), (1, 0)])

    lead, trail = slice(LEAD, LEAD + 1), slice(1 - LEAD, 2 - LEAD)
    keep, send = score(half, rows, early, [theirs])
    added, theirs = lax.optimization_barrier((add(keep, over_dim(send)), theirs))
    given = lax.ppermute(added, "groups", swap)
    keep, send = score(half, rows, early[trail], [ours], cuts[1 - LEAD], [begun_own])
    shares = [given, keep, over_dim(send)]

    begun = score(half, 0, late[lead], [theirs, ours], cuts[LEAD])
    their_keep, their_send, own_keep, own_send = score(
        half, rows, late[trail], [theirs, ours], cuts[1 - LEAD], begun, LATE_WEIGHT
    )
    given = lax.ppermute(add(their_keep, over_dim(their_send)), "groups", swap)
    last = [given, own_keep, over_dim(own_send)]
    return place(order, example_ids, [shares, last], rows // 2)


def solution(mesh):
    placed = (
        P("ex", None, "dim"),
        P(("groups", "ex"), "dim"),
        P(("groups", "ex"), "dim"),
        P(("groups", "ex"), None),
    )
    return jax.shard_map(
        functools.partial(shards, fast_length(mesh), mesh.shape["groups"], mesh.shape["ex"]),
        mesh=mesh,
        in_specs=placed,
        out_specs=P(None, "dim", ("groups", "ex")),
        check_vma=False,
    )
```
